128 devices in a mesh: space: 32 (over x, z, core), chan: 4 (over y).
Axes of the slice: x: 4, y: 4, z: 4, core: 2. Of those that a mesh axis runs over, the one named last changes fastest.
Arguments:
- pages: bfloat16 [3584, 84, 256], P(('space', 'chan')), may hold values from -6 to 6
- merge_gain: bfloat16 [1024], replicated, may hold values from 0.25 to 1.75
- merge_shift: bfloat16 [1024], replicated, may hold values from -1.75 to 1.75
- merge_weight: bfloat16 [1024, 512], replicated, may hold values from -0.1875 to 0.1875
- norm_gain: bfloat16 [2, 512], replicated, may hold values from 0.25 to 1.75
- norm_shift: bfloat16 [2, 512], replicated, may hold values from -1.75 to 1.75
- qkv_weight: bfloat16 [512, 3, 512], P(None, None, 'chan'), may hold values from -0.25 to 0.25
- qv_bias: bfloat16 [2, 512], P(None, 'chan'), may hold values from -1.75 to 1.75
- rel_table: bfloat16 [16, 169], P('chan'), may hold values from -6 to 6
- out_weight: bfloat16 [512, 512], P('chan'), may hold values from -1 to 1
- out_bias: bfloat16 [512], P('chan'), may hold values from -1.75 to 1.75
- up_weight: bfloat16 [512, 2048], P(None, 'chan'), may hold values from -0.25 to 0.25
- up_bias: bfloat16 [2048], P('chan'), may hold values from -1.75 to 1.75
- down_weight: bfloat16 [2048, 512], P('chan'), may hold values from -0.125 to 0.125
- down_bias: bfloat16 [512], P('chan'), may hold values from -1.75 to 1.75
- cotangent: bfloat16 [1792, 42, 512], P('space', None, 'chan'), may hold values from -6 to 6
Outputs:
- block_out: float32 [1792, 42, 512], P('space', None, 'chan')
- pages_grad: float32 [3584, 84, 256], P(('space', 'chan'))
- merge_gain_grad: float32 [1024], replicated
- merge_shift_grad: float32 [1024], replicated
- merge_weight_grad: float32 [1024, 512], replicated
- norm_gain_grad: float32 [2, 512], replicated
- norm_shift_grad: float32 [2, 512], replicated
- qkv_weight_grad: float32 [512, 3, 512], P(None, None, 'chan')
- qv_bias_grad: float32 [2, 512], P(None, 'chan')
- rel_table_grad: float32 [16, 169], P('chan')
- out_weight_grad: float32 [512, 512], P('chan')
- out_bias_grad: float32 [512], P('chan')
- up_weight_grad: float32 [512, 2048], P(None, 'chan')
- up_bias_grad: float32 [2048], P('chan')
- down_weight_grad: float32 [2048, 512], P('chan')
- down_bias_grad: float32 [512], P('chan')
- branch_rms: float32 [3], replicated
The draws below stay inside these ranges and needn't reach their ends.
All inputs are finite; a program needn't handle non-finite values.
Results may differ from the reference program's by a relative error of at most 0.025.
Values may be sent and summed in bfloat16 or wider, within the bound.
A program may use at most 128 MiB of HBM per device.

```python
import jax
import jax.numpy as jnp
from jax import lax

C2 = 256
D = 512
HEADS = 16
FF = 2048
HD = 32
WIN = 7
SHIFT = 3
REL = 169
PAGE_ROWS = 56
COLS = 42
NH = 1792


def steps_of(stream_key, extent, shards, smallest, high):
    def one(axis_at, shards_of):
        steps = jax.random.uniform(jax.random.fold_in(jax.random.fold_in(stream_key, 6), axis_at), (shards_of,), jnp.float32, smallest / len(shards), high / len(shards))
        return jnp.repeat(jnp.exp(steps), extent[axis_at] // shards_of).reshape((-1,) + (1,) * (len(extent) - axis_at - 1))

    level = one(*shards[0])
    for cut in shards[1:]:
        level = level * one(*cut)
    return level


def noise(stream_key, shape, deviation, most, cuts=(), kind=jnp.bfloat16):
    factor_of = steps_of(stream_key, shape, cuts, -0.22, 0.18) if cuts else 1.0
    array = jax.random.normal(stream_key, shape, jnp.float32) * deviation * factor_of
    return jnp.minimum(jnp.maximum(array, -most), most).astype(kind)


def setup_inputs(seed: int = 0) -> dict:
    key_list = jax.random.split(jax.random.key(seed), 17)
    return {
        "pages": noise(key_list[0], (2 * NH, 2 * COLS, C2), 1.0, 6.0, ((0, 128),)),
        "merge_gain": jnp.clip(1.0 + 0.15 * jax.random.normal(key_list[1], (4 * C2,), jnp.float32), 0.25, 1.75).astype(jnp.bfloat16),
        "merge_shift": noise(key_list[2], (4 * C2,), 0.3, 1.75),
        "merge_weight": noise(key_list[3], (4 * C2, D), (4 * C2) ** -0.5, 0.1875),
        "norm_gain": jnp.clip(1.0 + 0.15 * jax.random.normal(key_list[4], (2, D), jnp.float32), 0.25, 1.75).astype(jnp.bfloat16),
        "norm_shift": noise(key_list[5], (2, D), 0.3, 1.75),
        "qkv_weight": noise(key_list[6], (D, 3, D), D ** -0.5, 0.25, ((2, 4),)),
        "qv_bias": noise(key_list[7], (2, D), 0.3, 1.75, ((1, 4),)),
        "rel_table": noise(key_list[8], (HEADS, REL), 1.0, 6.0, ((0, 4),)),
        "out_weight": noise(key_list[9], (D, D), (D // 16) ** -0.5, 1.0, ((0, 4),)),
        "out_bias": noise(key_list[10], (D,), 0.3, 1.75, ((0, 4),)),
        "up_weight": noise(key_list[11], (D, FF), D ** -0.5, 0.25, ((1, 4),)),
        "up_bias": noise(key_list[12], (FF,), 0.3, 1.75, ((0, 4),)),
        "down_weight": noise(key_list[13], (FF, D), FF ** -0.5, 0.125, ((0, 4),)),
        "down_bias": noise(key_list[14], (D,), 0.3, 1.75, ((0, 4),)),
        "cotangent": noise(key_list[15], (NH, COLS, D), 1.0, 6.0, ((0, 32), (2, 4))),
    }


norm_epsilon = 1e-05
masked_score = -1000000000.0
highest = lax.Precision.HIGHEST

@jax.custom_vjp
def low(v):
    return lax.optimization_barrier(v.astype(jnp.bfloat16)).astype(jnp.float32)

@jax.custom_vjp
def low_back(v):
    return v

def low_keep(v):
    return (low(v), None)

def low_pass(kept, grad):
    return (grad,)

def back_keep(v):
    return (v, None)

def back_low(kept, grad):
    return (low(grad),)
low.defvjp(low_keep, low_pass)
low_back.defvjp(back_keep, back_low)

def layer_norm(inputs, gain_vector, offset):
    average = lax.optimization_barrier(jnp.mean(inputs, -1, keepdims=True))
    centered = inputs - average
    variance = lax.optimization_barrier(jnp.mean(centered * centered, -1, keepdims=True))
    return centered * lax.rsqrt(variance + norm_epsilon) * gain_vector + offset

def to_windows(grid_values):
    rows_all, cols_all, channels = grid_values.shape
    blocks = grid_values.reshape(rows_all // WIN, WIN, cols_all // WIN, WIN, channels)
    return blocks.transpose(0, 2, 1, 3, 4).reshape(-1, WIN * WIN, channels)

def from_windows(blocks, rows_all, cols_all):
    channels = blocks.shape[-1]
    grid_values = blocks.reshape(rows_all // WIN, cols_all // WIN, WIN, WIN, channels)
    return grid_values.transpose(0, 2, 1, 3, 4).reshape(rows_all, cols_all, channels)

def relative_code():
    places = jnp.arange(WIN * WIN, dtype=jnp.int32)
    row_place = places // WIN
    col_place = places % WIN
    return (row_place[:, None] - row_place[None, :] + WIN - 1) * (2 * WIN - 1) + col_place[:, None] - col_place[None, :] + WIN - 1

def region_codes(first_row, rows_band, cols_all, total_rows):
    row_global = first_row + jnp.arange(rows_band, dtype=jnp.int32)
    page_number = (row_global + SHIFT) % total_rows // PAGE_ROWS
    col_part = (jnp.arange(cols_all, dtype=jnp.int32) + SHIFT) // cols_all
    return page_number[:, None] * 2 + col_part[None, :]

def forward(pages, merge_gain, merge_shift, merge_weight, norm_gain, norm_shift, qkv_weight, qv_bias, rel_table, out_weight, out_bias, up_weight, up_bias, down_weight, down_bias):
    rolled = jnp.roll(pages, (-2 * SHIFT, -2 * SHIFT), axis=(0, 1))
    quad_tokens = rolled.reshape(NH, 2, COLS, 2, C2).transpose(0, 2, 3, 1, 4).reshape(NH, COLS, 4 * C2)
    merge_normed = low(layer_norm(quad_tokens, merge_gain, merge_shift))
    merged = low(low_back(jnp.einsum('rwc,cd->rwd', merge_normed, merge_weight, precision=highest)))
    normed_one = low(layer_norm(merged, norm_gain[0], norm_shift[0]))
    projected = jnp.einsum('tnc,cke->tnke', to_windows(normed_one), qkv_weight, precision=highest)
    window_count = projected.shape[0]

    def heads_of(flat_values):
        return low(low_back(flat_values)).reshape(window_count, WIN * WIN, HEADS, HD)
    queries = heads_of(projected[:, :, 0] + qv_bias[0])
    key_heads = heads_of(projected[:, :, 1])
    values = heads_of(projected[:, :, 2] + qv_bias[1])
    scores = jnp.einsum('tqhd,tkhd->thqk', queries, key_heads, precision=highest) * HD ** (-0.5) + rel_table[:, relative_code()]
    scores = low_back(scores)
    region_grid = to_windows(region_codes(0, NH, COLS, NH)[:, :, None])[:, :, 0]
    allowed = (region_grid[:, :, None] == region_grid[:, None, :])[:, None]
    weights = jax.nn.softmax(jnp.where(allowed, scores, masked_score), axis=-1)
    attended = jnp.einsum('thqk,tkhd->tqhd', low(weights), values, precision=highest)
    attended = low(low_back(attended)).reshape(window_count, WIN * WIN, D)
    projected_out = low_back(jnp.einsum('tnc,cd->tnd', attended, out_weight, precision=highest))
    branch_one = from_windows(projected_out, NH, COLS) + out_bias
    resid_one = merged + branch_one
    normed_two = low(layer_norm(low(resid_one), norm_gain[1], norm_shift[1]))
    hidden_pre = low_back(jnp.einsum('rwc,cf->rwf', normed_two, up_weight, precision=highest) + up_bias)
    hidden = low(jax.nn.gelu(hidden_pre, approximate=False))
    branch_two = low_back(jnp.einsum('rwf,fd->rwd', hidden, down_weight, precision=highest)) + down_bias
    resid_two = resid_one + branch_two
    return (jnp.roll(resid_two, (SHIFT, SHIFT), axis=(0, 1)), (branch_one, branch_two))

def reference(pages, merge_gain, merge_shift, merge_weight, norm_gain, norm_shift, qkv_weight, qv_bias, rel_table, out_weight, out_bias, up_weight, up_bias, down_weight, down_bias, cotangent):
    inputs_float = tuple((argument.astype(jnp.float32) for argument in (pages, merge_gain, merge_shift, merge_weight, norm_gain, norm_shift, qkv_weight, qv_bias, rel_table, out_weight, out_bias, up_weight, up_bias, down_weight, down_bias)))
    block_out, pullback, branches = jax.vjp(forward, *inputs_float, has_aux=True)
    gradients = pullback(cotangent.astype(jnp.float32))
    branch_rms = jnp.sqrt(jnp.stack([jnp.mean(block_out * block_out), jnp.mean(branches[0] * branches[0]), jnp.mean(branches[1] * branches[1])]))
    return (block_out, gradients[0], gradients[1], gradients[2], gradients[3], gradients[4], gradients[5], gradients[6], gradients[7], gradients[8], gradients[9], gradients[10], gradients[11], gradients[12], gradients[13], gradients[14], branch_rms)
```

```python
import functools

import jax
import jax.numpy as jnp
import numpy as np
from jax import lax
from jax.experimental import pallas as pl
from jax.experimental.pallas import tpu as pltpu
from jax.sharding import PartitionSpec as P

D = 512
HEADS = 16
HD = 32
FF = 2048
WIN = 7
SHIFT = 3
COLS = 42
ROWS = 14
WC = COLS // WIN
SLOT = 8
PAIR = 2 * WIN * SLOT
NPAIR = WC
T = PAIR * NPAIR
BAND = WC * WIN * SLOT
CHUNKS = 4
CH = D // CHUNKS
HEADS_C = HEADS // CHUNKS
LIFT = 2 * SHIFT
EPS = 1e-05
MASKED = -1e9
SCALE = HD ** (-0.5)
F32 = jnp.float32
BF16 = jnp.bfloat16


def dot(a, b):
    return jnp.dot(a, b, preferred_element_type=F32)


def dot_nt(a, b):
    return lax.dot_general(a, b, (((1,), (1,)), ((), ())), preferred_element_type=F32)


def dot_tn(a, b):
    return lax.dot_general(a, b, (((0,), (0,)), ((), ())), preferred_element_type=F32)


def constants():
    slots = np.arange(WC * SLOT)
    column = slots // SLOT * WIN + slots % SLOT
    real = slots % SLOT < WIN
    pages_sel = np.zeros((2, WC * SLOT, 2 * COLS), np.float32)
    for parity in range(2):
        source = (2 * column + parity + LIFT) % (2 * COLS)
        pages_sel[parity, slots[real], source[real]] = 1
    pages_sel = pages_sel.reshape(2 * WC * SLOT, 2 * COLS)
    token_sel = np.zeros((WC * SLOT, COLS), np.float32)
    source = (column + SHIFT) % COLS
    token_sel[slots[real], source[real]] = 1
    table_sel = np.zeros((256, SLOT, 128), np.float32)
    for b_q in range(WIN):
        for i in range(2 * WIN - 1):
            for b_k in range(WIN):
                code = (12 - i) * 13 + b_q - b_k + 6
                table_sel[code, b_q, i * SLOT + b_k] = 1
    table_sel = table_sel.reshape(256, SLOT * 128)
    return [jnp.asarray(a, BF16) for a in (pages_sel, pages_sel.T, token_sel, token_sel.T, table_sel)]


def iota(shape, dim):
    return lax.broadcasted_iota(jnp.int32, shape, dim)


def gelu_parts(x):
    z = jnp.abs(x) * (0.5**0.5)
    t = 1.0 / (1.0 + 0.3275911 * z)
    e = jnp.exp(-z * z)
    poly = t * (0.254829592 + t * (-0.284496736 + t * (1.421413741 + t * (-1.453152027 + t * 1.061405429))))
    tail = 0.5 * poly * e
    cdf = jnp.where(x >= 0, 1.0 - tail, tail)
    return x * cdf, cdf + x * e * 0.3989422804014327


def unit_of(x):
    centered = x - jnp.mean(x, -1, keepdims=True)
    inverse = lax.rsqrt(jnp.mean(centered * centered, -1, keepdims=True) + EPS)
    return centered * inverse, inverse


def norm_back(dy, u, inverse, gain):
    scaled = dy * gain
    first = jnp.mean(scaled, -1, keepdims=True)
    second = jnp.mean(scaled * u, -1, keepdims=True)
    return inverse * (scaled - first - u * second)


def col_sum(x):
    return jnp.sum(x, 0, keepdims=True)


def pair_mask(p, last_chan):
    q, k = iota((PAIR, 128), 0), iota((PAIR, 128), 1)
    half = PAIR // 2
    win_q, win_k = q // half, k // half
    a_q, a_k = (q % half) // SLOT, (k % half) // SLOT
    b_q, b_k = q % SLOT, k % SLOT
    w_col = (2 * p + win_q) % WC
    row_cut = jnp.logical_and(last_chan, 2 * p >= WC)
    ok = (win_q == win_k) & (k < PAIR) & (b_k < WIN)
    cut_r = WIN - SHIFT
    ok &= ((a_q < cut_r) == (a_k < cut_r)) | jnp.logical_not(row_cut)
    ok &= ((b_q < cut_r) == (b_k < cut_r)) | (w_col != WC - 1)
    return jnp.where(ok, 0.0, MASKED)


def head_lanes(x, h):
    lane = iota((1, CH), 1)
    return jnp.where(lane // HD == h, x, jnp.zeros_like(x))


def spread(x):
    padded = jnp.concatenate([x, jnp.zeros((128 - PAIR, CH), x.dtype)], 0)
    return jnp.concatenate([head_lanes(padded, h) for h in range(HEADS_C)], 0)


def stacked(x):
    return jnp.concatenate([head_lanes(x, h) for h in range(HEADS_C)], 0)


def by_head(x):
    return jnp.concatenate([x[:, 128 * h : 128 * h + 128] for h in range(HEADS_C)], 0)


def tile4(x):
    return jnp.concatenate([x] * HEADS_C, 1)


def rows_of(p, count=PAIR):
    return pl.ds(pl.multiple_of(p * count, 16), count)


SM_QV, SM_TABLE, SM_OUT_B, SM_UP_B, SM_DOWN_B = 0, 2, 10, 11, 15
RP_GAIN0, RP_SHIFT0, RP_GAIN, RP_SHIFT = 0, 1, 2, 4


def row_of(ref, c, first, count):
    return jnp.concatenate([ref[c, first + i : first + i + 1, :] for i in range(count)], 1)


def compute(
    pages, cot, merge_w, qkv_w, out_w, up_w, down_w, small, repl,
    pages_sel, pages_sel_t, token_sel, token_sel_t, table_sel,
    block_o, pages_o, d_merge_o, d_qkv_o, d_out_o, d_up_o, d_down_o, d_small_o, d_repl_o, squares_o,
    x0, inv0, mn, mt, u1, inv1, n1, qkv, prob, att, r1, u2, inv2, n2, g2, br2, dy2,
    gelu_d, hid, dpre, bias, lmat, gsum, dqkv, dy1, g1, g1f, gz, tmp,
):
    chan = lax.axis_index("chan")
    last_chan = chan == CHUNKS - 1
    valid = (iota((PAIR, 1), 0) % SLOT < WIN).astype(F32)

    def quads(i, _):
        base = (i // WIN) * BAND + (i % WIN) * SLOT
        for q in range(2):
            y = dot(pages_sel[...], pages[2 * i + q + LIFT])
            for par in range(2):
                for wc in range(WC):
                    lanes = par * 512 + q * 256
                    at = pl.multiple_of(base + wc * WIN * SLOT, SLOT)
                    first = par * WC * SLOT + wc * SLOT
                    x0[pl.ds(at, SLOT), lanes : lanes + 256] = y[first : first + SLOT]
        y = jnp.concatenate([dot(token_sel[...], cot[c, i]) for c in range(CHUNKS)], 1)
        for wc in range(WC):
            at = pl.multiple_of(base + wc * WIN * SLOT, SLOT)
            tmp[pl.ds(at, SLOT), 0:D] = y[wc * SLOT : wc * SLOT + SLOT]
        return 0

    lax.fori_loop(0, ROWS, quads, 0)

    def norm0(p, _):
        r = rows_of(p)
        u, inverse = unit_of(x0[r, :])
        x0[r, :] = u
        inv0[r, :] = inverse
        mn[r, :] = (u * repl[RP_GAIN0 : RP_GAIN0 + 1, :] + repl[RP_SHIFT0 : RP_SHIFT0 + 1, :]).astype(BF16)
        g2[r, :] = tmp[r, 0:D].astype(BF16)
        return 0

    lax.fori_loop(0, NPAIR, norm0, 0)
    mt[...] = dot(mn[...], merge_w[...]).astype(BF16)

    gain = [repl[RP_GAIN + i : RP_GAIN + i + 1, 0:D] for i in range(2)]
    shift = [repl[RP_SHIFT + i : RP_SHIFT + i + 1, 0:D] for i in range(2)]

    def norm1(p, _):
        r = rows_of(p)
        u, inverse = unit_of(mt[r, :].astype(F32))
        u1[r, :] = u
        inv1[r, :] = inverse
        n1[r, :] = (u * gain[0] + shift[0]).astype(BF16)
        return 0

    lax.fori_loop(0, NPAIR, norm1, 0)

    bias[...] = jnp.zeros_like(bias)

    def tables(c, _):
        table = jnp.concatenate([small[c, SM_TABLE : SM_TABLE + 4, :], small[c, SM_TABLE + 4 : SM_TABLE + 8, :]], 1)
        table = jnp.concatenate([table, jnp.zeros_like(table)], 0).astype(BF16)
        placed = dot(table, table_sel[...])
        for b_q in range(WIN):
            for h in range(HEADS_C):
                lmat[h * SLOT + b_q : h * SLOT + b_q + 1, :] = placed[h : h + 1, b_q * 128 : b_q * 128 + 128]
        for h in range(HEADS_C):
            tab = lmat[h * SLOT : h * SLOT + SLOT, :]
            lane = iota((SLOT, 128), 1)
            for a in range(WIN):
                moved = pltpu.roll(tab, (128 - (WIN - 1 - a) * SLOT) % 128, 1) if a < WIN - 1 else tab
                low = jnp.where(lane < WIN * SLOT, moved, 0.0)
                both = low + pltpu.roll(low, WIN * SLOT, 1)
                for half in range(2):
                    at = half * WIN * SLOT + a * SLOT
                    bias[c, at : at + SLOT, h * 128 : h * 128 + 128] = both
        return 0

    lmat[...] = jnp.zeros_like(lmat)
    lax.fori_loop(0, CHUNKS, tables, 0)

    def attend(c, _):
        projected = dot(n1[...], qkv_w[c])
        zeros = jnp.zeros((1, CH), F32)
        offset = jnp.concatenate([small[c, SM_QV : SM_QV + 1, :], zeros, small[c, SM_QV + 1 : SM_QV + 2, :]], 1)
        qkv[c] = (projected + offset).astype(BF16)

        def window_pair(p, _):
            r = rows_of(p)
            q, k, v = (qkv[c, r, i * CH : i * CH + CH] for i in range(3))
            s = dot_nt(q, spread(k)) * SCALE + bias[c] + tile4(pair_mask(p, last_chan))
            weights = []
            for h in range(HEADS_C):
                sh = s[:, 128 * h : 128 * h + 128]
                e = jnp.exp(sh - jnp.max(sh, -1, keepdims=True))
                weights.append((e * (1.0 / jnp.sum(e, -1, keepdims=True))).astype(BF16))
            w = jnp.concatenate(weights, 1)
            prob[c, p] = w
            att[c, r, :] = dot(w, spread(v)).astype(BF16)
            return 0

        lax.fori_loop(0, NPAIR, window_pair, 0)
        return 0

    lax.fori_loop(0, CHUNKS, attend, 0)

    def out_proj(j, _):
        tmp[:, 0:D] += dot(att[j], out_w[j])
        return 0

    tmp[:, 0:D] = jnp.zeros((T, D), F32)
    lax.fori_loop(0, CHUNKS, out_proj, 0)
    out_b = jnp.concatenate([small[c, SM_OUT_B : SM_OUT_B + 1, :] for c in range(CHUNKS)], 1)
    down_b = jnp.concatenate([small[c, SM_DOWN_B : SM_DOWN_B + 1, :] for c in range(CHUNKS)], 1)

    def norm2(p, total):
        r = rows_of(p)
        branch = tmp[r, 0:D] + out_b
        resid = mt[r, :].astype(F32) + branch
        r1[r, :] = resid
        u, inverse = unit_of(resid.astype(BF16).astype(F32))
        u2[r, :] = u
        inv2[r, :] = inverse
        n2[r, :] = (u * gain[1] + shift[1]).astype(BF16)
        return total + col_sum(branch * branch * valid)

    sq_one = lax.fori_loop(0, NPAIR, norm2, jnp.zeros((1, D), F32))

    br2[...] = jnp.zeros_like(br2)
    dy2[...] = jnp.zeros_like(dy2)

    def feed(c, _):
        tmp[:, 0:512] = dot(n2[...], up_w[c])
        tmp[:, 512:1024] = dot_nt(g2[...], down_w[c])
        up_b = row_of(small, c, SM_UP_B, 4)

        def gelus(p, total):
            r = rows_of(p)
            value, slope = gelu_parts(tmp[r, 0:512] + up_b)
            hid[r, :] = value.astype(BF16)
            d = slope * tmp[r, 512:1024]
            dpre[r, :] = d.astype(BF16)
            return total + col_sum(d)

        d_up_b = lax.fori_loop(0, NPAIR, gelus, jnp.zeros((1, 512), F32))
        for i in range(4):
            d_small_o[c, SM_UP_B + i : SM_UP_B + i + 1, :] = d_up_b[:, i * 128 : i * 128 + 128]
        br2[...] += dot(hid[...], down_w[c])
        d_down_o[c] = dot_tn(hid[...], g2[...]).astype(BF16)
        d_up_o[c] = dot_tn(n2[...], dpre[...]).astype(BF16)
        dy2[...] += dot_nt(dpre[...], up_w[c])
        return 0

    lax.fori_loop(0, CHUNKS, feed, 0)

    def norm2_back(p, carry):
        sq_two, sq_out, d_down_b, d_gain, d_shift, d_out_b = carry
        r = rows_of(p)
        branch = br2[r, :] + down_b
        result = r1[r, :] + branch
        r1[r, :] = result
        u = u2[r, :]
        dy = dy2[r, :]
        g = g2[r, :].astype(F32)
        grad = g + norm_back(dy, u, inv2[r, :], gain[1])
        g1f[r, :] = grad
        g1[r, :] = grad.astype(BF16)
        return (
            sq_two + col_sum(branch * branch * valid),
            sq_out + col_sum(result * result * valid),
            d_down_b + col_sum(g),
            d_gain + col_sum(dy * u),
            d_shift + col_sum(dy),
            d_out_b + col_sum(grad),
        )

    start = (jnp.zeros((1, D), F32),) * 6
    sq_two, sq_out, d_down_b, d_gain1, d_shift1, d_out_b = lax.fori_loop(0, NPAIR, norm2_back, start)
    for c in range(CHUNKS):
        d_small_o[c, SM_DOWN_B : SM_DOWN_B + 1, :] = d_down_b[:, c * CH : c * CH + CH]
        d_small_o[c, SM_OUT_B : SM_OUT_B + 1, :] = d_out_b[:, c * CH : c * CH + CH]
    squares_o[...] = jnp.zeros_like(squares_o)
    for i, sq in enumerate((sq_out, sq_one, sq_two)):
        squares_o[i : i + 1, :] = sq

    def block_rows(i, _):
        base = (i // WIN) * BAND + (i % WIN) * SLOT
        parts = [r1[pl.ds(pl.multiple_of(base + wc * WIN * SLOT, SLOT), SLOT), :] for wc in range(WC)]
        block_o[i] = dot(token_sel_t[...], jnp.concatenate(parts, 0).astype(BF16)).astype(BF16)
        return 0

    lax.fori_loop(0, ROWS, block_rows, 0)

    dy1[...] = jnp.zeros_like(dy1)

    def attend_back(c, _):
        d_out_o[c] = dot_tn(att[c], g1[...]).astype(BF16)
        hid[:, 0:CH] = dot_nt(g1[...], out_w[c]).astype(BF16)
        gsum[...] = jnp.zeros_like(gsum)

        def window_pair(p, _):
            r = rows_of(p)
            q, k, v = (qkv[c, r, i * CH : i * CH + CH] for i in range(3))
            d_att = hid[r, 0:CH]
            w = prob[c, p]
            d_w = dot_nt(d_att, spread(v))
            d_s = []
            for h in range(HEADS_C):
                wh = w[:, 128 * h : 128 * h + 128].astype(F32)
                gh = d_w[:, 128 * h : 128 * h + 128]
                d_s.append(wh * (gh - jnp.sum(gh * wh, -1, keepdims=True)))
            d_s = jnp.concatenate(d_s, 1)
            gsum[...] += d_s
            d_s = d_s.astype(BF16)
            d_q = dot(d_s, spread(k)) * SCALE
            d_k = dot_tn(by_head(d_s), stacked(q))[0:PAIR] * SCALE
            d_v = dot_tn(by_head(w), stacked(d_att))[0:PAIR]
            dqkv[r, :] = jnp.concatenate([d_q, d_k, d_v], 1).astype(BF16)
            return 0

        lax.fori_loop(0, NPAIR, window_pair, 0)
        d_qkv_o[c] = dot_tn(n1[...], dqkv[...]).astype(BF16)
        dy1[...] += dot_nt(dqkv[...], qkv_w[c])

        def sums(p, total):
            return total + col_sum(dqkv[rows_of(p), :].astype(F32))

        total = lax.fori_loop(0, NPAIR, sums, jnp.zeros((1, 3 * CH), F32))
        d_small_o[c, SM_QV : SM_QV + 1, :] = total[:, 0:CH]
        d_small_o[c, SM_QV + 1 : SM_QV + 2, :] = total[:, 2 * CH : 3 * CH]

        half = WIN * SLOT
        for h in range(HEADS_C):
            lanes = slice(h * 128, h * 128 + 128)
            folded = gsum[0:half, lanes] + pltpu.roll(gsum[half:PAIR, lanes], 128 - half, 1)
            acc = jnp.zeros((SLOT, 128), F32)
            for a in range(WIN):
                slab = folded[a * SLOT : a * SLOT + SLOT]
                moved = (WIN - 1 - a) * SLOT
                acc += pltpu.roll(slab, moved, 1) if moved else slab
            lmat[h * SLOT : h * SLOT + SLOT, :] = acc
        d_table = jnp.zeros((SLOT, 256), F32)
        for b_q in range(WIN):
            rows = [lmat[h * SLOT + b_q : h * SLOT + b_q + 1, :] for h in range(HEADS_C)]
            rows = jnp.concatenate(rows + [jnp.zeros((SLOT - HEADS_C, 128), F32)], 0)
            d_table += dot_nt(rows.astype(BF16), table_sel[:, b_q * 128 : b_q * 128 + 128])
        d_small_o[c, SM_TABLE : SM_TABLE + 4, :] = d_table[0:4, 0:128]
        d_small_o[c, SM_TABLE + 4 : SM_TABLE + 8, :] = d_table[0:4, 128:256]
        return 0

    lax.fori_loop(0, CHUNKS, attend_back, 0)

    def norm1_back(p, carry):
        d_gain, d_shift = carry
        r = rows_of(p)
        u = u1[r, :]
        dy = dy1[r, :]
        gz[r, :] = (g1f[r, :] + norm_back(dy, u, inv1[r, :], gain[0])).astype(BF16)
        return d_gain + col_sum(dy * u), d_shift + col_sum(dy)

    d_gain0, d_shift0 = lax.fori_loop(0, NPAIR, norm1_back, start[:2])

    d_merge_o[...] = dot_tn(mn[...], gz[...]).astype(BF16)
    tmp[...] = dot_nt(gz[...], merge_w[...])

    def norm0_back(p, carry):
        d_gain, d_shift = carry
        r = rows_of(p)
        u = x0[r, :]
        dy = tmp[r, :]
        tmp[r, :] = norm_back(dy, u, inv0[r, :], repl[RP_GAIN0 : RP_GAIN0 + 1, :])
        return d_gain + col_sum(dy * u), d_shift + col_sum(dy)

    start0 = (jnp.zeros((1, 1024), F32),) * 2
    d_gain_m, d_shift_m = lax.fori_loop(0, NPAIR, norm0_back, start0)
    d_repl_o[0:1, :] = d_gain_m
    d_repl_o[1:2, :] = d_shift_m
    d_repl_o[2:3, :] = jnp.concatenate([d_gain0, d_gain1], 1)
    d_repl_o[3:4, :] = jnp.concatenate([d_shift0, d_shift1], 1)
    d_repl_o[4:8, :] = jnp.zeros((4, 1024), F32)

    def page_rows(i, _):
        base = (i // WIN) * BAND + (i % WIN) * SLOT
        for q in range(2):
            parts = []
            for par in range(2):
                lanes = par * 512 + q * 256
                for wc in range(WC):
                    at = pl.multiple_of(base + wc * WIN * SLOT, SLOT)
                    parts.append(tmp[pl.ds(at, SLOT), lanes : lanes + 256])
            pages_o[2 * i + q] = dot(pages_sel_t[...], jnp.concatenate(parts, 0).astype(BF16))
        return 0

    lax.fori_loop(0, ROWS, page_rows, 0)


def kernel_call(args):
    vm = pl.BlockSpec(memory_space=pltpu.VMEM)
    s = jax.ShapeDtypeStruct
    outs = [
        s((ROWS, COLS, D), BF16),
        s((2 * ROWS, 2 * COLS, 256), F32),
        s((1024, D), BF16),
        s((CHUNKS, D, 3 * CH), BF16),
        s((CHUNKS, CH, D), BF16),
        s((CHUNKS, D, 512), BF16),
        s((CHUNKS, 512, D), BF16),
        s((CHUNKS, 16, 128), F32),
        s((8, 1024), F32),
        s((8, D), F32),
    ]
    v = pltpu.VMEM
    scratch = [
        v((T, 1024), F32), v((T, 1), F32), v((T, 1024), BF16), v((T, D), BF16),
        v((T, D), F32), v((T, 1), F32), v((T, D), BF16),
        v((CHUNKS, T, 3 * CH), BF16), v((CHUNKS, NPAIR, PAIR, 512), BF16), v((CHUNKS, T, CH), BF16),
        v((T, D), F32), v((T, D), F32), v((T, 1), F32), v((T, D), BF16), v((T, D), BF16),
        v((T, D), F32), v((T, D), F32),
        v((8, 128), F32), v((T, 512), BF16), v((T, 512), BF16),
        v((CHUNKS, PAIR, 512), F32), v((HEADS_C * SLOT, 128), F32), v((PAIR, 512), F32),
        v((T, 3 * CH), BF16), v((T, D), F32), v((T, D), BF16), v((T, D), F32), v((T, D), BF16),
        v((T, 1024), F32),
    ]
    return pl.pallas_call(
        compute,
        out_shape=outs,
        in_specs=[vm] * len(args),
        out_specs=[vm] * len(outs),
        scratch_shapes=scratch,
        compiler_params=pltpu.CompilerParams(vmem_limit_bytes=60 * 1024 * 1024),
    )(*args)


def shifted(shard, axis, by):
    count = lax.axis_size(axis)
    return lax.ppermute(shard, axis, [(i, (i + by) % count) for i in range(count)])


def pack_small(qv_bias, rel_table, out_bias, up_bias, down_bias):
    table = jnp.pad(rel_table, ((0, 0), (0, 256 - rel_table.shape[1])))
    parts = [qv_bias, table[:, :128], table[:, 128:], out_bias[None], up_bias.reshape(4, 128), down_bias[None]]
    return jnp.concatenate(parts, 0).astype(F32)


def body(
    pages, merge_gain, merge_shift, merge_weight, norm_gain, norm_shift, qkv_weight, qv_bias, rel_table,
    out_weight, out_bias, up_weight, up_bias, down_weight, down_bias, cotangent,
):
    small = pack_small(qv_bias, rel_table, out_bias, up_bias, down_bias)
    repl = jnp.concatenate(
        [merge_gain[None], merge_shift[None], jnp.pad(norm_gain, ((0, 0), (0, 512))), jnp.pad(norm_shift, ((0, 0), (0, 512)))], 0
    ).astype(F32)
    repl = jnp.pad(repl, ((0, 2), (0, 0)))
    gather = functools.partial(lax.all_gather, axis_name="chan", axis=0, tiled=False)
    pages_ext = jnp.concatenate([pages, shifted(pages[:LIFT], ("space", "chan"), -1)], 0)
    cot_ext = jnp.concatenate([cotangent[SHIFT:], shifted(cotangent[:SHIFT], "space", -1)], 0)
    cot = lax.all_to_all(cot_ext.reshape(CHUNKS, ROWS, COLS, CH), "chan", split_axis=0, concat_axis=0, tiled=True)
    args = [
        pages_ext, cot, merge_weight, gather(qkv_weight.reshape(D, 3 * CH)), gather(out_weight),
        gather(up_weight), gather(down_weight), gather(small), repl, *constants(),
    ]
    block, grad_pages, d_merge, d_qkv, d_out, d_up, d_down, d_small, d_repl, squares = kernel_call(args)
    block = lax.all_to_all(block, "chan", split_axis=2, concat_axis=0, tiled=True)
    block = jnp.concatenate([shifted(block[-SHIFT:], "space", 1), block[:-SHIFT]], 0).astype(F32)
    grad_pages = jnp.concatenate(
        [shifted(grad_pages[-LIFT:].astype(BF16), ("space", "chan"), 1).astype(F32), grad_pages[:-LIFT]], 0
    )

    def reduced(chunked):
        mine = lax.psum_scatter(chunked, "chan", scatter_dimension=0, tiled=False)
        return lax.psum(mine, "space").astype(F32)

    d_merge, d_repl, squares, d_small = lax.psum((d_merge, d_repl, squares, d_small), ("space", "chan"))
    d_small = lax.dynamic_index_in_dim(d_small, lax.axis_index("chan"), 0, keepdims=False)
    rms = jnp.sqrt(jnp.sum(squares[:3], 1) / float(1792 * COLS * D))
    table = jnp.concatenate([d_small[2:6], d_small[6:10]], 1)[:, :169]
    return (
        block, grad_pages, d_repl[0], d_repl[1], d_merge.astype(F32),
        d_repl[2].reshape(2, D), d_repl[3].reshape(2, D),
        reduced(d_qkv).reshape(D, 3, CH), d_small[0:2], table, reduced(d_out), d_small[10],
        reduced(d_up), d_small[11:15].reshape(512), reduced(d_down), d_small[15], rms,
    )


def solution(mesh):
    placed = (
        P(("space", "chan"), None, None), P(), P(), P(), P(), P(), P(None, None, "chan"), P(None, "chan"),
        P("chan", None), P("chan", None), P("chan"), P(None, "chan"), P("chan"), P("chan", None), P("chan"),
        P("space", None, "chan"),
    )
    outs = (
        P("space", None, "chan"), P(("space", "chan"), None, None), P(), P(), P(), P(), P(),
        P(None, None, "chan"), P(None, "chan"), P("chan", None), P("chan", None), P("chan"),
        P(None, "chan"), P("chan"), P("chan", None), P("chan"), P(),
    )
    return jax.shard_map(body, mesh=mesh, in_specs=placed, out_specs=outs, check_vma=False)
```

```python
import functools

import jax
import jax.numpy as jnp
import numpy as np
from jax import lax
from jax.experimental import pallas as pl
from jax.experimental.pallas import tpu as pltpu
from jax.sharding import PartitionSpec as P

D = 512
HEADS = 16
HD = 32
FF = 2048
WIN = 7
SHIFT = 3
COLS = 42
ROWS = 14
WC = COLS // WIN
SLOT = 8
PAIR = 2 * WIN * SLOT
NPAIR = WC
T = PAIR * NPAIR
BAND = WC * WIN * SLOT
CHUNKS = 4
CH = D // CHUNKS
HEADS_C = HEADS // CHUNKS
LIFT = 2 * SHIFT
EPS = 1e-05
MASKED = -1e9
SCALE = HD ** (-0.5)
F32 = jnp.float32
BF16 = jnp.bfloat16


def dot(a, b):
    return jnp.dot(a, b, preferred_element_type=F32)


def dot_nt(a, b):
    return lax.dot_general(a, b, (((1,), (1,)), ((), ())), preferred_element_type=F32)


def dot_tn(a, b):
    return lax.dot_general(a, b, (((0,), (0,)), ((), ())), preferred_element_type=F32)


def constants():
    slots = np.arange(WC * SLOT)
    column = slots // SLOT * WIN + slots % SLOT
    real = slots % SLOT < WIN
    pages_sel = np.zeros((2, WC * SLOT, 2 * COLS), np.float32)
    for parity in range(2):
        source = (2 * column + parity + LIFT) % (2 * COLS)
        pages_sel[parity, slots[real], source[real]] = 1
    pages_sel = pages_sel.reshape(2 * WC * SLOT, 2 * COLS)
    token_sel = np.zeros((WC * SLOT, COLS), np.float32)
    source = (column + SHIFT) % COLS
    token_sel[slots[real], source[real]] = 1
    table_sel = np.zeros((256, SLOT, 128), np.float32)
    for b_q in range(WIN):
        for i in range(2 * WIN - 1):
            for b_k in range(WIN):
                code = (12 - i) * 13 + b_q - b_k + 6
                table_sel[code, b_q, i * SLOT + b_k] = 1
    table_sel = table_sel.reshape(256, SLOT * 128)
    return [jnp.asarray(a, BF16) for a in (pages_sel, pages_sel.T, token_sel, token_sel.T, table_sel)]


def iota(shape, dim):
    return lax.broadcasted_iota(jnp.int32, shape, dim)


def gelu_parts(x):
    z = jnp.abs(x) * (0.5**0.5)
    t = 1.0 / (1.0 + 0.3275911 * z)
    e = jnp.exp(-z * z)
    poly = t * (0.254829592 + t * (-0.284496736 + t * (1.421413741 + t * (-1.453152027 + t * 1.061405429))))
    tail = 0.5 * poly * e
    cdf = jnp.where(x >= 0, 1.0 - tail, tail)
    return x * cdf, cdf + x * e * 0.3989422804014327


def unit_of(x):
    centered = x - jnp.mean(x, -1, keepdims=True)
    inverse = lax.rsqrt(jnp.mean(centered * centered, -1, keepdims=True) + EPS)
    return centered * inverse, inverse


def norm_back(dy, u, inverse, gain):
    scaled = dy * gain
    first = jnp.mean(scaled, -1, keepdims=True)
    second = jnp.mean(scaled * u, -1, keepdims=True)
    return inverse * (scaled - first - u * second)


def col_sum(x):
    return jnp.sum(x, 0, keepdims=True)


def pair_mask(p, last_chan):
    q, k = iota((PAIR, 128), 0), iota((PAIR, 128), 1)
    half = PAIR // 2
    win_q, win_k = q // half, k // half
    a_q, a_k = (q % half) // SLOT, (k % half) // SLOT
    b_q, b_k = q % SLOT, k % SLOT
    w_col = (2 * p + win_q) % WC
    row_cut = jnp.logical_and(last_chan, 2 * p >= WC)
    ok = (win_q == win_k) & (k < PAIR) & (b_k < WIN)
    cut_r = WIN - SHIFT
    ok &= ((a_q < cut_r) == (a_k < cut_r)) | jnp.logical_not(row_cut)
    ok &= ((b_q < cut_r) == (b_k < cut_r)) | (w_col != WC - 1)
    return jnp.where(ok, 0.0, MASKED)


def head_lanes(x, h):
    lane = iota((1, CH), 1)
    return jnp.where(lane // HD == h, x, jnp.zeros_like(x))


def spread(x):
    padded = jnp.concatenate([x, jnp.zeros((128 - PAIR, CH), x.dtype)], 0)
    return jnp.concatenate([head_lanes(padded, h) for h in range(HEADS_C)], 0)


def stacked(x):
    return jnp.concatenate([head_lanes(x, h) for h in range(HEADS_C)], 0)


def by_head(x):
    return jnp.concatenate([x[:, 128 * h : 128 * h + 128] for h in range(HEADS_C)], 0)


def tile4(x):
    return jnp.concatenate([x] * HEADS_C, 1)


def rows_of(p, count=PAIR):
    return pl.ds(pl.multiple_of(p * count, 16), count)


SM_QV, SM_TABLE, SM_OUT_B, SM_UP_B, SM_DOWN_B = 0, 2, 10, 11, 15
RP_GAIN0, RP_SHIFT0, RP_GAIN, RP_SHIFT = 0, 1, 2, 4


def row_of(ref, c, first, count):
    return jnp.concatenate([ref[c, first + i : first + i + 1, :] for i in range(count)], 1)


MESH = pl.DeviceIdType.MESH
HALF = 256
PEERS = CHUNKS - 1


class Sems:
    def __init__(self):
        self.count = 0

    def take(self, n):
        self.count += n
        return self.count - n


IDS = Sems()
ID_PAGES = IDS.take(1)
ID_SMALL = IDS.take(PEERS)
ID_W = IDS.take(4 * PEERS)
ID_WF = IDS.take(4 * PEERS)
ID_COT_HALO = IDS.take(1)
ID_COT = IDS.take(PEERS)
ID_BLK = IDS.take(PEERS)
ID_BLK_HALO = IDS.take(1)
ID_CORE = IDS.take(4 * CHUNKS)
ID_CORE_M = IDS.take(1)
ID_Y = IDS.take(4 * PEERS)
ID_Y_M = IDS.take(PEERS)
ID_RZ = IDS.take(2 * PEERS)
ID_RX = IDS.take(2 * PEERS)
ID_GX = IDS.take(2 * PEERS)
ID_GZ = IDS.take(2 * PEERS)
ID_GC = IDS.take(2)
ID_GY_M = IDS.take(PEERS)
ID_GC_M = IDS.take(1)
ID_PG = IDS.take(1)
ID_SG_C = IDS.take(1)
ID_SG_Y = IDS.take(PEERS)
ID_SG_Z = IDS.take(PEERS)
ID_SG_X = IDS.take(PEERS)
LOCAL = 16
QKV, OUT, UP, DOWN = 0, 1, 2, 3

SG_CHUNK, SG_REPL, SG_SQ, SG_ROWS = 0, 64, 96, 104


def chunk_off(j):
    return lax.rem(3 * j, 5) - 2 * (j // 3)


def back_off(j):
    return lax.rem(j + 1, CHUNKS)


def compute(
    pages_in, cot_in, merge_in, qkv_in, out_in, up_in, down_in, small_in, repl,
    pages_sel, pages_sel_t, token_sel, token_sel_t, table_sel,
    block_o, pages_o, mlp_o, attn_o, merge_o, small_o,
    pages, cot_v, cot, merge_w, qkv_w, out_w, up_w, down_w, small,
    x0, inv0, mn, mt, n1, qkv, prob, att, r1, u2, inv2, n2, g2, br2, dy2,
    hid, dpre, bias, lmat, gsum, dqkv, g1, gz, tmp,
    blk_tx, blk_rx, pg,
    d_merge, d_qkv, d_out, d_up, d_down, d_small, d_repl,
    l1_qkv, l1_out, l1_up, l1_down, l1_m, l2_qkv, l2_out, l2_up, l2_down, l2_m,
    ga, rza, hza, rxa, gfa, gb, rzb, hzb, rxb, gfb, mf,
    sg, sg_c, sg_y, sg_z, sg_x,
    ssem, rsem, lsem,
):
    chan = lax.axis_index("chan")
    space = lax.axis_index("space")
    n_space = lax.axis_size("space")
    core = lax.rem(space, 2)
    z = lax.rem(space // 2, 4)
    x = space // 8
    last_chan = chan == CHUNKS - 1
    valid = (iota((PAIR, 1), 0) % SLOT < WIN).astype(F32)

    def at_y(d):
        return (space, lax.rem(chan + d, CHUNKS))

    def at_z(d):
        return (x * 8 + lax.rem(z + d, 4) * 2 + core, chan)

    def at_x(d):
        return (lax.rem(x + d, 4) * 8 + z * 2 + core, chan)

    sibling = (x * 8 + z * 2 + 1 - core, chan)
    up_band = (lax.rem(space + n_space - 1, n_space), chan)
    down_band = (lax.rem(space + 1, n_space), chan)
    rank = space * CHUNKS + chan
    n_rank = n_space * CHUNKS
    before = lax.rem(rank + n_rank - 1, n_rank)
    after = lax.rem(rank + 1, n_rank)
    up_rank = (before // CHUNKS, lax.rem(before, CHUNKS))
    down_rank = (after // CHUNKS, lax.rem(after, CHUNKS))

    def send(src, dst, n, device):
        return pltpu.make_async_remote_copy(
            src_ref=src, dst_ref=dst, send_sem=ssem.at[n], recv_sem=rsem.at[n], device_id=device, device_id_type=MESH
        )

    def local(src, dst, n):
        return pltpu.make_async_copy(src, dst, lsem.at[n])

    own_pages = local(pages_in, pages.at[pl.ds(0, 2 * ROWS)], 0)
    own_merge = local(merge_in, merge_w, 1)
    own_w = [
        local(src, dst.at[chan], 2 + i)
        for i, (src, dst) in enumerate(((qkv_in, qkv_w), (out_in, out_w), (up_in, up_w), (down_in, down_w)))
    ]
    own_small = local(small_in, small.at[chan], 6)
    own_cot = local(cot_in, cot_v.at[pl.ds(0, 4 * ROWS)], 7)
    for copy in (own_pages, own_merge, own_small, own_w[QKV], own_w[OUT], own_cot, own_w[UP], own_w[DOWN]):
        copy.start()

    barrier = pltpu.get_barrier_semaphore()
    greeted = [at_y(d) for d in (1, 2, 3)] + [at_z(d) for d in (1, 2, 3)] + [at_x(d) for d in (1, 2, 3)]
    greeted += [sibling, up_band, down_band, up_rank, down_rank]
    for device in greeted:
        pl.semaphore_signal(barrier, inc=1, device_id=device, device_id_type=MESH)
    pl.semaphore_wait(barrier, len(greeted))

    halves = (HALF, CH // 2, HALF, HALF)

    def half_of(ref, w, c, k):
        rows = pl.ds(pl.multiple_of(k * halves[w], 16), halves[w])
        return ref.at[c, :, rows] if w == QKV else ref.at[c, rows]

    weights = (qkv_w, out_w, up_w, down_w)
    sources = (qkv_in, out_in, up_in, down_in)

    def weight_copy(w, d):
        rows = pl.ds(pl.multiple_of(core * halves[w], 16), halves[w])
        src = sources[w].at[:, rows] if w == QKV else sources[w].at[rows]
        return send(src, half_of(weights[w], w, chan, core), ID_W + w * PEERS + d - 1, at_y(d))

    def arrived(w, d, c):
        part = half_of(weights[w], w, c, core)
        send(part, part, ID_W + w * PEERS + d - 1, at_y(d)).wait_recv()

    def forward_copy(w, d, c):
        part = half_of(weights[w], w, c, core)
        return send(part, part, ID_WF + w * PEERS + d - 1, sibling)

    def forwarded(w, d, c):
        part = half_of(weights[w], w, c, 1 - core)
        send(part, part, ID_WF + w * PEERS + d - 1, sibling).wait_recv()

    def pass_on(w, j):
        off = chunk_off(j)
        c, d = lax.rem(chan + off, CHUNKS), CHUNKS - off
        arrived(w, d, c)
        forward_copy(w, d, c).start()

    def have(w, j):
        off = chunk_off(j)
        forwarded(w, CHUNKS - off, lax.rem(chan + off, CHUNKS))

    pages_halo = send(pages_in.at[pl.ds(0, LIFT)], pages.at[pl.ds(2 * ROWS, LIFT)], ID_PAGES, up_rank)
    pages_halo.start()
    small_copies = [send(small_in, small.at[chan], ID_SMALL + d - 1, at_y(d)) for d in (1, 3, 2)]
    cot_halo = send(cot_in.at[pl.ds(0, SHIFT)], cot_v.at[pl.ds(4 * ROWS, SHIFT)], ID_COT_HALO, up_band)
    weight_copies = [[weight_copy(w, d) for d in (1, 3, 2)] for w in range(4)]
    for copy in small_copies + weight_copies[QKV] + [cot_halo] + weight_copies[OUT]:
        copy.start()

    def quads(i, _):
        base = (i // WIN) * BAND + lax.rem(i, WIN) * SLOT
        for q in range(2):
            y = dot(pages_sel[...], pages[2 * i + q + LIFT])
            for par in range(2):
                for wc in range(WC):
                    lanes = par * 512 + q * 256
                    at = pl.multiple_of(base + wc * WIN * SLOT, SLOT)
                    first = par * WC * SLOT + wc * SLOT
                    x0[pl.ds(at, SLOT), lanes : lanes + 256] = y[first : first + SLOT]
        return 0

    own_pages.wait()
    whole = ROWS - LIFT // 2
    lax.fori_loop(0, whole, quads, 0)
    pages_halo.wait_recv()
    lax.fori_loop(whole, ROWS, quads, 0)

    def norm0(p, _):
        r = rows_of(p)
        u, inverse = unit_of(x0[r, :])
        x0[r, :] = u
        inv0[r, :] = inverse
        mn[r, :] = (u * repl[RP_GAIN0 : RP_GAIN0 + 1, :] + repl[RP_SHIFT0 : RP_SHIFT0 + 1, :]).astype(BF16)
        return 0

    lax.fori_loop(0, NPAIR, norm0, 0)
    own_merge.wait()
    mt[...] = dot(mn[...], merge_w[...]).astype(BF16)

    gain = [repl[RP_GAIN + i : RP_GAIN + i + 1, 0:D] for i in range(2)]
    shift = [repl[RP_SHIFT + i : RP_SHIFT + i + 1, 0:D] for i in range(2)]

    def norm1(p, _):
        r = rows_of(p)
        u, _inverse = unit_of(mt[r, :].astype(F32))
        n1[r, :] = (u * gain[0] + shift[0]).astype(BF16)
        return 0

    lax.fori_loop(0, NPAIR, norm1, 0)

    for copy in weight_copies[UP]:
        copy.start()

    own_cot.wait()
    cot_halo.wait_recv()

    def cot_rows(c):
        return cot_v.at[pl.ds(ROWS * c + SHIFT, ROWS)]

    cot_copies = [send(cot_rows(lax.rem(chan + d, CHUNKS)), cot.at[chan], ID_COT + d - 1, at_y(d)) for d in (1, 3, 2)]
    for copy in cot_copies:
        copy.start()
    cot_own = local(cot_rows(chan), cot.at[chan], 8)
    cot_own.start()

    own_small.wait()
    for d in (1, 2, 3):
        part = small.at[lax.rem(chan + CHUNKS - d, CHUNKS)]
        send(part, part, ID_SMALL + d - 1, at_y(d)).wait_recv()
    bias[...] = jnp.zeros_like(bias)
    lmat[...] = jnp.zeros_like(lmat)

    def tables(c, _):
        table = jnp.concatenate([small[c, SM_TABLE : SM_TABLE + 4, :], small[c, SM_TABLE + 4 : SM_TABLE + 8, :]], 1)
        table = jnp.concatenate([table, jnp.zeros_like(table)], 0).astype(BF16)
        placed = dot(table, table_sel[...])
        for b_q in range(WIN):
            for h in range(HEADS_C):
                lmat[h * SLOT + b_q : h * SLOT + b_q + 1, :] = placed[h : h + 1, b_q * 128 : b_q * 128 + 128]
        for h in range(HEADS_C):
            tab = lmat[h * SLOT : h * SLOT + SLOT, :]
            lane = iota((SLOT, 128), 1)
            for a in range(WIN):
                moved = pltpu.roll(tab, (128 - (WIN - 1 - a) * SLOT) % 128, 1) if a < WIN - 1 else tab
                low = jnp.where(lane < WIN * SLOT, moved, 0.0)
                both = low + pltpu.roll(low, WIN * SLOT, 1)
                for half in range(2):
                    at = half * WIN * SLOT + a * SLOT
                    bias[c, at : at + SLOT, h * 128 : h * 128 + 128] = both
        return 0

    lax.fori_loop(0, CHUNKS, tables, 0)

    def wide(c):
        return jnp.concatenate([qkv_w[c, i] for i in range(3)], 1)

    own_w[QKV].wait()

    def attend(j, _):
        c = lax.rem(chan + chunk_off(j), CHUNKS)

        @pl.when(j > 0)
        def _():
            have(QKV, j)

        projected = dot(n1[...], wide(c))
        zeros = jnp.zeros((1, CH), F32)
        offset = jnp.concatenate([small[c, SM_QV : SM_QV + 1, :], zeros, small[c, SM_QV + 1 : SM_QV + 2, :]], 1)
        qkv[c] = (projected + offset).astype(BF16)

        @pl.when(j < PEERS)
        def _():
            pass_on(QKV, j + 1)

        def window_pair(p, _):
            r = rows_of(p)
            q, k, v = (qkv[c, r, i * CH : i * CH + CH] for i in range(3))
            s = dot_nt(q, spread(k)) * SCALE + bias[c] + tile4(pair_mask(p, last_chan))
            weights = []
            for h in range(HEADS_C):
                sh = s[:, 128 * h : 128 * h + 128]
                e = jnp.exp(sh - jnp.max(sh, -1, keepdims=True))
                weights.append((e * (1.0 / jnp.sum(e, -1, keepdims=True))).astype(BF16))
            w = jnp.concatenate(weights, 1)
            prob[c, p] = w
            att[c, r, :] = dot(w, spread(v)).astype(BF16)
            return 0

        lax.fori_loop(0, NPAIR, window_pair, 0)

        @pl.when(j == 0)
        def _():
            for copy in weight_copies[DOWN]:
                copy.start()

        @pl.when(j < PEERS)
        def _():
            pass_on(OUT, j + 1)

        return 0

    lax.fori_loop(0, CHUNKS, attend, 0)

    tmp[:, 0:D] = jnp.zeros((T, D), F32)
    own_w[OUT].wait()

    def out_proj(j, _):
        c = lax.rem(chan + chunk_off(j), CHUNKS)

        @pl.when(j > 0)
        def _():
            have(OUT, j)

        tmp[:, 0:D] += dot(att[c], out_w[c])
        return 0

    lax.fori_loop(0, CHUNKS, out_proj, 0)
    out_b = jnp.concatenate([small[c, SM_OUT_B : SM_OUT_B + 1, :] for c in range(CHUNKS)], 1)
    down_b = jnp.concatenate([small[c, SM_DOWN_B : SM_DOWN_B + 1, :] for c in range(CHUNKS)], 1)

    def norm2(p, total):
        r = rows_of(p)
        branch = tmp[r, 0:D] + out_b
        resid = mt[r, :].astype(F32) + branch
        r1[r, :] = resid
        u, inverse = unit_of(resid.astype(BF16).astype(F32))
        u2[r, :] = u
        inv2[r, :] = inverse
        n2[r, :] = (u * gain[1] + shift[1]).astype(BF16)
        return total + col_sum(branch * branch * valid)

    sq_one = lax.fori_loop(0, NPAIR, norm2, jnp.zeros((1, D), F32))

    cot_own.wait()
    for d in (1, 2, 3):
        part = cot.at[lax.rem(chan + CHUNKS - d, CHUNKS)]
        send(part, part, ID_COT + d - 1, at_y(d)).wait_recv()

    def cot_slots(i, _):
        base = (i // WIN) * BAND + lax.rem(i, WIN) * SLOT
        y = jnp.concatenate([dot(token_sel[...], cot[c, i]) for c in range(CHUNKS)], 1)
        for wc in range(WC):
            at = pl.multiple_of(base + wc * WIN * SLOT, SLOT)
            tmp[pl.ds(at, SLOT), 0:D] = y[wc * SLOT : wc * SLOT + SLOT]
        return 0

    lax.fori_loop(0, ROWS, cot_slots, 0)
    g2[...] = tmp[:, 0:D].astype(BF16)

    grads = (d_qkv, d_out, d_up, d_down)
    firsts = (l1_qkv, l1_out, l1_up, l1_down)
    seconds = (l2_qkv, l2_out, l2_up, l2_down)

    def half_grad(w, c, k):
        return grads[w].at[c, pl.ds(pl.multiple_of(k * halves[w], 16), halves[w])]

    def core_copy(w, j, c):
        return send(half_grad(w, c, 1 - core), firsts[w].at[j], ID_CORE + w * CHUNKS + j, sibling)

    def owner_copy(w, off):
        c = lax.rem(chan + off, CHUNKS)
        return send(half_grad(w, c, core), seconds[w].at[off - 1], ID_Y + w * PEERS + off - 1, at_y(off))

    def core_sum(w, j, off):
        c = lax.rem(chan + off, CHUNKS)
        core_copy(w, j, c).wait_recv()
        step = min(halves[w], 64)
        for t in range(0, halves[w], step):
            r = pl.ds(pl.multiple_of(core * halves[w] + t, 16), step)
            total = grads[w][c, r, :].astype(F32) + firsts[w][j, t : t + step, :].astype(F32)
            grads[w][c, r, :] = total.astype(BF16)

        @pl.when(off > 0)
        def _():
            owner_copy(w, off).start()

    def owner_sum(w, t, step):
        r = pl.ds(pl.multiple_of(core * halves[w] + t, 16), step)
        total = grads[w][chan, r, :].astype(F32)
        for d in range(PEERS):
            total += seconds[w][d, t : t + step, :].astype(F32)
        return total.astype(BF16)

    def owner_wait(w):
        for d in (1, 2, 3):
            part = seconds[w].at[d - 1]
            send(part, part, ID_Y + w * PEERS + d - 1, at_y(d)).wait_recv()

    br2[...] = jnp.zeros_like(br2)
    dy2[...] = jnp.zeros_like(dy2)
    own_w[UP].wait()
    own_w[DOWN].wait()

    def feed(j, _):
        c = lax.rem(chan + chunk_off(j), CHUNKS)

        @pl.when(j > 0)
        def _():
            have(UP, j)
            have(DOWN, j)

        tmp[:, 0:512] = dot(n2[...], up_w[c])
        tmp[:, 512:1024] = dot_nt(g2[...], down_w[c])

        @pl.when(j < PEERS)
        def _():
            pass_on(UP, j + 1)
            pass_on(DOWN, j + 1)

        up_b = row_of(small, c, SM_UP_B, 4)

        def gelus(p, total):
            r = rows_of(p)
            value, slope = gelu_parts(tmp[r, 0:512] + up_b)
            hid[r, :] = value.astype(BF16)
            d = slope * tmp[r, 512:1024]
            dpre[r, :] = d.astype(BF16)
            return total + col_sum(d)

        d_up_b = lax.fori_loop(0, NPAIR, gelus, jnp.zeros((1, 512), F32))
        for i in range(4):
            d_small[c, SM_UP_B + i : SM_UP_B + i + 1, :] = d_up_b[:, i * 128 : i * 128 + 128]
        d_down[c] = dot_tn(hid[...], g2[...]).astype(BF16)
        core_copy(DOWN, j, c).start()
        d_up[c] = dot_tn(n2[...], dpre[...]).astype(BF16)
        core_copy(UP, j, c).start()
        br2[...] += dot(hid[...], down_w[c])
        dy2[...] += dot_nt(dpre[...], up_w[c])

        @pl.when(j > 0)
        def _():
            core_sum(DOWN, j - 1, chunk_off(j - 1))
            core_sum(UP, j - 1, chunk_off(j - 1))

        return 0

    lax.fori_loop(0, CHUNKS, feed, 0)

    def norm2_back(p, carry):
        sq_two, sq_out, d_down_b, d_gain, d_shift, d_out_b = carry
        r = rows_of(p)
        branch = br2[r, :] + down_b
        result = r1[r, :] + branch
        r1[r, :] = result
        u = u2[r, :]
        dy = dy2[r, :]
        g = g2[r, :].astype(F32)
        grad = g + norm_back(dy, u, inv2[r, :], gain[1])
        tmp[r, 0:D] = grad
        g1[r, :] = grad.astype(BF16)
        return (
            sq_two + col_sum(branch * branch * valid),
            sq_out + col_sum(result * result * valid),
            d_down_b + col_sum(g),
            d_gain + col_sum(dy * u),
            d_shift + col_sum(dy),
            d_out_b + col_sum(grad),
        )

    start = (jnp.zeros((1, D), F32),) * 6
    sq_two, sq_out, d_down_b, d_gain1, d_shift1, d_out_b = lax.fori_loop(0, NPAIR, norm2_back, start)
    for c in range(CHUNKS):
        d_small[c, SM_DOWN_B : SM_DOWN_B + 1, :] = d_down_b[:, c * CH : c * CH + CH]
        d_small[c, SM_OUT_B : SM_OUT_B + 1, :] = d_out_b[:, c * CH : c * CH + CH]

    core_sum(DOWN, PEERS, 2)
    core_sum(UP, PEERS, 2)

    def block_rows(i, _):
        base = (i // WIN) * BAND + lax.rem(i, WIN) * SLOT
        parts = [r1[pl.ds(pl.multiple_of(base + wc * WIN * SLOT, SLOT), SLOT), :] for wc in range(WC)]
        y = dot(token_sel_t[...], jnp.concatenate(parts, 0).astype(BF16)).astype(BF16)
        for c in range(CHUNKS):
            blk_tx[c, i] = y[:, c * CH : c * CH + CH]
        return 0

    lax.fori_loop(0, ROWS, block_rows, 0)

    def blk_rows(c):
        return blk_rx.at[pl.ds(ROWS * c + SHIFT, ROWS)]

    blk_copies = [
        send(blk_tx.at[lax.rem(chan + d, CHUNKS)], blk_rows(chan), ID_BLK + d - 1, at_y(d)) for d in (1, 3, 2)
    ]
    for copy in blk_copies:
        copy.start()
    blk_own = local(blk_tx.at[chan], blk_rows(chan), 9)
    blk_own.start()

    planes = ((ga, rza, hza, rxa, gfa), (gb, rzb, hzb, rxb, gfb))

    def rz_copy(i, d):
        rows = pl.ds(pl.multiple_of(lax.rem(z + d, 4) * 64, 16), 64)
        return send(planes[i][0].at[rows], planes[i][1].at[d - 1], ID_RZ + i * PEERS + d - 1, at_z(d))

    def rx_copy(i, d):
        rows = pl.ds(pl.multiple_of(lax.rem(x + d, 4) * 16, 16), 16)
        return send(planes[i][2].at[rows], planes[i][3].at[d - 1], ID_RX + i * PEERS + d - 1, at_x(d))

    def gx_copy(i, d):
        part = planes[i][4].at[core, pl.ds(pl.multiple_of(z * 64 + x * 16, 16), 16)]
        return send(part, part, ID_GX + i * PEERS + d - 1, at_x(d))

    def gx_wait(i, d):
        part = planes[i][4].at[core, pl.ds(pl.multiple_of(z * 64 + lax.rem(x + 4 - d, 4) * 16, 16), 16)]
        send(part, part, ID_GX + i * PEERS + d - 1, at_x(d)).wait_recv()

    def gz_copy(i, d):
        part = planes[i][4].at[core, pl.ds(pl.multiple_of(z * 64, 16), 64)]
        return send(part, part, ID_GZ + i * PEERS + d - 1, at_z(d))

    def gz_wait(i, d):
        part = planes[i][4].at[core, pl.ds(pl.multiple_of(lax.rem(z + 4 - d, 4) * 64, 16), 64)]
        send(part, part, ID_GZ + i * PEERS + d - 1, at_z(d)).wait_recv()

    def gc_copy(i):
        part = planes[i][4].at[core]
        return send(part, part, ID_GC + i, sibling)

    def gc_wait(i):
        part = planes[i][4].at[1 - core]
        send(part, part, ID_GC + i, sibling).wait_recv()

    order = (1, 3, 2)

    def plane_rz(i):
        for d in order:
            rz_copy(i, d).start()

    def plane_rx(i):
        g, rz, hz = planes[i][0:3]
        for d in order:
            rz_copy(i, d).wait_recv()
        total = g[pl.ds(pl.multiple_of(z * 64, 16), 64), :].astype(F32)
        for d in range(PEERS):
            total += rz[d].astype(F32)
        hz[...] = total.astype(BF16)
        for d in order:
            rx_copy(i, d).start()

    def plane_gx(i):
        hz, rx, gf = planes[i][2:5]
        for d in order:
            rx_copy(i, d).wait_recv()
        total = hz[pl.ds(pl.multiple_of(x * 16, 16), 16), :].astype(F32)
        for d in range(PEERS):
            total += rx[d].astype(F32)
        gf[core, pl.ds(pl.multiple_of(z * 64 + x * 16, 16), 16), :] = total.astype(BF16)
        for d in order:
            gx_copy(i, d).start()

    def plane_gz(i):
        for d in order:
            gx_wait(i, d)
        for d in order:
            gz_copy(i, d).start()

    def plane_gc(i):
        for d in order:
            gz_wait(i, d)
        gc_copy(i).start()

    tmp[:, D : 2 * D] = jnp.zeros((T, D), F32)

    def attend_back(j, _):
        c = lax.rem(chan + back_off(j), CHUNKS)
        d_out[c] = dot_tn(att[c], g1[...]).astype(BF16)
        core_copy(OUT, j, c).start()
        hid[:, 0:CH] = dot_nt(g1[...], out_w[c]).astype(BF16)
        gsum[...] = jnp.zeros_like(gsum)

        def window_pair(p, _):
            r = rows_of(p)
            q, k, v = (qkv[c, r, i * CH : i * CH + CH] for i in range(3))
            d_att = hid[r, 0:CH]
            w = prob[c, p]
            d_w = dot_nt(d_att, spread(v))
            d_s = []
            for h in range(HEADS_C):
                wh = w[:, 128 * h : 128 * h + 128].astype(F32)
                gh = d_w[:, 128 * h : 128 * h + 128]
                d_s.append(wh * (gh - jnp.sum(gh * wh, -1, keepdims=True)))
            d_s = jnp.concatenate(d_s, 1)
            gsum[...] += d_s
            d_s = d_s.astype(BF16)
            d_q = dot(d_s, spread(k)) * SCALE
            d_k = dot_tn(by_head(d_s), stacked(q))[0:PAIR] * SCALE
            d_v = dot_tn(by_head(w), stacked(d_att))[0:PAIR]
            dqkv[r, :] = jnp.concatenate([d_q, d_k, d_v], 1).astype(BF16)
            return 0

        lax.fori_loop(0, NPAIR, window_pair, 0)
        d_qkv[c] = dot_tn(n1[...], dqkv[...]).astype(BF16)
        core_copy(QKV, j, c).start()
        tmp[:, D : 2 * D] += dot_nt(dqkv[...], wide(c))

        def sums(p, total):
            return total + col_sum(dqkv[rows_of(p), :].astype(F32))

        total = lax.fori_loop(0, NPAIR, sums, jnp.zeros((1, 3 * CH), F32))
        d_small[c, SM_QV : SM_QV + 1, :] = total[:, 0:CH]
        d_small[c, SM_QV + 1 : SM_QV + 2, :] = total[:, 2 * CH : 3 * CH]

        half = WIN * SLOT
        for h in range(HEADS_C):
            lanes = slice(h * 128, h * 128 + 128)
            folded = gsum[0:half, lanes] + pltpu.roll(gsum[half:PAIR, lanes], 128 - half, 1)
            acc = jnp.zeros((SLOT, 128), F32)
            for a in range(WIN):
                slab = folded[a * SLOT : a * SLOT + SLOT]
                moved = (WIN - 1 - a) * SLOT
                acc += pltpu.roll(slab, moved, 1) if moved else slab
            lmat[h * SLOT : h * SLOT + SLOT, :] = acc
        d_table = jnp.zeros((SLOT, 256), F32)
        for b_q in range(WIN):
            rows = [lmat[h * SLOT + b_q : h * SLOT + b_q + 1, :] for h in range(HEADS_C)]
            rows = jnp.concatenate(rows + [jnp.zeros((SLOT - HEADS_C, 128), F32)], 0)
            d_table += dot_nt(rows.astype(BF16), table_sel[:, b_q * 128 : b_q * 128 + 128])
        d_small[c, SM_TABLE : SM_TABLE + 4, :] = d_table[0:4, 0:128]
        d_small[c, SM_TABLE + 4 : SM_TABLE + 8, :] = d_table[0:4, 128:256]

        @pl.when(j > 0)
        def _():
            core_sum(OUT, j - 1, back_off(j - 1))
            core_sum(QKV, j - 1, back_off(j - 1))

        @pl.when(j == 0)
        def _():
            owner_wait(DOWN)
            owner_wait(UP)
            for t in range(0, HALF, 64):
                ga[t : t + 64, 0:512] = owner_sum(DOWN, t, 64)
                ga[t : t + 64, 512:1024] = owner_sum(UP, t, 64)
            plane_rz(0)

        @pl.when(j == 1)
        def _():
            plane_rx(0)

        @pl.when(j == 2)
        def _():
            plane_gx(0)

        @pl.when(j == 3)
        def _():
            plane_gz(0)

        return 0

    lax.fori_loop(0, CHUNKS, attend_back, 0)

    def norm1_back(p, carry):
        d_gain, d_shift = carry
        r = rows_of(p)
        u, inverse = unit_of(mt[r, :].astype(F32))
        dy = tmp[r, D : 2 * D]
        gz[r, :] = (tmp[r, 0:D] + norm_back(dy, u, inverse, gain[0])).astype(BF16)
        return d_gain + col_sum(dy * u), d_shift + col_sum(dy)

    d_gain0, d_shift0 = lax.fori_loop(0, NPAIR, norm1_back, start[:2])

    mine = pl.ds(pl.multiple_of(core * HALF, HALF), HALF)
    other = pl.ds(pl.multiple_of((1 - core) * HALF, HALF), HALF)
    merge_core = send(d_merge.at[:, other], l1_m, ID_CORE_M, sibling)
    d_merge[:, other] = dot_tn(mn[...], gz[:, other]).astype(BF16)
    merge_core.start()
    d_merge[:, mine] = dot_tn(mn[...], gz[:, mine]).astype(BF16)
    core_sum(OUT, PEERS, 0)
    core_sum(QKV, PEERS, 0)
    plane_gc(0)

    blk_own.wait()
    for d in (1, 2, 3):
        part = blk_rows(lax.rem(chan + CHUNKS - d, CHUNKS))
        send(part, part, ID_BLK + d - 1, at_y(d)).wait_recv()
    blk_halo = send(blk_rx.at[pl.ds(4 * ROWS, SHIFT)], blk_rx.at[pl.ds(0, SHIFT)], ID_BLK_HALO, down_band)
    blk_halo.start()

    merge_core.wait_recv()
    for t in range(0, 1024, 128):
        total = d_merge[t : t + 128, mine].astype(F32) + l1_m[t : t + 128, :].astype(F32)
        d_merge[t : t + 128, mine] = total.astype(BF16)

    def merge_owner(d):
        rows = pl.ds(pl.multiple_of(lax.rem(chan + d, CHUNKS) * HALF, HALF), HALF)
        return send(d_merge.at[rows, mine], l2_m.at[d - 1], ID_Y_M + d - 1, at_y(d))

    for d in order:
        merge_owner(d).start()

    tmp[...] = dot_nt(gz[...], merge_w[...])

    def norm0_back(p, carry):
        d_gain, d_shift = carry
        r = rows_of(p)
        u = x0[r, :]
        dy = tmp[r, :]
        tmp[r, :] = norm_back(dy, u, inv0[r, :], repl[RP_GAIN0 : RP_GAIN0 + 1, :])
        return d_gain + col_sum(dy * u), d_shift + col_sum(dy)

    start0 = (jnp.zeros((1, 1024), F32),) * 2
    d_gain_m, d_shift_m = lax.fori_loop(0, NPAIR, norm0_back, start0)

    for c in range(CHUNKS):
        sg[0, SG_CHUNK + 16 * c : SG_CHUNK + 16 * c + 16, :] = d_small[c]
    rows = [d_gain_m, d_shift_m, d_gain0, d_gain1, d_shift0, d_shift1]
    at = SG_REPL
    for row in rows:
        for i in range(row.shape[1] // 128):
            sg[0, at : at + 1, :] = row[:, i * 128 : i * 128 + 128]
            at += 1
    squares = [sum(sq[:, i * 128 : i * 128 + 128] for i in range(4)) for sq in (sq_out, sq_one, sq_two)]
    sg[0, SG_SQ:SG_ROWS, :] = jnp.concatenate(squares + [jnp.zeros((5, 128), F32)], 0)

    def sg_copies(level):
        if level == 0:
            return [send(sg.at[0], sg_c.at[0], ID_SG_C, sibling)]
        into, first, at = ((sg_y, ID_SG_Y, at_y), (sg_z, ID_SG_Z, at_z), (sg_x, ID_SG_X, at_x))[level - 1]
        return [send(sg.at[level], into.at[d - 1], first + d - 1, at(d)) for d in order]

    def sg_start(level):
        for copy in sg_copies(level):
            copy.start()

    def sg_sum(level):
        for copy in sg_copies(level):
            copy.wait_recv()
        into = (sg_c, sg_y, sg_z, sg_x)[level]
        total = sg[level]
        for d in range(into.shape[0]):
            total += into[d]
        sg[level + 1] = total

    sg_start(0)

    owner_wait(QKV)
    owner_wait(OUT)
    for t in range(0, HALF, 64):
        gb[t : t + 64, 0:384] = owner_sum(QKV, t, 64)
    out_half = owner_sum(OUT, 0, 64)
    for g in range(4):
        gb[g * 64 : g * 64 + 64, 384:512] = out_half[:, g * 128 : g * 128 + 128]
    for d in order:
        merge_owner(d).wait_recv()
    for t in range(0, HALF, 64):
        r = pl.ds(pl.multiple_of(chan * HALF + t, 16), 64)
        total = d_merge[r, mine].astype(F32)
        for d in range(PEERS):
            total += l2_m[d, t : t + 64, :].astype(F32)
        gb[t : t + 64, 512:768] = total.astype(BF16)
    plane_rz(1)
    sg_sum(0)
    sg_start(1)

    def page_rows(i, _):
        base = (i // WIN) * BAND + lax.rem(i, WIN) * SLOT
        for q in range(2):
            parts = []
            for par in range(2):
                lanes = par * 512 + q * 256
                for wc in range(WC):
                    at = pl.multiple_of(base + wc * WIN * SLOT, SLOT)
                    parts.append(tmp[pl.ds(at, SLOT), lanes : lanes + 256])
            y = dot(pages_sel_t[...], jnp.concatenate(parts, 0).astype(BF16))
            pg[2 * i + q + LIFT] = y.astype(BF16)
        return 0

    lax.fori_loop(0, ROWS, page_rows, 0)
    pg_halo = send(pg.at[pl.ds(2 * ROWS, LIFT)], pg.at[pl.ds(0, LIFT)], ID_PG, down_rank)
    pg_halo.start()

    plane_rx(1)
    sg_sum(1)
    sg_start(2)
    plane_gx(1)
    sg_sum(2)
    sg_start(3)
    plane_gz(1)

    blk_halo.wait_recv()
    block_copy = local(blk_rx.at[pl.ds(0, 4 * ROWS)], block_o, 10)
    block_copy.start()
    gc_wait(0)
    mlp_copy = local(gfa, mlp_o, 11)
    mlp_copy.start()
    pg_halo.wait_recv()
    pages_copy = local(pg.at[pl.ds(0, 2 * ROWS)], pages_o, 12)
    pages_copy.start()
    sg_sum(3)
    small_copy = local(sg.at[4], small_o, 13)
    small_copy.start()

    plane_gc(1)
    own_rows = pl.ds(pl.multiple_of(chan * HALF, HALF), HALF)
    mf[own_rows, mine] = gfb[core, :, 512:768]
    gy_copies = [send(mf.at[own_rows, mine], mf.at[own_rows, mine], ID_GY_M + d - 1, at_y(d)) for d in order]
    for copy in gy_copies:
        copy.start()
    for d in order:
        r = pl.ds(pl.multiple_of(lax.rem(chan + CHUNKS - d, CHUNKS) * HALF, HALF), HALF)
        send(mf.at[r, mine], mf.at[r, mine], ID_GY_M + d - 1, at_y(d)).wait_recv()
    gc_merge = send(mf.at[:, mine], mf.at[:, mine], ID_GC_M, sibling)
    gc_merge.start()
    gc_wait(1)
    attn_copy = local(gfb, attn_o, 14)
    attn_copy.start()
    send(mf.at[:, other], mf.at[:, other], ID_GC_M, sibling).wait_recv()
    merge_copy = local(mf, merge_o, 15)
    merge_copy.start()

    for copy in [pages_halo, cot_halo, blk_halo, pg_halo, merge_core, gc_merge] + small_copies + cot_copies + blk_copies:
        copy.wait_send()
    for w in range(4):
        for copy in weight_copies[w]:
            copy.wait_send()
        for d in order:
            forward_copy(w, d, lax.rem(chan + CHUNKS - d, CHUNKS)).wait_send()
            owner_copy(w, d).wait_send()
        for j in range(CHUNKS):
            off = chunk_off(j) if w in (UP, DOWN) else back_off(j)
            core_copy(w, j, lax.rem(chan + off, CHUNKS)).wait_send()
    for i in range(2):
        for d in order:
            for make in (rz_copy, rx_copy, gx_copy, gz_copy):
                make(i, d).wait_send()
        gc_copy(i).wait_send()
    for level in range(4):
        for copy in sg_copies(level):
            copy.wait_send()
    for d in order:
        merge_owner(d).wait_send()
    for copy in gy_copies:
        copy.wait_send()
    for copy in (block_copy, mlp_copy, pages_copy, small_copy, attn_copy, merge_copy):
        copy.wait()


def kernel_call(args):
    vm = pl.BlockSpec(memory_space=pltpu.VMEM)
    hbm = pl.BlockSpec(memory_space=pl.ANY)
    s = jax.ShapeDtypeStruct
    outs = [
        s((4 * ROWS, COLS, CH), BF16),
        s((2 * ROWS, 2 * COLS, 256), BF16),
        s((2, HALF, 1024), BF16),
        s((2, HALF, 768), BF16),
        s((1024, D), BF16),
        s((SG_ROWS, 128), F32),
    ]

    def v(shape, dtype):
        return pltpu.VMEM(shape, dtype)

    scratch = [
        v((2 * ROWS + LIFT, 2 * COLS, 256), BF16), v((4 * ROWS + SHIFT, COLS, CH), BF16), v((CHUNKS, ROWS, COLS, CH), BF16),
        v((1024, D), BF16), v((CHUNKS, 3, D, CH), BF16), v((CHUNKS, CH, D), BF16),
        v((CHUNKS, D, 512), BF16), v((CHUNKS, 512, D), BF16), v((CHUNKS, 16, 128), F32),
        v((T, 1024), F32), v((T, 1), F32), v((T, 1024), BF16), v((T, D), BF16), v((T, D), BF16),
        v((CHUNKS, T, 3 * CH), BF16), v((CHUNKS, NPAIR, PAIR, 512), BF16), v((CHUNKS, T, CH), BF16),
        v((T, D), F32), v((T, D), F32), v((T, 1), F32), v((T, D), BF16), v((T, D), BF16),
        v((T, D), F32), v((T, D), F32),
        v((T, 512), BF16), v((T, 512), BF16),
        v((CHUNKS, PAIR, 512), F32), v((HEADS_C * SLOT, 128), F32), v((PAIR, 512), F32),
        v((T, 3 * CH), BF16), v((T, D), BF16), v((T, D), BF16), v((T, 1024), F32),
        v((CHUNKS, ROWS, COLS, CH), BF16), v((4 * ROWS + SHIFT, COLS, CH), BF16),
        v((2 * ROWS + LIFT, 2 * COLS, 256), BF16),
        v((1024, D), BF16), v((CHUNKS, D, 3 * CH), BF16), v((CHUNKS, CH, D), BF16),
        v((CHUNKS, D, 512), BF16), v((CHUNKS, 512, D), BF16), v((CHUNKS, 16, 128), F32), v((8, 1024), F32),
        v((CHUNKS, HALF, 3 * CH), BF16), v((CHUNKS, CH // 2, D), BF16), v((CHUNKS, HALF, 512), BF16),
        v((CHUNKS, HALF, D), BF16), v((1024, HALF), BF16),
        v((PEERS, HALF, 3 * CH), BF16), v((PEERS, CH // 2, D), BF16), v((PEERS, HALF, 512), BF16),
        v((PEERS, HALF, D), BF16), v((PEERS, HALF, HALF), BF16),
    ]
    for lanes in (1024, 768):
        scratch += [
            v((HALF, lanes), BF16), v((PEERS, 64, lanes), BF16), v((64, lanes), BF16), v((PEERS, 16, lanes), BF16),
            v((2, HALF, lanes), BF16),
        ]
    scratch += [v((1024, D), BF16), v((5, SG_ROWS, 128), F32), v((1, SG_ROWS, 128), F32)]
    scratch += [v((PEERS, SG_ROWS, 128), F32)] * 3
    scratch += [
        pltpu.SemaphoreType.DMA((IDS.count,)),
        pltpu.SemaphoreType.DMA((IDS.count,)),
        pltpu.SemaphoreType.DMA((LOCAL,)),
    ]
    return pl.pallas_call(
        compute,
        out_shape=outs,
        in_specs=[hbm] * 8 + [vm] * (len(args) - 8),
        out_specs=[hbm] * len(outs),
        scratch_shapes=scratch,
        compiler_params=pltpu.CompilerParams(
            vmem_limit_bytes=63 * 1024 * 1024, collective_id=0, has_side_effects=True
        ),
    )(*args)


def pack_small(qv_bias, rel_table, out_bias, up_bias, down_bias):
    table = jnp.pad(rel_table, ((0, 0), (0, 256 - rel_table.shape[1])))
    parts = [qv_bias, table[:, :128], table[:, 128:], out_bias[None], up_bias.reshape(4, 128), down_bias[None]]
    return jnp.concatenate(parts, 0).astype(F32)


def body(
    pages, merge_gain, merge_shift, merge_weight, norm_gain, norm_shift, qkv_weight, qv_bias, rel_table,
    out_weight, out_bias, up_weight, up_bias, down_weight, down_bias, cotangent,
):
    small = pack_small(qv_bias, rel_table, out_bias, up_bias, down_bias)
    repl = jnp.concatenate(
        [merge_gain[None], merge_shift[None], jnp.pad(norm_gain, ((0, 0), (0, 512))), jnp.pad(norm_shift, ((0, 0), (0, 512)))], 0
    ).astype(F32)
    repl = jnp.pad(repl, ((0, 2), (0, 0)))
    args = [
        pages, cotangent, merge_weight, qkv_weight.transpose(1, 0, 2), out_weight,
        up_weight, down_weight, small, repl, *constants(),
    ]
    block, grad_pages, mlp, attn, d_merge, sums = kernel_call(args)
    chunk = lax.dynamic_slice_in_dim(sums, lax.axis_index("chan") * 16, 16, 0)
    rms = jnp.sqrt(jnp.sum(sums[SG_SQ : SG_SQ + 3], 1) / float(1792 * COLS * D))
    table = jnp.concatenate([chunk[2:6], chunk[6:10]], 1)[:, :169]
    norms = sums[SG_REPL : SG_REPL + 32].reshape(4, 1024)
    d_out = attn[:, :, 384:512].reshape(2, 4, 64, 128).transpose(0, 2, 1, 3).reshape(CH, D)
    return (
        block.astype(F32), grad_pages.astype(F32), norms[0], norms[1], d_merge.astype(F32),
        norms[2].reshape(2, D), norms[3].reshape(2, D),
        attn[:, :, 0:384].reshape(D, 3, CH).astype(F32), chunk[0:2], table, d_out.astype(F32), chunk[10],
        mlp[:, :, 512:1024].reshape(D, 512).astype(F32), chunk[11:15].reshape(512),
        mlp[:, :, 0:512].reshape(512, D).astype(F32), chunk[15], rms,
    )


def solution(mesh):
    placed = (
        P(("space", "chan"), None, None), P(), P(), P(), P(), P(), P(None, None, "chan"), P(None, "chan"),
        P("chan", None), P("chan", None), P("chan"), P(None, "chan"), P("chan"), P("chan", None), P("chan"),
        P("space", None, "chan"),
    )
    outs = (
        P("space", None, "chan"), P(("space", "chan"), None, None), P(), P(), P(), P(), P(),
        P(None, None, "chan"), P(None, "chan"), P("chan", None), P("chan", None), P("chan"),
        P(None, "chan"), P("chan"), P("chan", None), P("chan"), P(),
    )
    return jax.shard_map(body, mesh=mesh, in_specs=placed, out_specs=outs, check_vma=False)
```

```python
import functools

import jax
import jax.numpy as jnp
import numpy as np
from jax import lax
from jax.experimental import pallas as pl
from jax.experimental.pallas import tpu as pltpu
from jax.sharding import PartitionSpec as P

D = 512
HEADS = 16
HD = 32
FF = 2048
WIN = 7
SHIFT = 3
COLS = 42
ROWS = 14
WC = COLS // WIN
SLOT = 8
PAIR = 2 * WIN * SLOT
NPAIR = WC
T = PAIR * NPAIR
BAND = WC * WIN * SLOT
CHUNKS = 4
CH = D // CHUNKS
HEADS_C = HEADS // CHUNKS
LIFT = 2 * SHIFT
EPS = 1e-05
MASKED = -1e9
SCALE = HD ** (-0.5)
F32 = jnp.float32
BF16 = jnp.bfloat16


def dot(a, b):
    return jnp.dot(a, b, preferred_element_type=F32)


def dot_nt(a, b):
    return lax.dot_general(a, b, (((1,), (1,)), ((), ())), preferred_element_type=F32)


def dot_tn(a, b):
    return lax.dot_general(a, b, (((0,), (0,)), ((), ())), preferred_element_type=F32)


def constants():
    slots = np.arange(WC * SLOT)
    column = slots // SLOT * WIN + slots % SLOT
    real = slots % SLOT < WIN
    pages_sel = np.zeros((2, WC * SLOT, 2 * COLS), np.float32)
    for parity in range(2):
        source = (2 * column + parity + LIFT) % (2 * COLS)
        pages_sel[parity, slots[real], source[real]] = 1
    pages_sel = pages_sel.reshape(2 * WC * SLOT, 2 * COLS)
    table_sel = np.zeros((256, SLOT, 128), np.float32)
    for b_q in range(WIN):
        for i in range(2 * WIN - 1):
            for b_k in range(WIN):
                code = (12 - i) * 13 + b_q - b_k + 6
                table_sel[code, b_q, i * SLOT + b_k] = 1
    table_sel = table_sel.reshape(256, SLOT * 128)
    table_sel_t = np.zeros((256, SLOT, 128), np.float32)
    for b_k in range(WIN):
        for i in range(2 * WIN - 1):
            for b_q in range(WIN):
                table_sel_t[i * 13 + b_q - b_k + 6, b_k, i * SLOT + b_q] = 1
    table_sel_t = table_sel_t.reshape(256, SLOT * 128)
    arrays = (pages_sel, pages_sel.T, table_sel, table_sel_t)
    return [jnp.asarray(a, BF16) for a in arrays]


def iota(shape, dim):
    return lax.broadcasted_iota(jnp.int32, shape, dim)


def gelu_parts(x):
    z = jnp.abs(x) * (0.5**0.5)
    t = 1.0 / (1.0 + 0.3275911 * z)
    e = jnp.exp(-z * z)
    poly = t * (0.254829592 + t * (-0.284496736 + t * (1.421413741 + t * (-1.453152027 + t * 1.061405429))))
    tail = 0.5 * poly * e
    cdf = jnp.where(x >= 0, 1.0 - tail, tail)
    return x * cdf, cdf + x * e * 0.3989422804014327


def unit_of(x):
    centered = x - jnp.mean(x, -1, keepdims=True)
    inverse = lax.rsqrt(jnp.mean(centered * centered, -1, keepdims=True) + EPS)
    return centered * inverse, inverse


def norm_back(dy, u, inverse, gain):
    scaled = dy * gain
    first = jnp.mean(scaled, -1, keepdims=True)
    second = jnp.mean(scaled * u, -1, keepdims=True)
    return inverse * (scaled - first - u * second)


def col_sum(x):
    return jnp.sum(x, 0, keepdims=True)


def pair_mask(row_cut, col_cut):
    k, q = iota((128, 128), 0), iota((128, 128), 1)
    half = PAIR // 2
    win_q, win_k = q // half, k // half
    a_q, a_k = (q % half) // SLOT, (k % half) // SLOT
    b_q, b_k = q % SLOT, k % SLOT
    ok = (win_q == win_k) & (k < PAIR) & (b_k < WIN)
    cut = WIN - SHIFT
    if row_cut:
        ok &= (a_q < cut) == (a_k < cut)
    if col_cut:
        ok &= ((b_q < cut) == (b_k < cut)) | (win_q == 0)
    return jnp.where(ok, 0.0, MASKED)


def head_lanes(x, h):
    lane = iota((1, CH), 1)
    return jnp.where(lane // HD == h, x, jnp.zeros_like(x))


def spread(x):
    padded = jnp.concatenate([x, jnp.zeros((128 - PAIR, CH), x.dtype)], 0)
    return jnp.concatenate([head_lanes(padded, h) for h in range(HEADS_C)], 0)


def stacked(x):
    return jnp.concatenate([head_lanes(x, h) for h in range(HEADS_C)], 0)


def by_head(x):
    return jnp.concatenate([x[:, 128 * h : 128 * h + 128] for h in range(HEADS_C)], 0)


def rows_of(p, count=PAIR):
    return pl.ds(pl.multiple_of(p * count, 16), count)


SM_QV, SM_TABLE, SM_OUT_B, SM_UP_B, SM_DOWN_B = 0, 2, 10, 11, 15
RP_GAIN0, RP_SHIFT0, RP_GAIN, RP_SHIFT = 0, 1, 2, 4


def row_of(ref, c, first, count):
    return jnp.concatenate([ref[c, first + i : first + i + 1, :] for i in range(count)], 1)


MESH = pl.DeviceIdType.MESH
HALF = 256
PEERS = CHUNKS - 1
PLANE = 15


class Sems:
    def __init__(self):
        self.count = 0

    def take(self, n):
        self.count += n
        return self.count - n


IDS = Sems()
ID_PAGES = IDS.take(1)
ID_SMALL = IDS.take(PEERS)
ID_W = IDS.take(4 * PEERS)
ID_WF = IDS.take(4 * PEERS)
ID_WN = IDS.take(4 * PEERS * 4)
ID_COT_HALO = IDS.take(1)
ID_COT = IDS.take(PEERS)
ID_BLK = IDS.take(PEERS)
ID_BLK_HALO = IDS.take(1)
ID_CORE = IDS.take(4 * CHUNKS)
ID_CORE_M = IDS.take(1)
ID_Y = IDS.take(2 * PEERS)
ID_Y_M = IDS.take(PEERS)
ID_FIRST = IDS.take(3 * CHUNKS * PLANE)
ID_THIRD = IDS.take(3 * PEERS)
ID_BACK_Y = IDS.take(2 * PEERS)
ID_BACK = IDS.take(3 * PLANE)
ID_A = IDS.take(2 * 2 * PLANE)
ID_GC = IDS.take(6)
ID_PG = IDS.take(1)
ID_MN = IDS.take(1)
ID_SG = IDS.take(2 * (1 + 3 * PEERS))
LOCAL = 56
UNROLL = 3
QKV, OUT, UP, DOWN = 0, 1, 2, 3

EARLY = 10
SE_NORM, SE_SQ, SE_ROWS = CHUNKS * (16 - EARLY), CHUNKS * (16 - EARLY) + 8, 40
SL_NORM, SL_MERGE, SL_ROWS = CHUNKS * EARLY, CHUNKS * EARLY + 8, 64


def chunk_off(j):
    return lax.rem(3 * j, 5) - 2 * (j // 3)


def feed_off(j):
    return lax.rem(2 * j, 5) - (j // 2 - j // 3)


def back_off(j):
    return lax.rem(j + 1, CHUNKS)


def compute(
    pages_in, cot_in, merge_in, qkv_in, out_in, up_in, down_in,
    qv_in, table_in, out_b_in, up_b_in, down_b_in, gain_m_in, shift_m_in, gain_in, shift_in,
    pages_sel_in, pages_sel_t_in, table_sel_in, table_sel_t_in,
    block_o, block_halo_o, pages_o, down_o, up_o, qkv_o, out_o, merge_o, early_o, late_o,
    qv_v, table_v, out_b_v, up_b_v, down_b_v, gain_m_v, shift_m_v, gain_v, shift_v,
    pages_sel, pages_sel_t, table_sel, table_sel_t, repl,
    pages, m_htx, m_hrx, g_htx, g_hrx, mn_htx, mn_hrx, cot_v, cot_tx, cot_hf, cot_htx, cot_hrx, merge_w, qkv_w, out_w, up_w, down_w, small,
    x0, inv, mn, mt, n1, qkv, prob, att, norm, r1, u2, n2, g2,
    hid, dpre, bias, ones, unit, lmat, gsum, dqkv, g1, gz, tmp,
    blk_rx, blk_htx, blk_hrx, pg,
    d_merge, d_qkv, d_out, d_up, d_down, d_small,
    l1_qkv, l1_out, l1_up, l1_down, l1_m, l2_out, l2_down, l2_m,
    up_1, up_h, up_3, qkv_1, qkv_h, qkv_3, mb_1, mb_h, mb_3,
    ga, rxa, gf_down, gb, rxb, gfb, gf_up, gf_qkv, gf_out, mf,
    se, se_c, se_y, se_z, se_x, sl, sl_c, sl_y, sl_z, sl_x,
    ssem, rsem, lsem,
):
    chan = lax.axis_index("chan")
    space = lax.axis_index("space")
    n_space = lax.axis_size("space")
    core = lax.rem(space, 2)
    z = lax.rem(space // 2, 4)
    x = space // 8
    last_chan = chan == CHUNKS - 1
    valid = (iota((PAIR, 1), 0) % SLOT < WIN).astype(F32)

    def at_y(d):
        return (space, lax.rem(chan + d, CHUNKS))

    def at_z(d):
        return (x * 8 + lax.rem(z + d, 4) * 2 + core, chan)

    def at_x(d):
        return (lax.rem(x + d, 4) * 8 + z * 2 + core, chan)

    def at_plane(m):
        return (lax.rem(x + m // 4, 4) * 8 + lax.rem(z + m % 4, 4) * 2 + core, chan)

    def place_of(m):
        return lax.rem(x + m // 4, 4) * 4 + lax.rem(z + m % 4, 4)

    def place_before(m):
        return lax.rem(x + 4 - m // 4, 4) * 4 + lax.rem(z + 4 - m % 4, 4)

    sibling = (x * 8 + z * 2 + 1 - core, chan)
    up_band = (lax.rem(space + n_space - 1, n_space), chan)
    down_band = (lax.rem(space + 1, n_space), chan)
    rank = space * CHUNKS + chan
    n_rank = n_space * CHUNKS
    before = lax.rem(rank + n_rank - 1, n_rank)
    after = lax.rem(rank + 1, n_rank)
    up_rank = (before // CHUNKS, lax.rem(before, CHUNKS))
    down_rank = (after // CHUNKS, lax.rem(after, CHUNKS))

    def send(src, dst, n, device, into=None):
        return pltpu.make_async_remote_copy(
            src_ref=src, dst_ref=dst, send_sem=ssem.at[n], recv_sem=rsem.at[n if into is None else into],
            device_id=device, device_id_type=MESH,
        )

    def local(src, dst, n):
        return pltpu.make_async_copy(src, dst, lsem.at[n])

    own_pages = local(pages_in, pages, 0)
    own_merge = local(merge_in, merge_w, 1)
    own_w = [
        local(src, dst.at[chan], 2 + i)
        for i, (src, dst) in enumerate(((qkv_in, qkv_w), (out_in, out_w)))
    ]
    own_mlp = [
        local(src.at[pl.ds(64 * i, 64)], dst.at[chan, i // 2, i % 2], 40 + 8 * n + i)
        for n, (src, dst) in enumerate(((up_in, up_w), (down_in, down_w)))
        for i in range(8)
    ]
    own_cot = local(cot_in, cot_v, 6)
    tiny = (qv_in, table_in, out_b_in, up_b_in, down_b_in, gain_m_in, shift_m_in, gain_in, shift_in)
    tiny_v = (qv_v, table_v, out_b_v, up_b_v, down_b_v, gain_m_v, shift_m_v, gain_v, shift_v)
    tiny_copies = [local(src, dst, 24 + i) for i, (src, dst) in enumerate(zip(tiny, tiny_v))]
    tables_in = (pages_sel_in, pages_sel_t_in, table_sel_in, table_sel_t_in)
    sel_copies = [
        local(src, dst, 33 + i) for i, (src, dst) in enumerate(zip(tables_in, (pages_sel, pages_sel_t, table_sel, table_sel_t)))
    ]
    for copy in tiny_copies + sel_copies[0:1] + [own_pages, own_cot, own_merge, sel_copies[3], own_w[QKV]]:
        copy.start()
    for copy in [own_w[OUT]] + own_mlp + [sel_copies[1], sel_copies[2]]:
        copy.start()

    barrier = pltpu.get_barrier_semaphore()
    greeted = [at_y(d) for d in (1, 2, 3)] + [at_plane(m) for m in range(1, PLANE + 1)]
    greeted += [sibling, up_band, down_band, up_rank, down_rank]
    for by in (1, 3):
        greeted.append((lax.rem(x + by, 4) * 8 + z * 2 + 1 - core, chan))
        greeted.append((x * 8 + lax.rem(z + by, 4) * 2 + 1 - core, chan))
    for device in greeted:
        pl.semaphore_signal(barrier, inc=1, device_id=device, device_id_type=MESH)

    for copy in tiny_copies:
        copy.wait()
    lane_rows = lambda ref, n: ref[...].astype(F32).reshape(1, n)
    small[chan, SM_QV : SM_QV + 2, :] = qv_v[...].astype(F32)
    table = table_v[...].astype(F32)
    small[chan, SM_TABLE : SM_TABLE + 4, :] = table[:, 0:128]
    small[chan, SM_TABLE + 4 : SM_TABLE + 8, :] = jnp.concatenate([table[:, 128:169], jnp.zeros((4, 87), F32)], 1)
    small[chan, SM_OUT_B : SM_OUT_B + 1, :] = lane_rows(out_b_v, 128)
    up_row = lane_rows(up_b_v, 512)
    for i in range(4):
        small[chan, SM_UP_B + i : SM_UP_B + i + 1, :] = up_row[:, i * 128 : i * 128 + 128]
    small[chan, SM_DOWN_B : SM_DOWN_B + 1, :] = lane_rows(down_b_v, 128)
    repl[RP_GAIN0 : RP_GAIN0 + 1, :] = lane_rows(gain_m_v, 1024)
    repl[RP_SHIFT0 : RP_SHIFT0 + 1, :] = lane_rows(shift_m_v, 1024)
    repl[RP_GAIN : RP_GAIN + 2, 0:D] = gain_v[...].astype(F32)
    repl[RP_SHIFT : RP_SHIFT + 2, 0:D] = shift_v[...].astype(F32)
    pl.semaphore_wait(barrier, len(greeted))

    halves = (HALF, CH // 2, HALF, HALF)
    weights = (qkv_w, out_w, up_w, down_w)
    sources = (qkv_in, out_in, up_in, down_in)

    def axis_of(w):
        return (x, lambda d, k: (lax.rem(x + d, 4) * 8 + z * 2 + k, chan)) if w in (QKV, UP) else (
            z, lambda d, k: (x * 8 + lax.rem(z + d, 4) * 2 + k, chan)
        )

    def rows_in(ref, w, first, n, c=None):
        rows = pl.ds(pl.multiple_of(first, 16), n)
        if c is None:
            return ref.at[:, rows] if w == QKV else ref.at[rows]
        return ref.at[c, :, rows] if w == QKV else ref.at[c, rows]

    def quarter(w, k):
        return lax.rem(axis_of(w)[0], 2) * halves[w] + k * (halves[w] // 2)

    def weight_copy(w, d):
        n = halves[w] // 2
        src = rows_in(sources[w], w, quarter(w, core), n)
        return send(src, rows_in(weights[w], w, quarter(w, core), n, chan), ID_W + w * PEERS + d - 1, at_y(d))

    def arrived(w, d, c):
        part = rows_in(weights[w], w, quarter(w, core), halves[w] // 2, c)
        send(part, part, ID_W + w * PEERS + d - 1, at_y(d)).wait_recv()

    def forward_copies(w, d, c):
        part = rows_in(weights[w], w, quarter(w, core), halves[w] // 2, c)
        yield send(part, part, ID_WF + w * PEERS + d - 1, sibling)
        n = halves[w] // 4
        base = ID_WN + (w * PEERS + d - 1) * 4
        for i, by in enumerate((1, 3)):
            part = rows_in(weights[w], w, quarter(w, core) + i * n, n, c)
            for same in range(2):
                device = axis_of(w)[1](by, core if same else 1 - core)
                yield send(part, part, base + i * 2 + same, device, base + i * 2 + core)

    def forwarded(w, d, c):
        part = rows_in(weights[w], w, quarter(w, 1 - core), halves[w] // 2, c)
        send(part, part, ID_WF + w * PEERS + d - 1, sibling).wait_recv()
        n = halves[w] // 4
        base = ID_WN + (w * PEERS + d - 1) * 4
        half = (1 - lax.rem(axis_of(w)[0], 2)) * halves[w]
        for i in range(2):
            for k in range(2):
                part = rows_in(weights[w], w, half + (k * 2 + i) * n, n, c)
                send(part, part, base + i * 2 + k, sibling).wait_recv()

    fourth = lax.rem(x + 2 * z, 4)

    def eighth_copy(w, d):
        part = weights[w].at[chan, fourth, core]
        src = sources[w].at[pl.ds(pl.multiple_of(fourth * 128 + core * 64, 64), 64)]
        return send(src, part, ID_W + w * PEERS + d - 1, at_y(d))

    def around_copies(w, d, c):
        part = weights[w].at[c, fourth, core]
        base = ID_WN + (w * PEERS + d - 1) * 4
        yield send(part, part, base, at_x(1))
        yield send(part, part, base + 1, at_x(3))
        for i, by in enumerate((1, 3)):
            half = part.at[pl.ds(32 * i, 32)]
            yield send(half, half, base + 2 + i, at_z(by))

    def across_copy(w, d, c):
        part = weights[w].at[c, :, core]
        return send(part, part, ID_WF + w * PEERS + d - 1, sibling)

    def chunk_peer(j):
        off = feed_off(j)
        return CHUNKS - off, lax.rem(chan + off, CHUNKS)

    def pass_around(w, j):
        d, c = chunk_peer(j)
        part = weights[w].at[c, fourth, core]
        send(part, part, ID_W + w * PEERS + d - 1, at_y(d)).wait_recv()
        for copy in around_copies(w, d, c):
            copy.start()

    def pass_across(w, j):
        d, c = chunk_peer(j)
        base = ID_WN + (w * PEERS + d - 1) * 4
        for i, by in enumerate((3, 1)):
            part = weights[w].at[c, lax.rem(fourth + by, 4), core]
            send(part, part, base + i, sibling).wait_recv()
        for i in range(2):
            part = weights[w].at[c, lax.rem(fourth + 2, 4), core, pl.ds(32 * i, 32)]
            send(part, part, base + 2 + i, sibling).wait_recv()
        across_copy(w, d, c).start()

    def have_across(w, j):
        d, c = chunk_peer(j)
        part = weights[w].at[c, :, 1 - core]
        send(part, part, ID_WF + w * PEERS + d - 1, sibling).wait_recv()

    def pass_on(w, j):
        off = chunk_off(j)
        c, d = lax.rem(chan + off, CHUNKS), CHUNKS - off
        arrived(w, d, c)
        for copy in forward_copies(w, d, c):
            copy.start()

    def have(w, j):
        off = chunk_off(j)
        forwarded(w, CHUNKS - off, lax.rem(chan + off, CHUNKS))

    small_copies = [send(small.at[chan], small.at[chan], ID_SMALL + d - 1, at_y(d)) for d in (1, 3, 2)]
    weight_copies = [[(weight_copy if w in (QKV, OUT) else eighth_copy)(w, d) for d in (1, 3, 2)] for w in range(4)]
    for copy in small_copies + weight_copies[QKV][0:1]:
        copy.start()

    def quads(i, _):
        base = (i // WIN) * BAND + lax.rem(i, WIN) * SLOT
        for q in range(2):
            y = dot(pages_sel[...], pages[lax.rem(2 * i + q + LIFT, 2 * ROWS)])
            for par in range(2):
                for wc in range(WC):
                    lanes = par * 512 + q * 256
                    at = pl.multiple_of(base + wc * WIN * SLOT, SLOT)
                    first = par * WC * SLOT + wc * SLOT
                    tmp[pl.ds(at, SLOT), lanes : lanes + 256] = y[first : first + SLOT]
        return 0

    own_pages.wait()
    sel_copies[0].wait()
    gain = [repl[RP_GAIN + i : RP_GAIN + i + 1, 0:D] for i in range(2)]
    shift = [repl[RP_SHIFT + i : RP_SHIFT + i + 1, 0:D] for i in range(2)]
    three = range(NPAIR // 2)
    cut_rows = WIN - SHIFT
    n_halo = SHIFT * SLOT

    def pair_rows(half, i):
        return slice(half * BAND + i * PAIR, half * BAND + i * PAIR + PAIR)

    def band(half):
        return slice(half * BAND, half * BAND + BAND)

    def merge_rows(half):
        lax.fori_loop(half * WIN, half * WIN + WIN, quads, 0)
        for i in three:
            r = pair_rows(half, i)
            u, inverse = unit_of(tmp[r, :])
            x0[r, :] = u.astype(BF16)
            inv[r, 0:1] = inverse
            mn[r, :] = (u * repl[RP_GAIN0 : RP_GAIN0 + 1, :] + repl[RP_SHIFT0 : RP_SHIFT0 + 1, :]).astype(BF16)
        return dot(mn[band(half), :], merge_w[...])

    def norm1(half):
        for i in three:
            r = pair_rows(half, i)
            u, _inverse = unit_of(mt[r, :].astype(F32))
            n1[r, :] = (u * gain[0] + shift[0]).astype(BF16)

    def halo_of(rows):
        starts = [wc * WIN * SLOT + cut_rows * SLOT for wc in range(WC)]
        return jnp.concatenate([rows[at : at + n_halo] for at in starts], 0)

    def with_halo(rows, halo):
        parts = []
        for wc in range(WC):
            at = wc * WIN * SLOT
            parts += [rows[at : at + cut_rows * SLOT], halo[wc * n_halo : wc * n_halo + n_halo]]
        return jnp.concatenate(parts, 0)

    own_merge.wait()
    merged_last = merge_rows(1)
    mt[band(1), :] = merged_last.astype(BF16)
    m_htx[...] = halo_of(merged_last).astype(BF16)
    merged_halo = send(m_htx, m_hrx, ID_PAGES, up_rank)
    merged_halo.start()
    for copy in weight_copies[QKV][1:] + weight_copies[OUT]:
        copy.start()
    for i in (2, 0, 1):
        for w in (UP, DOWN):
            weight_copies[w][i].start()
    mt[band(0), :] = merge_rows(0).astype(BF16)
    norm1(0)

    own_cot.wait()
    norm[...] = jnp.zeros_like(norm)
    cot_hf[...] = jnp.zeros_like(cot_hf)
    for wc in range(WC):
        for b in range(WIN):
            column = cot_v[(wc * WIN + b + SHIFT) % COLS].astype(F32)
            cot_hf[pl.ds(wc * SHIFT * SLOT + b, SHIFT, stride=SLOT), :] = column[0:SHIFT]
            for m in range(4 * ROWS // WIN):
                c, wr = m // 2, m % 2
                n = cut_rows if m == 4 * ROWS // WIN - 1 else WIN
                slot = wr * BAND + wc * WIN * SLOT + b
                norm[c, pl.ds(slot, n, stride=SLOT), :] = column[SHIFT + WIN * m : SHIFT + WIN * m + n]
    cot_htx[...] = cot_hf[...].astype(BF16)
    cot_halo = send(cot_htx, cot_hrx, ID_COT_HALO, up_band)
    cot_halo.start()

    sel_copies[3].wait()
    for d in (1, 2, 3):
        part = small.at[lax.rem(chan + CHUNKS - d, CHUNKS)]
        send(part, part, ID_SMALL + d - 1, at_y(d)).wait_recv()
    lmat[...] = jnp.zeros_like(lmat)
    masks = [pair_mask(kind // 2, kind % 2) for kind in range(4)]
    for h in range(HEADS_C):
        lanes = jnp.where(iota((128, CH), 1) // HD == h, 1.0, 0.0)
        ones[h * 128 : h * 128 + 128, :] = lanes.astype(BF16)
    unit[...] = jnp.where(iota((PAIR, 128), 0) == iota((PAIR, 128), 1), 1.0, 0.0).astype(BF16)

    def tables(c, _):
        table = jnp.concatenate([small[c, SM_TABLE : SM_TABLE + 4, :], small[c, SM_TABLE + 4 : SM_TABLE + 8, :]], 1)
        table = jnp.concatenate([table, jnp.zeros_like(table)], 0).astype(BF16)
        placed = dot(table, table_sel_t[...])
        for b_k in range(WIN):
            for h in range(HEADS_C):
                lmat[h * SLOT + b_k : h * SLOT + b_k + 1, :] = placed[h : h + 1, b_k * 128 : b_k * 128 + 128]
        for h in range(HEADS_C):
            tab = lmat[h * SLOT : h * SLOT + SLOT, :]
            lane = iota((SLOT, 128), 1)
            slabs = []
            for a in range(WIN):
                moved = pltpu.roll(tab, (128 - (WIN - 1 - a) * SLOT) % 128, 1) if a < WIN - 1 else tab
                low = jnp.where(lane < WIN * SLOT, moved, 0.0)
                slabs.append(low + pltpu.roll(low, WIN * SLOT, 1))
            one = jnp.concatenate(slabs * 2 + [jnp.zeros((128 - PAIR, 128), F32)], 0)
            for kind in range(4):
                bias[kind, c, h * 128 : h * 128 + 128, :] = (one + masks[kind]).astype(BF16)
        return 0

    lax.fori_loop(0, CHUNKS, tables, 0)

    pass_on(QKV, 1)
    merged_halo.wait_recv()
    mt[band(1), :] = with_halo(mt[band(1), :].astype(F32), m_hrx[...].astype(F32)).astype(BF16)
    norm1(1)
    pass_on(QKV, 2)

    cot_halo.wait_recv()
    norm[PEERS, BAND:T, :] = with_halo(norm[PEERS, BAND:T, :], cot_hrx[...].astype(F32))
    cot_tx[...] = norm[...].astype(BF16)
    lanes_here = pl.ds(pl.multiple_of(chan * CH, CH), CH)
    cot_copies = [
        send(cot_tx.at[lax.rem(chan + d, CHUNKS)], g2.at[:, lanes_here], ID_COT + d - 1, at_y(d)) for d in (1, 3, 2)
    ]
    for copy in cot_copies:
        copy.start()
    g2[:, lanes_here] = cot_tx[chan]

    mn_htx[...] = halo_of(mn[band(1), :].astype(F32)).astype(BF16)
    normed_halo = send(mn_htx, mn_hrx, ID_MN, up_rank)
    normed_halo.start()

    def wide(c):
        return jnp.concatenate([qkv_w[c, i] for i in range(3)], 1)

    own_w[QKV].wait()

    def attend(j, _):
        c = lax.rem(chan + chunk_off(j), CHUNKS)
        heads = pl.ds(pl.multiple_of(c * CH, CH), CH)

        @pl.when(j > 0)
        def _():
            have(QKV, j)

        projected = dot(n1[...], wide(c))
        zeros = jnp.zeros((1, CH), F32)
        offset = jnp.concatenate([small[c, SM_QV : SM_QV + 1, :], zeros, small[c, SM_QV + 1 : SM_QV + 2, :]], 1)
        scaled = jnp.concatenate([jnp.full((1, CH), SCALE, F32), jnp.ones((1, 2 * CH), F32)], 1)
        qkv[c] = ((projected + offset) * scaled).astype(BF16)

        @pl.when(j == 0)
        def _():
            pass_on(QKV, 3)

        def window_pairs(t, _):
            pairs = [UNROLL * t + i for i in range(UNROLL)]
            parts = [[qkv[c, rows_of(p), i * CH : i * CH + CH] for i in range(3)] for p in pairs]
            results = []
            for i, (q, k, v) in enumerate(parts):
                table = bias[2 * (chan // PEERS) * t + i // (UNROLL - 1), c]
                s = dot_nt(jnp.concatenate([q, unit[...]], 1), jnp.concatenate([spread(k), table], 1))
                weights = []
                for h in range(HEADS_C):
                    sh = s[:, 128 * h : 128 * h + 128]
                    weights.append(jnp.exp(sh - jnp.max(sh, -1, keepdims=True)).astype(BF16))
                w = jnp.concatenate(weights, 1)
                o = dot(w, jnp.concatenate([spread(v), ones[...]], 1))
                inverse = 1.0 / o[:, CH:]
                results.append((w, o[:, 0:CH] * inverse, inverse))
            for p, (w, o, inverse) in zip(pairs, results):
                prob[c, p] = w
                att[rows_of(p), heads] = o.astype(BF16)
                norm[c, rows_of(p), :] = inverse
            return 0

        lax.fori_loop(0, NPAIR // UNROLL, window_pairs, 0)

        @pl.when(j == 1)
        def _():
            for i in range(1, CHUNKS):
                pass_on(OUT, i)
            for w in (UP, DOWN):
                pass_around(w, 1)

        @pl.when(j == 2)
        def _():
            for w in (UP, DOWN):
                pass_around(w, 2)

        @pl.when(j == 3)
        def _():
            for w in (UP, DOWN):
                pass_around(w, 3)
                pass_across(w, 1)

        return 0

    lax.fori_loop(0, CHUNKS, attend, 0)

    own_w[OUT].wait()
    for j in range(1, CHUNKS):
        have(OUT, j)
    tmp[:, 0:D] = dot(att[...], out_w[...].reshape(D, D))
    out_b = jnp.concatenate([small[c, SM_OUT_B : SM_OUT_B + 1, :] for c in range(CHUNKS)], 1)
    down_b = jnp.concatenate([small[c, SM_DOWN_B : SM_DOWN_B + 1, :] for c in range(CHUNKS)], 1)

    def norm2(half):
        total = 0.0
        for i in three:
            r = pair_rows(half, i)
            branch = tmp[r, 0:D] + out_b
            resid = mt[r, :].astype(F32) + branch
            r1[r, :] = resid
            u, inverse = unit_of(resid.astype(BF16).astype(F32))
            u2[r, :] = u.astype(BF16)
            inv[r, 1:2] = inverse
            n2[r, :] = (u * gain[1] + shift[1]).astype(BF16)
            total = total + col_sum(branch * branch * valid)
        return total

    sq_one = norm2(0) + norm2(1)
    for w in (UP, DOWN):
        pass_across(w, 2)

    for d in (1, 2, 3):
        part = g2.at[:, pl.ds(pl.multiple_of(lax.rem(chan + CHUNKS - d, CHUNKS) * CH, CH), CH)]
        send(part, part, ID_COT + d - 1, at_y(d)).wait_recv()

    grads = (d_qkv, d_out, d_up, d_down)
    firsts = (l1_qkv, l1_out, l1_up, l1_down)
    order = (1, 3, 2)
    around = range(1, PLANE + 1)
    here = x * 4 + z

    def step(n, lead=0):
        return pl.ds(pl.multiple_of(lead, 16), n)

    def half_grad(w, c, k):
        return grads[w].at[c, step(halves[w], k * halves[w])]

    def core_copy(w, j, c):
        return send(half_grad(w, c, 1 - core), firsts[w].at[j], ID_CORE + w * CHUNKS + j, sibling)

    def core_sum(w, j, off):
        c = lax.rem(chan + off, CHUNKS)
        core_copy(w, j, c).wait_recv()
        size = min(halves[w], 64)
        for t in range(0, halves[w], size):
            r = step(size, core * halves[w] + t)
            total = grads[w][c, r, :].astype(F32) + firsts[w][j, t : t + size, :].astype(F32)
            grads[w][c, r, :] = total.astype(BF16)

    owners = {DOWN: (0, l2_down), OUT: (1, l2_out)}

    def owner_copy(w, off):
        n, into = owners[w]
        c = lax.rem(chan + off, CHUNKS)
        return send(half_grad(w, c, core), into.at[off - 1], ID_Y + n * PEERS + off - 1, at_y(off))

    def to_owner(w, off):
        @pl.when(off > 0)
        def _():
            owner_copy(w, off).start()

    def owner_wait(w):
        n, into = owners[w]
        for d in order:
            send(into.at[d - 1], into.at[d - 1], ID_Y + n * PEERS + d - 1, at_y(d)).wait_recv()

    def owner_sum(w, t, size):
        total = grads[w][chan, step(size, core * halves[w] + t), :].astype(F32)
        for d in range(PEERS):
            total += owners[w][1][d, t : t + size, :].astype(F32)
        return total.astype(BF16)

    class Plane:
        def __init__(self, n, g, rx, gf):
            self.n, self.g, self.rx, self.gf = n, g, rx, gf

        def out_copies(self):
            for m in around:
                src = self.g.at[step(16, place_of(m) * 16)]
                yield send(src, self.rx.at[m - 1], ID_A + self.n * 2 * PLANE + m - 1, at_plane(m))

        def back_copies(self, wait):
            for m in around:
                part = self.gf.at[core, step(16, (place_before(m) if wait else here) * 16)]
                yield send(part, part, ID_A + (self.n * 2 + 1) * PLANE + m - 1, at_plane(m))

        def start(self):
            for copy in self.out_copies():
                copy.start()

        def back_start(self):
            for copy in self.out_copies():
                copy.wait_recv()
            total = self.g[step(16, here * 16), :].astype(F32)
            for m in around:
                total += self.rx[m - 1].astype(F32)
            self.gf[core, step(16, here * 16), :] = total.astype(BF16)
            for copy in self.back_copies(False):
                copy.start()

        def finish(self):
            for copy in self.back_copies(True):
                copy.wait_recv()

        def left(self):
            for copy in [*self.out_copies(), *self.back_copies(False)]:
                copy.wait_send()

    plane_a = Plane(0, ga, rxa, gf_down)
    plane_b = Plane(1, gb, rxb, gfb)

    class Spread:
        def __init__(self, n, src, first, h, third, into):
            self.n, self.src, self.first, self.h, self.third, self.into = n, src, first, h, third, into

        def first_copies(self, j, c):
            for m in around:
                src = self.src(c, place_of(m) * 16, 16)
                n = ID_FIRST + (self.n * CHUNKS + j) * PLANE + m - 1
                yield send(src, self.first.at[c, m - 1], n, at_plane(m))

        def first_start(self, j, c):
            for copy in self.first_copies(j, c):
                copy.start()

        def third_copies(self):
            for d in order:
                src = self.h.at[lax.rem(chan + d, CHUNKS)]
                yield send(src, self.third.at[d - 1], ID_THIRD + self.n * PEERS + d - 1, at_y(d))

        def third_start(self, chunk_of):
            for j in range(CHUNKS):
                c = chunk_of(j)
                for copy in self.first_copies(j, c):
                    copy.wait_recv()
                total = self.src(c, here * 16, 16)[...].astype(F32)
                for m in around:
                    total += self.first[c, m - 1].astype(F32)
                self.h[c] = total.astype(BF16)
            for copy in self.third_copies():
                copy.start()

        def third_sum(self):
            for copy in self.third_copies():
                copy.wait_recv()
            total = self.h[chan].astype(F32)
            for d in range(PEERS):
                total += self.third[d].astype(F32)
            self.into(chan, here * 16, 16)[...] = total.astype(BF16)

        def back_y(self, wait):
            for d in order:
                part = self.into(lax.rem(chan + (CHUNKS - d if wait else 0), CHUNKS), here * 16, 16)
                yield send(part, part, ID_BACK_Y + d - 1, at_y(d))

        def back_copies(self, wait):
            for m in around:
                part = self.into(None, (place_before(m) if wait else here) * 16, 16)
                yield send(part, part, ID_BACK + self.n * PLANE + m - 1, at_plane(m))

        def back_start(self):
            for copy in self.back_copies(False):
                copy.start()

        def finish(self):
            for copy in self.back_copies(True):
                copy.wait_recv()

        def left(self, chunk_of):
            for j in range(CHUNKS):
                for copy in self.first_copies(j, chunk_of(j)):
                    copy.wait_send()
            for copy in [*self.third_copies(), *self.back_copies(False)]:
                copy.wait_send()

    def half_rows(w):
        return lambda c, row, n: grads[w].at[c, step(n, core * halves[w] + row)]

    group_a, group_b = 2 * core, 2 * core + 1
    spread_up = Spread(0, half_rows(UP), up_1, up_h, up_3, lambda c, row, n: gf_up.at[core, step(n, row)])
    spread_qkv = Spread(1, half_rows(QKV), qkv_1, qkv_h, qkv_3, lambda c, row, n: gf_qkv.at[core, step(n, row)])
    spread_m = Spread(
        2, lambda c, row, n: d_merge.at[group_b, c, step(n, row)], mb_1, mb_h, mb_3,
        lambda c, row, n: mf.at[group_b, slice(None) if c is None else c, step(n, row)],
    )

    def core_out(n, part):
        return send(part, part, ID_GC + n, sibling)

    def feed_chunk(j):
        return lax.rem(chan + feed_off(j), CHUNKS)

    def back_chunk(j):
        return lax.rem(chan + back_off(j), CHUNKS)

    def feed_sums(j):
        core_sum(DOWN, j, feed_off(j))
        to_owner(DOWN, feed_off(j))
        core_sum(UP, j, feed_off(j))
        spread_up.first_start(j, feed_chunk(j))

    def back_sums(j):
        core_sum(OUT, j, back_off(j))
        to_owner(OUT, back_off(j))
        core_sum(QKV, j, back_off(j))
        spread_qkv.first_start(j, back_chunk(j))

    class Small:
        def __init__(self, n, own, into):
            self.n, self.own, self.into = n, own, into

        def copies(self, level):
            base = ID_SG + self.n * (1 + 3 * PEERS)
            if level == 0:
                return [send(self.own.at[0], self.into[0].at[0], base, sibling)]
            at = (at_y, at_z, at_x)[level - 1]
            base += (level - 1) * PEERS
            return [send(self.own.at[level], self.into[level].at[d - 1], base + d, at(d)) for d in order]

        def start(self, level):
            for copy in self.copies(level):
                copy.start()

        def sum(self, level):
            for copy in self.copies(level):
                copy.wait_recv()
            total = self.own[level]
            for d in range(self.into[level].shape[0]):
                total += self.into[level][d]
            self.own[level + 1] = total

    small_early = Small(0, se, (se_c, se_y, se_z, se_x))
    small_late = Small(1, sl, (sl_c, sl_y, sl_z, sl_x))

    def lay(ref, at, row):
        for i in range(row.shape[1] // 128):
            ref[0, at + i : at + i + 1, :] = row[:, i * 128 : i * 128 + 128]

    tmp[...] = jnp.zeros_like(tmp)
    for copy in own_mlp:
        copy.wait()

    def feed(j, _):
        c = feed_chunk(j)

        @pl.when(j > 0)
        def _():
            have_across(UP, j)
            have_across(DOWN, j)

        @pl.when(j == 0)
        def _():
            for w in (UP, DOWN):
                pass_across(w, 3)

        up_c, down_c = up_w[c].reshape(D, 512), down_w[c].reshape(512, D)
        up_b = row_of(small, c, SM_UP_B, 4)
        d_up_b = 0.0
        for first in range(0, T, T // 3):
            r = slice(first, first + T // 3)
            value, slope = gelu_parts(dot(n2[r, :], up_c) + up_b)
            hid[r, :] = value.astype(BF16)
            d = slope * dot_nt(g2[r, :], down_c)
            dpre[r, :] = d.astype(BF16)
            d_up_b = d_up_b + col_sum(d)
        for i in range(4):
            d_small[c, SM_UP_B + i : SM_UP_B + i + 1, :] = d_up_b[:, i * 128 : i * 128 + 128]
        d_down[c] = dot_tn(hid[...], g2[...]).astype(BF16)
        core_copy(DOWN, j, c).start()
        d_up[c] = dot_tn(n2[...], dpre[...]).astype(BF16)
        core_copy(UP, j, c).start()
        tmp[:, 0:D] += dot(hid[...], down_c)
        tmp[:, D : 2 * D] += dot_nt(dpre[...], up_c)

        feed_sums(j)
        return 0

    lax.fori_loop(0, CHUNKS, feed, 0)

    for copy in [cot_halo] + cot_copies:
        copy.wait_send()
    blk_tx = cot_tx
    def norm2_back(half):
        totals = [0.0] * 6
        for i in three:
            r = pair_rows(half, i)
            branch = tmp[r, 0:D] + down_b
            result = r1[r, :] + branch
            for c in range(CHUNKS):
                blk_tx[c, r, :] = result[:, c * CH : c * CH + CH].astype(BF16)
            u = u2[r, :].astype(F32)
            dy = tmp[r, D : 2 * D]
            g = g2[r, :].astype(F32)
            grad = g + norm_back(dy, u, inv[r, 1:2], gain[1])
            tmp[r, 0:D] = grad
            g1[r, :] = grad.astype(BF16)
            terms = (branch * branch * valid, result * result * valid, g, dy * u, dy, grad)
            totals = [total + col_sum(term) for total, term in zip(totals, terms)]
        return totals

    sq_two, sq_out, d_down_b, d_gain1, d_shift1, d_out_b = (a + b for a, b in zip(norm2_back(0), norm2_back(1)))
    for c in range(CHUNKS):
        d_small[c, SM_DOWN_B : SM_DOWN_B + 1, :] = d_down_b[:, c * CH : c * CH + CH]
        d_small[c, SM_OUT_B : SM_OUT_B + 1, :] = d_out_b[:, c * CH : c * CH + CH]

    for c in range(CHUNKS):
        se[0, c * 6 : c * 6 + 6, :] = d_small[c, EARLY:16, :]
    lay(se, SE_NORM, d_gain1)
    lay(se, SE_NORM + 4, d_shift1)
    squares = [sum(sq[:, i * 128 : i * 128 + 128] for i in range(4)) for sq in (sq_out, sq_one, sq_two)]
    se[0, SE_SQ:SE_ROWS, :] = jnp.concatenate(squares + [jnp.zeros((5, 128), F32)], 0)
    small_early.start(0)

    blk_copies = [
        send(blk_tx.at[lax.rem(chan + d, CHUNKS)], blk_rx.at[chan], ID_BLK + d - 1, at_y(d)) for d in (1, 3, 2)
    ]
    blk_rx[chan] = blk_tx[chan]

    normed_halo.wait_recv()
    mn[band(1), :] = with_halo(mn[band(1), :].astype(F32), mn_hrx[...].astype(F32)).astype(BF16)

    sel_copies[2].wait()
    d_out[...] = dot_tn(att[...], g1[...]).astype(BF16).reshape(CHUNKS, CH, D)
    hid[...] = dot_nt(g1[...], out_w[...].reshape(D, D)).astype(BF16)

    def attend_back(j, _):
        c = lax.rem(chan + back_off(j), CHUNKS)
        heads = pl.ds(pl.multiple_of(c * CH, CH), CH)
        core_copy(OUT, j, c).start()
        gsum[...] = jnp.zeros_like(gsum)

        def window_pairs(t, _):
            pairs = [UNROLL * t + i for i in range(UNROLL)]
            parts = [[qkv[c, rows_of(p), i * CH : i * CH + CH] for i in range(3)] for p in pairs]
            d_atts = [hid[rows_of(p), heads].astype(F32) * norm[c, rows_of(p), :] for p in pairs]
            outs = [att[rows_of(p), heads] for p in pairs]
            probs = [prob[c, p] for p in pairs]
            results, total = [], 0.0
            for (q, k, v), d_att, o, w in zip(parts, d_atts, outs, probs):
                left = jnp.concatenate([d_att, -d_att * o.astype(F32)], 1).astype(BF16)
                d_s = w.astype(F32) * dot_nt(left, jnp.concatenate([spread(v), ones[...]], 1))
                total = total + d_s
                d_s = d_s.astype(BF16)
                d_q = dot(d_s, spread(k)) * SCALE
                d_k = dot_tn(by_head(d_s), stacked(q))[0:PAIR]
                d_v = dot_tn(by_head(w), stacked(left[:, 0:CH]))[0:PAIR]
                results.append(jnp.concatenate([d_q, d_k, d_v], 1).astype(BF16))
            for p, result in zip(pairs, results):
                dqkv[c, rows_of(p), :] = result
            gsum[...] += total
            return 0

        lax.fori_loop(0, NPAIR // UNROLL, window_pairs, 0)
        d_qkv[c] = dot_tn(n1[...], dqkv[c]).astype(BF16)
        core_copy(QKV, j, c).start()

        def sums(p, total):
            return total + col_sum(dqkv[c, rows_of(p), :].astype(F32))

        total = lax.fori_loop(0, NPAIR, sums, jnp.zeros((1, 3 * CH), F32))
        d_small[c, SM_QV : SM_QV + 1, :] = total[:, 0:CH]
        d_small[c, SM_QV + 1 : SM_QV + 2, :] = total[:, 2 * CH : 3 * CH]

        half = WIN * SLOT
        for h in range(HEADS_C):
            lanes = slice(h * 128, h * 128 + 128)
            folded = gsum[0:half, lanes] + pltpu.roll(gsum[half:PAIR, lanes], 128 - half, 1)
            acc = jnp.zeros((SLOT, 128), F32)
            for a in range(WIN):
                slab = folded[a * SLOT : a * SLOT + SLOT]
                moved = (WIN - 1 - a) * SLOT
                acc += pltpu.roll(slab, moved, 1) if moved else slab
            lmat[h * SLOT : h * SLOT + SLOT, :] = acc
        d_table = jnp.zeros((SLOT, 256), F32)
        for b_q in range(WIN):
            rows = [lmat[h * SLOT + b_q : h * SLOT + b_q + 1, :] for h in range(HEADS_C)]
            rows = jnp.concatenate(rows + [jnp.zeros((SLOT - HEADS_C, 128), F32)], 0)
            d_table += dot_nt(rows.astype(BF16), table_sel[:, b_q * 128 : b_q * 128 + 128])
        d_small[c, SM_TABLE : SM_TABLE + 4, :] = d_table[0:4, 0:128]
        d_small[c, SM_TABLE + 4 : SM_TABLE + 8, :] = d_table[0:4, 128:256]

        @pl.when(j > 0)
        def _():
            back_sums(j - 1)

        @pl.when(j == 0)
        def _():
            small_early.sum(0)
            small_early.start(1)

        @pl.when(j == 1)
        def _():
            owner_wait(DOWN)
            for t in range(0, HALF, 64):
                ga[t : t + 64, :] = owner_sum(DOWN, t, 64)
            plane_a.start()
            spread_up.third_start(feed_chunk)
            for copy in blk_copies:
                copy.start()

        @pl.when(j == 2)
        def _():
            small_early.sum(1)
            small_early.start(2)

        @pl.when(j == 3)
        def _():
            plane_a.back_start()
            spread_up.third_sum()
            spread_up.back_start()

        return 0

    lax.fori_loop(0, CHUNKS, attend_back, 0)

    def norm1_back(half):
        rows = band(half)
        tmp[rows, D : 2 * D] = sum(dot_nt(dqkv[c, rows, :], wide(c)) for c in range(CHUNKS))
        d_gain, d_shift = 0.0, 0.0
        for i in three:
            r = pair_rows(half, i)
            u, inverse = unit_of(mt[r, :].astype(F32))
            dy = tmp[r, D : 2 * D]
            gz[r, :] = (tmp[r, 0:D] + norm_back(dy, u, inverse, gain[0])).astype(BF16)
            d_gain, d_shift = d_gain + col_sum(dy * u), d_shift + col_sum(dy)
        return d_gain, d_shift

    d_gain0, d_shift0 = norm1_back(1)
    g_htx[...] = halo_of(gz[band(1), :].astype(F32)).astype(BF16)
    grad_halo = send(g_htx, g_hrx, ID_PG, down_rank)
    grad_halo.start()
    more_gain, more_shift = norm1_back(0)
    d_gain0, d_shift0 = d_gain0 + more_gain, d_shift0 + more_shift
    back_sums(PEERS)

    merge_core = send(d_merge.at[pl.ds(2 - 2 * core, 2)], l1_m, ID_CORE_M, sibling)

    def merge_grad(k):
        lanes = pl.ds(pl.multiple_of(k * HALF, HALF), HALF)
        total = dot_tn(mn[...], gz[:, lanes]).astype(BF16)
        for i in range(2):
            d_merge[2 * k + i] = total[:, i * 128 : i * 128 + 128].reshape(CHUNKS, HALF, 128)

    merge_grad(1 - core)
    merge_core.start()
    merge_grad(core)
    small_early.sum(2)
    small_early.start(3)

    for d in (1, 2, 3):
        part = blk_rx.at[lax.rem(chan + CHUNKS - d, CHUNKS)]
        send(part, part, ID_BLK + d - 1, at_y(d)).wait_recv()
    blk_htx[...] = halo_of(blk_rx[PEERS, BAND:T, :].astype(F32)).astype(BF16)
    blk_halo = send(blk_htx, blk_hrx, ID_BLK_HALO, down_band)
    blk_halo.start()

    merge_core.wait_recv()
    for i in range(2):
        for c in range(CHUNKS):
            total = d_merge[2 * core + i, c].astype(F32) + l1_m[i, c].astype(F32)
            d_merge[2 * core + i, c] = total.astype(BF16)

    def merge_owner(d):
        return send(d_merge.at[group_a, lax.rem(chan + d, CHUNKS)], l2_m.at[d - 1], ID_Y_M + d - 1, at_y(d))

    for d in order:
        merge_owner(d).start()
    for c in range(CHUNKS):
        spread_m.first_start(c, c)
    spread_qkv.third_start(back_chunk)

    grad_halo.wait_recv()
    gz[band(1), :] = with_halo(gz[band(1), :].astype(F32), g_hrx[...].astype(F32)).astype(BF16)
    sel_copies[1].wait()
    tmp[...] = dot_nt(gz[...], merge_w[...])
    d_gain_m, d_shift_m = 0.0, 0.0
    for half in range(2):
        for i in three:
            r = pair_rows(half, i)
            u = x0[r, :].astype(F32)
            dy = tmp[r, :]
            tmp[r, :] = norm_back(dy, u, inv[r, 0:1], repl[RP_GAIN0 : RP_GAIN0 + 1, :])
            d_gain_m, d_shift_m = d_gain_m + col_sum(dy * u), d_shift_m + col_sum(dy)

    for c in range(CHUNKS):
        sl[0, EARLY * c : EARLY * c + EARLY, :] = d_small[c, 0:EARLY, :]
    lay(sl, SL_NORM, d_gain0)
    lay(sl, SL_NORM + 4, d_shift0)
    lay(sl, SL_MERGE, d_gain_m)
    lay(sl, SL_MERGE + 8, d_shift_m)
    small_late.start(0)
    plane_a.finish()
    spread_up.finish()
    core_out(0, gf_down.at[core]).start()
    core_out(1, gf_up.at[core]).start()
    small_early.sum(3)

    owner_wait(OUT)
    out_half = owner_sum(OUT, 0, 64)
    for g in range(4):
        gb[g * 64 : g * 64 + 64, 0:128] = out_half[:, g * 128 : g * 128 + 128]
    for d in order:
        merge_owner(d).wait_recv()
    total = d_merge[group_a, chan].astype(F32)
    for d in range(PEERS):
        total += l2_m[d].astype(F32)
    gb[:, 128:256] = total.astype(BF16)
    plane_b.start()
    spread_m.third_start(lambda c: c)
    spread_qkv.third_sum()
    spread_qkv.back_start()
    small_late.sum(0)
    small_late.start(1)

    def page_rows(i, _):
        base = (i // WIN) * BAND + lax.rem(i, WIN) * SLOT
        for q in range(2):
            parts = []
            for par in range(2):
                lanes = par * 512 + q * 256
                for wc in range(WC):
                    at = pl.multiple_of(base + wc * WIN * SLOT, SLOT)
                    parts.append(tmp[pl.ds(at, SLOT), lanes : lanes + 256])
            y = dot(pages_sel_t[...], jnp.concatenate(parts, 0).astype(BF16))
            pg[lax.rem(2 * i + q + LIFT, 2 * ROWS)] = y.astype(BF16)
        return 0

    lax.fori_loop(0, ROWS, page_rows, 0)
    pages_copy = local(pg, pages_o, 14)
    pages_copy.start()

    plane_b.back_start()
    spread_m.third_sum()
    for copy in spread_m.back_y(False):
        copy.start()
    spread_qkv.finish()
    core_out(2, gf_qkv.at[core]).start()
    small_late.sum(1)
    small_late.start(2)

    blk_halo.wait_recv()
    outs = [local(blk_rx, block_o, 10), local(blk_hrx, block_halo_o, 9), local(se.at[4], early_o, 11)]
    core_out(0, gf_down.at[1 - core]).wait_recv()
    outs.append(local(gf_down, down_o, 12))
    core_out(1, gf_up.at[1 - core]).wait_recv()
    outs.append(local(gf_up, up_o, 13))
    for copy in outs:
        copy.start()

    plane_b.finish()
    gf_out[core] = gfb[core, :, 0:128]
    mf[group_a, chan] = gfb[core, :, 128:256]

    def merge_back(c, d):
        part = mf.at[group_a, c]
        return send(part, part, ID_BACK_Y + PEERS + d - 1, at_y(d))

    for d in order:
        merge_back(chan, d).start()
    core_out(3, gf_out.at[core]).start()
    for copy in spread_m.back_y(True):
        copy.wait_recv()
    spread_m.back_start()
    small_late.sum(2)
    small_late.start(3)
    late = [local(sl.at[4], late_o, 15)]
    core_out(2, gf_qkv.at[1 - core]).wait_recv()
    late.append(local(gf_qkv, qkv_o, 16))
    late[1].start()
    for d in order:
        merge_back(lax.rem(chan + CHUNKS - d, CHUNKS), d).wait_recv()
    core_out(4, mf.at[group_a]).start()
    spread_m.finish()
    core_out(5, mf.at[group_b]).start()
    core_out(3, gf_out.at[1 - core]).wait_recv()
    last = [local(gf_out, out_o, 17)]
    last[0].start()
    small_late.sum(3)
    late[0].start()
    for i in range(2):
        core_out(4 + i, mf.at[2 - 2 * core + i]).wait_recv()
    last.append(local(mf, merge_o, 18))
    last[1].start()

    for copy in [merged_halo, normed_halo, blk_halo, grad_halo, merge_core] + small_copies + blk_copies:
        copy.wait_send()
    for w in range(4):
        for copy in weight_copies[w]:
            copy.wait_send()
        for d in order:
            c = lax.rem(chan + CHUNKS - d, CHUNKS)
            if w in (QKV, OUT):
                copies = forward_copies(w, d, c)
            else:
                copies = [*around_copies(w, d, c), across_copy(w, d, c)]
            for copy in copies:
                copy.wait_send()
        for j in range(CHUNKS):
            core_copy(w, j, feed_chunk(j) if w in (UP, DOWN) else back_chunk(j)).wait_send()
    for d in order:
        owner_copy(DOWN, d).wait_send()
        owner_copy(OUT, d).wait_send()
        merge_owner(d).wait_send()
        merge_back(chan, d).wait_send()
    plane_a.left()
    plane_b.left()
    spread_up.left(feed_chunk)
    spread_qkv.left(back_chunk)
    spread_m.left(lambda c: c)
    for copy in spread_m.back_y(False):
        copy.wait_send()
    for group in (small_early, small_late):
        for level in range(4):
            for copy in group.copies(level):
                copy.wait_send()
    parts = (gf_down.at[core], gf_up.at[core], gf_qkv.at[core], gf_out.at[core], mf.at[group_a], mf.at[group_b])
    for n, part in enumerate(parts):
        core_out(n, part).wait_send()
    for copy in outs + late + last + [pages_copy]:
        copy.wait()


def kernel_call(args):
    hbm = pl.BlockSpec(memory_space=pl.ANY)
    s = jax.ShapeDtypeStruct
    outs = [
        s((CHUNKS, T, CH), BF16),
        s((WC * SHIFT * SLOT, CH), BF16),
        s((2 * ROWS, 2 * COLS, 256), BF16),
        s((2, HALF, D), BF16),
        s((2, HALF, 512), BF16),
        s((2, HALF, 3 * CH), BF16),
        s((2, HALF, 128), BF16),
        s((CHUNKS, CHUNKS, HALF, 128), BF16),
        s((SE_ROWS, 128), F32),
        s((SL_ROWS, 128), F32),
    ]

    def v(shape, dtype):
        return pltpu.VMEM(shape, dtype)

    scratch = [
        *[v(a.shape, BF16) for a in args[7:20]], v((8, 1024), F32),
        v((2 * ROWS, 2 * COLS, 256), BF16), *[v((WC * SHIFT * SLOT, D), BF16)] * 4, *[v((WC * SHIFT * SLOT, 2 * D), BF16)] * 2, v((COLS, 4 * ROWS, CH), BF16), v((CHUNKS, T, CH), BF16),
        v((WC * SHIFT * SLOT, CH), F32), v((WC * SHIFT * SLOT, CH), BF16), v((WC * SHIFT * SLOT, CH), BF16),
        v((1024, D), BF16), v((CHUNKS, 3, D, CH), BF16), v((CHUNKS, CH, D), BF16),
        v((CHUNKS, 4, 2, 64, 512), BF16), v((CHUNKS, 4, 2, 64, D), BF16), v((CHUNKS, 16, 128), F32),
        v((T, 1024), BF16), v((T, 2), F32), v((T, 1024), BF16), v((T, D), BF16), v((T, D), BF16),
        v((CHUNKS, T, 3 * CH), BF16), v((CHUNKS, NPAIR, PAIR, 512), BF16), v((T, D), BF16), v((CHUNKS, T, CH), F32),
        v((T, D), F32), v((T, D), BF16), v((T, D), BF16), v((T, D), BF16),
        v((T, 512), BF16), v((T, 512), BF16),
        v((4, CHUNKS, 512, 128), BF16), v((512, CH), BF16), v((PAIR, 128), BF16), v((HEADS_C * SLOT, 128), F32), v((PAIR, 512), F32),
        v((CHUNKS, T, 3 * CH), BF16), v((T, D), BF16), v((T, D), BF16), v((T, 1024), F32),
        v((CHUNKS, T, CH), BF16), v((WC * SHIFT * SLOT, CH), BF16), v((WC * SHIFT * SLOT, CH), BF16),
        v((2 * ROWS, 2 * COLS, 256), BF16),
        v((CHUNKS, CHUNKS, HALF, 128), BF16), v((CHUNKS, D, 3 * CH), BF16), v((CHUNKS, CH, D), BF16),
        v((CHUNKS, D, 512), BF16), v((CHUNKS, 512, D), BF16), v((CHUNKS, 16, 128), F32),
        v((CHUNKS, HALF, 3 * CH), BF16), v((CHUNKS, CH // 2, D), BF16), v((CHUNKS, HALF, 512), BF16),
        v((CHUNKS, HALF, D), BF16), v((2, CHUNKS, HALF, 128), BF16),
        v((PEERS, CH // 2, D), BF16), v((PEERS, HALF, D), BF16), v((PEERS, HALF, 128), BF16),
    ]
    for lanes in (512, 384, 128):
        scratch += [v((CHUNKS, PLANE, 16, lanes), BF16), v((CHUNKS, 16, lanes), BF16), v((PEERS, 16, lanes), BF16)]
    for lanes in (512, 256):
        scratch += [v((HALF, lanes), BF16), v((PLANE, 16, lanes), BF16), v((2, HALF, lanes), BF16)]
    scratch += [v((2, HALF, 512), BF16), v((2, HALF, 384), BF16), v((2, HALF, 128), BF16), v((CHUNKS, CHUNKS, HALF, 128), BF16)]
    for rows in (SE_ROWS, SL_ROWS):
        scratch += [v((5, rows, 128), F32), v((1, rows, 128), F32)] + [v((PEERS, rows, 128), F32)] * 3
    scratch += [
        pltpu.SemaphoreType.DMA((IDS.count,)),
        pltpu.SemaphoreType.DMA((IDS.count,)),
        pltpu.SemaphoreType.DMA((LOCAL,)),
    ]
    return pl.pallas_call(
        compute,
        out_shape=outs,
        in_specs=[hbm] * len(args),
        out_specs=[hbm] * len(outs),
        scratch_shapes=scratch,
        compiler_params=pltpu.CompilerParams(
            vmem_limit_bytes=63 * 1024 * 1024, collective_id=0, has_side_effects=True
        ),
    )(*args)


def finish(
    block, pages, down, up, qkv, out, merge, block_halo, early, late,
    block_o, pages_o, gain_m_o, shift_m_o, merge_o, gain_o, shift_o, qkv_o, qv_o, table_o, out_o, out_b_o, up_o, up_b_o,
    down_o, down_b_o, rms_o,
    block_i, pages_i, down_i, up_i, qkv_i, out_i, merge_i, block_f, pages_f, down_f, up_f, qkv_f, out_f, merge_f, slots_f, halo_f, isem, osem,
):
    chan = lax.axis_index("chan")
    ins = (down, up, qkv, merge, pages, block, out)
    bufs = (down_i, up_i, qkv_i, merge_i, pages_i, block_i, out_i)
    copies = [pltpu.make_async_copy(a, b, isem.at[i]) for i, (a, b) in enumerate(zip(ins, bufs))]
    for copy in copies:
        copy.start()

    def early_row(i):
        return early[pl.ds(chan * 6 + i - EARLY, 1), :]

    def late_row(i):
        return late[pl.ds(chan * EARLY + i, 1), :]

    def joined(ref, at, n):
        return jnp.concatenate([ref[at + i : at + i + 1, :] for i in range(n)], 1)

    gain_m_o[...] = late[SL_MERGE : SL_MERGE + 8, :]
    shift_m_o[...] = late[SL_MERGE + 8 : SL_MERGE + 16, :]
    gain_o[...] = jnp.concatenate([joined(late, SL_NORM, 4), joined(early, SE_NORM, 4)], 0)
    shift_o[...] = jnp.concatenate([joined(late, SL_NORM + 4, 4), joined(early, SE_NORM + 4, 4)], 0)
    qv_o[...] = jnp.concatenate([late_row(SM_QV), late_row(SM_QV + 1)], 0)
    for h in range(HEADS_C):
        table_o[h : h + 1, 0:128] = late_row(SM_TABLE + h)
        table_o[h : h + 1, 128:169] = late_row(SM_TABLE + HEADS_C + h)[:, 0:41]
    out_b_o[...] = early_row(SM_OUT_B)
    for i in range(4):
        up_b_o[i : i + 1, :] = early_row(SM_UP_B + i)
    down_b_o[...] = early_row(SM_DOWN_B)
    sums = jnp.sum(early[SE_SQ : SE_SQ + 8, :], 1, keepdims=True)
    roots = jnp.sqrt(sums * (1.0 / (1792 * COLS * D)))
    for i in range(3):
        rms_o[i] = roots[i, 0]

    outs = (down_o, up_o, qkv_o, merge_o, pages_o, block_o, out_o)
    stages = (down_f, up_f, qkv_f, merge_f, pages_f, block_f, out_f)
    done = [pltpu.make_async_copy(a, b, osem.at[i]) for i, (a, b) in enumerate(zip(stages, outs))]

    for n, (i, f) in enumerate(((down_i, down_f), (up_i, up_f))):
        copies[n].wait()
        f[...] = i[...].astype(F32)
        done[n].start()
    copies[2].wait()
    for i in range(3):
        qkv_f[i] = qkv_i[:, i * CH : i * CH + CH].astype(F32)
    done[2].start()
    copies[3].wait()
    for i in range(CHUNKS):
        merge_f[:, i * 128 : i * 128 + 128] = merge_i[i].astype(F32)
    done[3].start()
    copies[4].wait()

    def page(i, _):
        pages_f[i] = pages_i[i].astype(F32)
        return 0

    lax.fori_loop(0, 2 * ROWS, page, 0)
    done[4].start()
    copies[5].wait()
    slots_f[...] = block_i[...].astype(F32)
    halo_f[...] = block_halo[...].astype(F32)
    for wc in range(WC):
        for b in range(WIN):
            j = (wc * WIN + b + SHIFT) % COLS
            block_f[j, 0:SHIFT, :] = halo_f[pl.ds(wc * SHIFT * SLOT + b, SHIFT, stride=SLOT), :]
            for m in range(4 * ROWS // WIN):
                c, wr = m // 2, m % 2
                n = WIN - SHIFT if m == 4 * ROWS // WIN - 1 else WIN
                slot = wr * BAND + wc * WIN * SLOT + b
                block_f[j, SHIFT + WIN * m : SHIFT + WIN * m + n, :] = slots_f[c, pl.ds(slot, n, stride=SLOT), :]
    done[5].start()
    copies[6].wait()
    for k in range(2):
        for g in range(4):
            out_f[k * 64 : k * 64 + 64, g * 128 : g * 128 + 128] = out_i[k, g * 64 : g * 64 + 64, :].astype(F32)
    done[6].start()
    for copy in done:
        copy.wait()


def finish_call(parts):
    block, block_halo, pages, down, up, qkv, out, merge, early, late = parts
    vm = pl.BlockSpec(memory_space=pltpu.VMEM)
    hbm = pl.BlockSpec(memory_space=pl.ANY)

    def s(*shape):
        return jax.ShapeDtypeStruct(shape, F32)

    big = {
        "block": s(COLS, 4 * ROWS, CH), "pages": s(2 * ROWS, 2 * COLS, 256), "merge": s(1024, D),
        "qkv": s(3, D, CH), "out": s(CH, D), "up": s(D, 512), "down": s(512, D),
    }
    shapes = [
        big["block"], big["pages"], s(8, 128), s(8, 128), big["merge"], s(2, D), s(2, D), big["qkv"], s(2, CH), s(HEADS_C, 169),
        big["out"], s(1, 128), big["up"], s(4, 128), big["down"], s(1, 128), s(3),
    ]
    large = [any(shape is b for b in big.values()) for shape in shapes]
    ins = [block, pages, down.reshape(512, D), up.reshape(D, 512), qkv.reshape(D, 3 * CH), out, merge.reshape(CHUNKS, 1024, 128)]
    results = pl.pallas_call(
        finish,
        out_shape=shapes,
        in_specs=[hbm] * 7 + [vm] * 3,
        out_specs=[hbm if b else vm for b in large[:-1]] + [pl.BlockSpec(memory_space=pltpu.SMEM)],
        scratch_shapes=[pltpu.VMEM(a.shape, BF16) for a in ins]
        + [pltpu.VMEM(big[n].shape, F32) for n in ("block", "pages", "down", "up", "qkv", "out", "merge")]
        + [pltpu.VMEM(block.shape, F32), pltpu.VMEM(block_halo.shape, F32)]
        + [pltpu.SemaphoreType.DMA((7,)), pltpu.SemaphoreType.DMA((7,))],
        compiler_params=pltpu.CompilerParams(vmem_limit_bytes=63 * 1024 * 1024),
    )(*ins, block_halo, early, late)
    r = list(results)
    r[0] = r[0].transpose(1, 0, 2)
    r[2], r[3] = r[2].reshape(1024), r[3].reshape(1024)
    r[7] = r[7].transpose(1, 0, 2)
    r[11], r[13], r[15] = r[11].reshape(CH), r[13].reshape(512), r[15].reshape(CH)
    return tuple(r)


def body(
    pages, merge_gain, merge_shift, merge_weight, norm_gain, norm_shift, qkv_weight, qv_bias, rel_table,
    out_weight, out_bias, up_weight, up_bias, down_weight, down_bias, cotangent,
):
    args = [
        pages, cotangent.transpose(1, 0, 2), merge_weight, qkv_weight.transpose(1, 0, 2), out_weight, up_weight, down_weight,
        qv_bias, rel_table, out_bias, up_bias, down_bias, merge_gain, merge_shift, norm_gain, norm_shift, *constants(),
    ]
    return finish_call(kernel_call(args))


def solution(mesh):
    placed = (
        P(("space", "chan"), None, None), P(), P(), P(), P(), P(), P(None, None, "chan"), P(None, "chan"),
        P("chan", None), P("chan", None), P("chan"), P(None, "chan"), P("chan"), P("chan", None), P("chan"),
        P("space", None, "chan"),
    )
    outs = (
        P("space", None, "chan"), P(("space", "chan"), None, None), P(), P(), P(), P(), P(),
        P(None, None, "chan"), P(None, "chan"), P("chan", None), P("chan", None), P("chan"),
        P(None, "chan"), P("chan"), P("chan", None), P("chan"), P(),
    )
    return jax.shard_map(body, mesh=mesh, in_specs=placed, out_specs=outs, check_vma=False)
```

```python
import functools

import jax
import jax.numpy as jnp
import numpy as np
from jax import lax
from jax.experimental import pallas as pl
from jax.experimental.pallas import tpu as pltpu
from jax.sharding import PartitionSpec as P

D = 512
HEADS = 16
HD = 32
FF = 2048
WIN = 7
SHIFT = 3
COLS = 42
ROWS = 14
WC = COLS // WIN
SLOT = 8
PAIR = 2 * WIN * SLOT
NPAIR = WC
T = PAIR * NPAIR
BAND = WC * WIN * SLOT
CHUNKS = 4
CH = D // CHUNKS
HEADS_C = HEADS // CHUNKS
LIFT = 2 * SHIFT
EPS = 1e-05
MASKED = -1e9
SCALE = HD ** (-0.5)
F32 = jnp.float32
BF16 = jnp.bfloat16


def dot(a, b):
    return jnp.dot(a, b, preferred_element_type=F32)


def dot_nt(a, b):
    return lax.dot_general(a, b, (((1,), (1,)), ((), ())), preferred_element_type=F32)


def dot_tn(a, b):
    return lax.dot_general(a, b, (((0,), (0,)), ((), ())), preferred_element_type=F32)


def constants():
    slots = np.arange(WC * SLOT)
    column = slots // SLOT * WIN + slots % SLOT
    real = slots % SLOT < WIN
    pages_sel = np.zeros((2, WC * SLOT, 2 * COLS), np.float32)
    for parity in range(2):
        source = (2 * column + parity + LIFT) % (2 * COLS)
        pages_sel[parity, slots[real], source[real]] = 1
    pages_sel = pages_sel.reshape(2 * WC * SLOT, 2 * COLS)
    table_sel = np.zeros((256, SLOT, 128), np.float32)
    for b_q in range(WIN):
        for i in range(2 * WIN - 1):
            for b_k in range(WIN):
                code = (12 - i) * 13 + b_q - b_k + 6
                table_sel[code, b_q, i * SLOT + b_k] = 1
    table_sel = table_sel.reshape(256, SLOT * 128)
    table_sel_t = np.zeros((256, SLOT, 128), np.float32)
    for b_k in range(WIN):
        for i in range(2 * WIN - 1):
            for b_q in range(WIN):
                table_sel_t[i * 13 + b_q - b_k + 6, b_k, i * SLOT + b_q] = 1
    table_sel_t = table_sel_t.reshape(256, SLOT * 128)
    arrays = (pages_sel, pages_sel.T, table_sel, table_sel_t)
    return [jnp.asarray(a, BF16) for a in arrays]


def iota(shape, dim):
    return lax.broadcasted_iota(jnp.int32, shape, dim)


def gelu_parts(x):
    z = jnp.abs(x) * (0.5**0.5)
    t = 1.0 / (1.0 + 0.3275911 * z)
    e = jnp.exp(-z * z)
    poly = t * (0.254829592 + t * (-0.284496736 + t * (1.421413741 + t * (-1.453152027 + t * 1.061405429))))
    tail = 0.5 * poly * e
    cdf = jnp.where(x >= 0, 1.0 - tail, tail)
    return x * cdf, cdf + x * e * 0.3989422804014327


def unit_of(x):
    centered = x - jnp.mean(x, -1, keepdims=True)
    inverse = lax.rsqrt(jnp.mean(centered * centered, -1, keepdims=True) + EPS)
    return centered * inverse, inverse


def norm_back(dy, u, inverse, gain):
    scaled = dy * gain
    first = jnp.mean(scaled, -1, keepdims=True)
    second = jnp.mean(scaled * u, -1, keepdims=True)
    return inverse * (scaled - first - u * second)


def col_sum(x):
    return jnp.sum(x, 0, keepdims=True)


def pair_mask(row_cut, col_cut):
    k, q = iota((128, 128), 0), iota((128, 128), 1)
    half = PAIR // 2
    win_q, win_k = q // half, k // half
    a_q, a_k = (q % half) // SLOT, (k % half) // SLOT
    b_q, b_k = q % SLOT, k % SLOT
    ok = (win_q == win_k) & (k < PAIR) & (b_k < WIN)
    cut = WIN - SHIFT
    if row_cut:
        ok &= (a_q < cut) == (a_k < cut)
    if col_cut:
        ok &= ((b_q < cut) == (b_k < cut)) | (win_q == 0)
    return jnp.where(ok, 0.0, MASKED)


def head_lanes(x, h):
    lane = iota((1, CH), 1)
    return jnp.where(lane // HD == h, x, jnp.zeros_like(x))


def spread(x):
    padded = jnp.concatenate([x, jnp.zeros((128 - PAIR, CH), x.dtype)], 0)
    return jnp.concatenate([head_lanes(padded, h) for h in range(HEADS_C)], 0)


def stacked(x):
    return jnp.concatenate([head_lanes(x, h) for h in range(HEADS_C)], 0)


def by_head(x):
    return jnp.concatenate([x[:, 128 * h : 128 * h + 128] for h in range(HEADS_C)], 0)


def rows_of(p, count=PAIR):
    return pl.ds(pl.multiple_of(p * count, 16), count)


SM_QV, SM_TABLE, SM_OUT_B, SM_UP_B, SM_DOWN_B = 0, 2, 10, 11, 15
RP_GAIN0, RP_SHIFT0, RP_GAIN, RP_SHIFT = 0, 1, 2, 4


def row_of(ref, c, first, count):
    return jnp.concatenate([ref[c, first + i : first + i + 1, :] for i in range(count)], 1)


MESH = pl.DeviceIdType.MESH
HALF = 256
PEERS = CHUNKS - 1
PLANE = 15


class Sems:
    def __init__(self):
        self.count = 0

    def take(self, n):
        self.count += n
        return self.count - n


IDS = Sems()
ID_PAGES = IDS.take(1)
ID_SMALL = IDS.take(PEERS)
ID_W = IDS.take(4 * PEERS)
ID_WF = IDS.take(4 * PEERS)
ID_WN = IDS.take(4 * PEERS * 4)
ID_COT_HALO = IDS.take(1)
ID_COT = IDS.take(PEERS)
ID_BLK = IDS.take(PEERS)
ID_BLK_HALO = IDS.take(1)
ID_CORE = IDS.take(4 * CHUNKS)
ID_CORE_M = IDS.take(1)
ID_Y = IDS.take(2 * PEERS)
ID_Y_M = IDS.take(PEERS)
ID_FIRST = IDS.take(3 * CHUNKS * PLANE)
ID_THIRD = IDS.take(3 * PEERS)
ID_BACK_Y = IDS.take(2 * PEERS)
ID_BACK = IDS.take(3 * PLANE)
ID_A = IDS.take(2 * 2 * PLANE)
ID_GC = IDS.take(6)
ID_PG = IDS.take(1)
ID_MN = IDS.take(1)
ID_SG = IDS.take(2 * (1 + 3 * PEERS))
LOCAL = 56
UNROLL = 3
QKV, OUT, UP, DOWN = 0, 1, 2, 3

EARLY = 10
SE_NORM, SE_SQ, SE_ROWS = CHUNKS * (16 - EARLY), CHUNKS * (16 - EARLY) + 8, 40
SL_NORM, SL_MERGE, SL_ROWS = CHUNKS * EARLY, CHUNKS * EARLY + 8, 64


def chunk_off(j):
    return lax.rem(3 * j, 5) - 2 * (j // 3)


def feed_off(j):
    return lax.rem(2 * j, 5) - (j // 2 - j // 3)


def back_off(j):
    return lax.rem(j + 1, CHUNKS)


def compute(
    pages_in, cot_in, merge_in, qkv_in, out_in, up_in, down_in,
    qv_in, table_in, out_b_in, up_b_in, down_b_in, gain_m_in, shift_m_in, gain_in, shift_in,
    pages_sel_in, pages_sel_t_in, table_sel_in, table_sel_t_in,
    block_o, block_halo_o, pages_o, down_o, up_o, qkv_o, out_o, merge_o, early_o, late_o,
    qv_v, table_v, out_b_v, up_b_v, down_b_v, gain_m_v, shift_m_v, gain_v, shift_v,
    pages_sel, pages_sel_t, table_sel, table_sel_t, repl,
    pages, m_htx, m_hrx, g_htx, g_hrx, mn_htx, mn_hrx, cot_v, cot_tx, cot_hf, cot_htx, cot_hrx, merge_w, qkv_w, out_w, up_w, down_w, small,
    x0, inv, mn, mt, n1, qkv, prob, att, norm, r1, u2, n2, g2,
    hid, dpre, bias, ones, unit, lmat, dqkv, g1, gz, tmp,
    blk_rx, blk_htx, blk_hrx, pg,
    d_merge, d_qkv, d_out, d_up, d_down, d_small,
    l1_qkv, l1_out, l1_up, l1_down, l1_m, l2_out, l2_down, l2_m,
    up_1, up_h, up_3, qkv_1, qkv_h, qkv_3, mb_1, mb_h, mb_3,
    ga, rxa, gf_down, gb, rxb, gfb, gf_up, gf_qkv, gf_out, mf,
    se, se_c, se_y, se_z, se_x, sl, sl_c, sl_y, sl_z, sl_x,
    ssem, rsem, lsem,
):
    chan = lax.axis_index("chan")
    space = lax.axis_index("space")
    n_space = lax.axis_size("space")
    core = lax.rem(space, 2)
    z = lax.rem(space // 2, 4)
    x = space // 8
    last_chan = chan == CHUNKS - 1
    valid = (iota((PAIR, 1), 0) % SLOT < WIN).astype(F32)

    def at_y(d):
        return (space, lax.rem(chan + d, CHUNKS))

    def at_z(d):
        return (x * 8 + lax.rem(z + d, 4) * 2 + core, chan)

    def at_x(d):
        return (lax.rem(x + d, 4) * 8 + z * 2 + core, chan)

    def at_plane(m):
        return (lax.rem(x + m // 4, 4) * 8 + lax.rem(z + m % 4, 4) * 2 + core, chan)

    def place_of(m):
        return lax.rem(x + m // 4, 4) * 4 + lax.rem(z + m % 4, 4)

    def place_before(m):
        return lax.rem(x + 4 - m // 4, 4) * 4 + lax.rem(z + 4 - m % 4, 4)

    sibling = (x * 8 + z * 2 + 1 - core, chan)
    up_band = (lax.rem(space + n_space - 1, n_space), chan)
    down_band = (lax.rem(space + 1, n_space), chan)
    rank = space * CHUNKS + chan
    n_rank = n_space * CHUNKS
    before = lax.rem(rank + n_rank - 1, n_rank)
    after = lax.rem(rank + 1, n_rank)
    up_rank = (before // CHUNKS, lax.rem(before, CHUNKS))
    down_rank = (after // CHUNKS, lax.rem(after, CHUNKS))

    def send(src, dst, n, device, into=None):
        return pltpu.make_async_remote_copy(
            src_ref=src, dst_ref=dst, send_sem=ssem.at[n], recv_sem=rsem.at[n if into is None else into],
            device_id=device, device_id_type=MESH,
        )

    def local(src, dst, n):
        return pltpu.make_async_copy(src, dst, lsem.at[n])

    own_pages = local(pages_in, pages, 0)
    own_merge = local(merge_in, merge_w, 1)
    own_w = [
        local(src, dst.at[chan], 2 + i)
        for i, (src, dst) in enumerate(((qkv_in, qkv_w), (out_in, out_w)))
    ]
    own_mlp = [
        local(src.at[pl.ds(64 * i, 64)], dst.at[chan, i // 2, i % 2], 40 + 8 * n + i)
        for n, (src, dst) in enumerate(((up_in, up_w), (down_in, down_w)))
        for i in range(8)
    ]
    own_cot = local(cot_in, cot_v, 6)
    tiny = (qv_in, table_in, out_b_in, up_b_in, down_b_in, gain_m_in, shift_m_in, gain_in, shift_in)
    tiny_v = (qv_v, table_v, out_b_v, up_b_v, down_b_v, gain_m_v, shift_m_v, gain_v, shift_v)
    tiny_copies = [local(src, dst, 24 + i) for i, (src, dst) in enumerate(zip(tiny, tiny_v))]
    tables_in = (pages_sel_in, pages_sel_t_in, table_sel_in, table_sel_t_in)
    sel_copies = [
        local(src, dst, 33 + i) for i, (src, dst) in enumerate(zip(tables_in, (pages_sel, pages_sel_t, table_sel, table_sel_t)))
    ]
    for copy in tiny_copies + sel_copies[0:1] + [own_pages, own_cot, own_merge, sel_copies[3], own_w[QKV]]:
        copy.start()
    for copy in [own_w[OUT]] + own_mlp + [sel_copies[1], sel_copies[2]]:
        copy.start()

    barrier = pltpu.get_barrier_semaphore()
    greeted = [at_y(d) for d in (1, 2, 3)] + [at_plane(m) for m in range(1, PLANE + 1)]
    greeted += [sibling, up_band, down_band, up_rank, down_rank]
    for by in (1, 3):
        greeted.append((lax.rem(x + by, 4) * 8 + z * 2 + 1 - core, chan))
        greeted.append((x * 8 + lax.rem(z + by, 4) * 2 + 1 - core, chan))
    for device in greeted:
        pl.semaphore_signal(barrier, inc=1, device_id=device, device_id_type=MESH)

    for copy in tiny_copies:
        copy.wait()
    lane_rows = lambda ref, n: ref[...].astype(F32).reshape(1, n)
    small[chan, SM_QV : SM_QV + 2, :] = qv_v[...].astype(F32)
    table = table_v[...].astype(F32)
    small[chan, SM_TABLE : SM_TABLE + 4, :] = table[:, 0:128]
    small[chan, SM_TABLE + 4 : SM_TABLE + 8, :] = jnp.concatenate([table[:, 128:169], jnp.zeros((4, 87), F32)], 1)
    small[chan, SM_OUT_B : SM_OUT_B + 1, :] = lane_rows(out_b_v, 128)
    up_row = lane_rows(up_b_v, 512)
    for i in range(4):
        small[chan, SM_UP_B + i : SM_UP_B + i + 1, :] = up_row[:, i * 128 : i * 128 + 128]
    small[chan, SM_DOWN_B : SM_DOWN_B + 1, :] = lane_rows(down_b_v, 128)
    repl[RP_GAIN0 : RP_GAIN0 + 1, :] = lane_rows(gain_m_v, 1024)
    repl[RP_SHIFT0 : RP_SHIFT0 + 1, :] = lane_rows(shift_m_v, 1024)
    repl[RP_GAIN : RP_GAIN + 2, 0:D] = gain_v[...].astype(F32)
    repl[RP_SHIFT : RP_SHIFT + 2, 0:D] = shift_v[...].astype(F32)
    pl.semaphore_wait(barrier, len(greeted))

    halves = (HALF, CH // 2, HALF, HALF)
    weights = (qkv_w, out_w, up_w, down_w)
    sources = (qkv_in, out_in, up_in, down_in)

    def axis_of(w):
        return (x, lambda d, k: (lax.rem(x + d, 4) * 8 + z * 2 + k, chan)) if w in (QKV, UP) else (
            z, lambda d, k: (x * 8 + lax.rem(z + d, 4) * 2 + k, chan)
        )

    def rows_in(ref, w, first, n, c=None):
        rows = pl.ds(pl.multiple_of(first, 16), n)
        if c is None:
            return ref.at[:, rows] if w == QKV else ref.at[rows]
        return ref.at[c, :, rows] if w == QKV else ref.at[c, rows]

    def quarter(w, k):
        return lax.rem(axis_of(w)[0], 2) * halves[w] + k * (halves[w] // 2)

    def weight_copy(w, d):
        n = halves[w] // 2
        src = rows_in(sources[w], w, quarter(w, core), n)
        return send(src, rows_in(weights[w], w, quarter(w, core), n, chan), ID_W + w * PEERS + d - 1, at_y(d))

    def arrived(w, d, c):
        part = rows_in(weights[w], w, quarter(w, core), halves[w] // 2, c)
        send(part, part, ID_W + w * PEERS + d - 1, at_y(d)).wait_recv()

    def forward_copies(w, d, c):
        part = rows_in(weights[w], w, quarter(w, core), halves[w] // 2, c)
        yield send(part, part, ID_WF + w * PEERS + d - 1, sibling)
        n = halves[w] // 4
        base = ID_WN + (w * PEERS + d - 1) * 4
        for i, by in enumerate((1, 3)):
            part = rows_in(weights[w], w, quarter(w, core) + i * n, n, c)
            for same in range(2):
                device = axis_of(w)[1](by, core if same else 1 - core)
                yield send(part, part, base + i * 2 + same, device, base + i * 2 + core)

    def forwarded(w, d, c):
        part = rows_in(weights[w], w, quarter(w, 1 - core), halves[w] // 2, c)
        send(part, part, ID_WF + w * PEERS + d - 1, sibling).wait_recv()
        n = halves[w] // 4
        base = ID_WN + (w * PEERS + d - 1) * 4
        half = (1 - lax.rem(axis_of(w)[0], 2)) * halves[w]
        for i in range(2):
            for k in range(2):
                part = rows_in(weights[w], w, half + (k * 2 + i) * n, n, c)
                send(part, part, base + i * 2 + k, sibling).wait_recv()

    fourth = lax.rem(x + 2 * z, 4)

    def eighth_copy(w, d):
        part = weights[w].at[chan, fourth, core]
        src = sources[w].at[pl.ds(pl.multiple_of(fourth * 128 + core * 64, 64), 64)]
        return send(src, part, ID_W + w * PEERS + d - 1, at_y(d))

    def around_copies(w, d, c):
        part = weights[w].at[c, fourth, core]
        base = ID_WN + (w * PEERS + d - 1) * 4
        yield send(part, part, base, at_x(1))
        yield send(part, part, base + 1, at_x(3))
        for i, by in enumerate((1, 3)):
            half = part.at[pl.ds(32 * i, 32)]
            yield send(half, half, base + 2 + i, at_z(by))

    def across_copy(w, d, c):
        part = weights[w].at[c, :, core]
        return send(part, part, ID_WF + w * PEERS + d - 1, sibling)

    def chunk_peer(j):
        off = feed_off(j)
        return CHUNKS - off, lax.rem(chan + off, CHUNKS)

    def pass_around(w, j):
        d, c = chunk_peer(j)
        part = weights[w].at[c, fourth, core]
        send(part, part, ID_W + w * PEERS + d - 1, at_y(d)).wait_recv()
        for copy in around_copies(w, d, c):
            copy.start()

    def pass_across(w, j):
        d, c = chunk_peer(j)
        base = ID_WN + (w * PEERS + d - 1) * 4
        for i, by in enumerate((3, 1)):
            part = weights[w].at[c, lax.rem(fourth + by, 4), core]
            send(part, part, base + i, sibling).wait_recv()
        for i in range(2):
            part = weights[w].at[c, lax.rem(fourth + 2, 4), core, pl.ds(32 * i, 32)]
            send(part, part, base + 2 + i, sibling).wait_recv()
        across_copy(w, d, c).start()

    def have_across(w, j):
        d, c = chunk_peer(j)
        part = weights[w].at[c, :, 1 - core]
        send(part, part, ID_WF + w * PEERS + d - 1, sibling).wait_recv()

    def pass_on(w, j):
        off = chunk_off(j)
        c, d = lax.rem(chan + off, CHUNKS), CHUNKS - off
        arrived(w, d, c)
        for copy in forward_copies(w, d, c):
            copy.start()

    def have(w, j):
        off = chunk_off(j)
        forwarded(w, CHUNKS - off, lax.rem(chan + off, CHUNKS))

    small_copies = [send(small.at[chan], small.at[chan], ID_SMALL + d - 1, at_y(d)) for d in (1, 3, 2)]
    weight_copies = [[(weight_copy if w in (QKV, OUT) else eighth_copy)(w, d) for d in (1, 3, 2)] for w in range(4)]
    for copy in small_copies + weight_copies[QKV][0:2]:
        copy.start()

    def quads(i, _):
        base = (i // WIN) * BAND + lax.rem(i, WIN) * SLOT
        for q in range(2):
            y = dot(pages_sel[...], pages[lax.rem(2 * i + q + LIFT, 2 * ROWS)])
            for par in range(2):
                for wc in range(WC):
                    lanes = par * 512 + q * 256
                    at = pl.multiple_of(base + wc * WIN * SLOT, SLOT)
                    first = par * WC * SLOT + wc * SLOT
                    tmp[pl.ds(at, SLOT), lanes : lanes + 256] = y[first : first + SLOT]
        return 0

    own_pages.wait()
    sel_copies[0].wait()
    gain = [repl[RP_GAIN + i : RP_GAIN + i + 1, 0:D] for i in range(2)]
    shift = [repl[RP_SHIFT + i : RP_SHIFT + i + 1, 0:D] for i in range(2)]
    three = range(NPAIR // 2)
    cut_rows = WIN - SHIFT
    n_halo = SHIFT * SLOT

    def pair_rows(half, i):
        return slice(half * BAND + i * PAIR, half * BAND + i * PAIR + PAIR)

    def band(half):
        return slice(half * BAND, half * BAND + BAND)

    def merge_rows(half):
        lax.fori_loop(half * WIN, half * WIN + WIN, quads, 0)
        for i in three:
            r = pair_rows(half, i)
            u, inverse = unit_of(tmp[r, :])
            x0[r, :] = u.astype(BF16)
            inv[r, 0:1] = inverse
            mn[r, :] = (u * repl[RP_GAIN0 : RP_GAIN0 + 1, :] + repl[RP_SHIFT0 : RP_SHIFT0 + 1, :]).astype(BF16)
        return dot(mn[band(half), :], merge_w[...])

    def norm1(half):
        for i in three:
            r = pair_rows(half, i)
            u, _inverse = unit_of(mt[r, :].astype(F32))
            n1[r, :] = (u * gain[0] + shift[0]).astype(BF16)

    def halo_of(rows):
        starts = [wc * WIN * SLOT + cut_rows * SLOT for wc in range(WC)]
        return jnp.concatenate([rows[at : at + n_halo] for at in starts], 0)

    def with_halo(rows, halo):
        parts = []
        for wc in range(WC):
            at = wc * WIN * SLOT
            parts += [rows[at : at + cut_rows * SLOT], halo[wc * n_halo : wc * n_halo + n_halo]]
        return jnp.concatenate(parts, 0)

    own_merge.wait()
    merged_last = merge_rows(1)
    mt[band(1), :] = merged_last.astype(BF16)
    m_htx[...] = halo_of(merged_last).astype(BF16)
    merged_halo = send(m_htx, m_hrx, ID_PAGES, up_rank)
    merged_halo.start()
    for copy in weight_copies[QKV][2:] + weight_copies[OUT]:
        copy.start()
    for i in (2, 0, 1):
        for w in (UP, DOWN):
            weight_copies[w][i].start()
    mt[band(0), :] = merge_rows(0).astype(BF16)
    norm1(0)

    own_cot.wait()
    norm[...] = jnp.zeros_like(norm)
    cot_hf[...] = jnp.zeros_like(cot_hf)
    for wc in range(WC):
        for b in range(WIN):
            column = cot_v[(wc * WIN + b + SHIFT) % COLS].astype(F32)
            cot_hf[pl.ds(wc * SHIFT * SLOT + b, SHIFT, stride=SLOT), :] = column[0:SHIFT]
            for m in range(4 * ROWS // WIN):
                c, wr = m // 2, m % 2
                n = cut_rows if m == 4 * ROWS // WIN - 1 else WIN
                slot = wr * BAND + wc * WIN * SLOT + b
                norm[c, pl.ds(slot, n, stride=SLOT), :] = column[SHIFT + WIN * m : SHIFT + WIN * m + n]
    cot_htx[...] = cot_hf[...].astype(BF16)
    cot_halo = send(cot_htx, cot_hrx, ID_COT_HALO, up_band)
    cot_halo.start()

    sel_copies[3].wait()
    for d in (1, 2, 3):
        part = small.at[lax.rem(chan + CHUNKS - d, CHUNKS)]
        send(part, part, ID_SMALL + d - 1, at_y(d)).wait_recv()
    lmat[...] = jnp.zeros_like(lmat)
    masks = [pair_mask(kind // 2, kind % 2) for kind in range(4)]
    for h in range(HEADS_C):
        lanes = jnp.where(iota((128, CH), 1) // HD == h, 1.0, 0.0)
        ones[h * 128 : h * 128 + 128, :] = lanes.astype(BF16)
    unit[...] = jnp.where(iota((PAIR, 128), 0) == iota((PAIR, 128), 1), 1.0, 0.0).astype(BF16)

    def tables(c, _):
        table = jnp.concatenate([small[c, SM_TABLE : SM_TABLE + 4, :], small[c, SM_TABLE + 4 : SM_TABLE + 8, :]], 1)
        table = jnp.concatenate([table, jnp.zeros_like(table)], 0).astype(BF16)
        placed = dot(table, table_sel_t[...])
        for b_k in range(WIN):
            for h in range(HEADS_C):
                lmat[h * SLOT + b_k : h * SLOT + b_k + 1, :] = placed[h : h + 1, b_k * 128 : b_k * 128 + 128]
        for h in range(HEADS_C):
            tab = lmat[h * SLOT : h * SLOT + SLOT, :]
            lane = iota((SLOT, 128), 1)
            slabs = []
            for a in range(WIN):
                moved = pltpu.roll(tab, (128 - (WIN - 1 - a) * SLOT) % 128, 1) if a < WIN - 1 else tab
                low = jnp.where(lane < WIN * SLOT, moved, 0.0)
                slabs.append(low + pltpu.roll(low, WIN * SLOT, 1))
            one = jnp.concatenate(slabs * 2 + [jnp.zeros((128 - PAIR, 128), F32)], 0)
            for kind in range(4):
                bias[kind, c, h * 128 : h * 128 + 128, :] = (one + masks[kind]).astype(BF16)
        return 0

    lax.fori_loop(0, CHUNKS, tables, 0)

    pass_on(QKV, 1)
    merged_halo.wait_recv()
    mt[band(1), :] = with_halo(mt[band(1), :].astype(F32), m_hrx[...].astype(F32)).astype(BF16)
    norm1(1)
    pass_on(QKV, 2)

    cot_halo.wait_recv()
    norm[PEERS, BAND:T, :] = with_halo(norm[PEERS, BAND:T, :], cot_hrx[...].astype(F32))
    cot_tx[...] = norm[...].astype(BF16)
    lanes_here = pl.ds(pl.multiple_of(chan * CH, CH), CH)
    cot_copies = [
        send(cot_tx.at[lax.rem(chan + d, CHUNKS)], g2.at[:, lanes_here], ID_COT + d - 1, at_y(d)) for d in (1, 3, 2)
    ]
    for copy in cot_copies:
        copy.start()
    g2[:, lanes_here] = cot_tx[chan]

    mn_htx[...] = halo_of(mn[band(1), :].astype(F32)).astype(BF16)
    normed_halo = send(mn_htx, mn_hrx, ID_MN, up_rank)
    normed_halo.start()

    def wide(c):
        return jnp.concatenate([qkv_w[c, i] for i in range(3)], 1)

    own_w[QKV].wait()

    def attend(j, _):
        c = lax.rem(chan + chunk_off(j), CHUNKS)
        heads = pl.ds(pl.multiple_of(c * CH, CH), CH)

        @pl.when(j > 0)
        def _():
            have(QKV, j)

        projected = dot(n1[...], wide(c))
        zeros = jnp.zeros((1, CH), F32)
        offset = jnp.concatenate([small[c, SM_QV : SM_QV + 1, :], zeros, small[c, SM_QV + 1 : SM_QV + 2, :]], 1)
        scaled = jnp.concatenate([jnp.full((1, CH), SCALE, F32), jnp.ones((1, 2 * CH), F32)], 1)
        qkv[c] = ((projected + offset) * scaled).astype(BF16)

        @pl.when(j == 0)
        def _():
            pass_on(QKV, 3)

        def window_pairs(t, _):
            pairs = [UNROLL * t + i for i in range(UNROLL)]
            parts = [[qkv[c, rows_of(p), i * CH : i * CH + CH] for i in range(3)] for p in pairs]
            results = []
            for i, (q, k, v) in enumerate(parts):
                table = bias[2 * (chan // PEERS) * t + i // (UNROLL - 1), c]
                s = dot_nt(jnp.concatenate([q, unit[...]], 1), jnp.concatenate([spread(k), table], 1))
                weights = []
                for h in range(HEADS_C):
                    sh = s[:, 128 * h : 128 * h + 128]
                    weights.append(jnp.exp(sh - jnp.max(sh, -1, keepdims=True)).astype(BF16))
                w = jnp.concatenate(weights, 1)
                o = dot(w, jnp.concatenate([spread(v), ones[...]], 1))
                inverse = 1.0 / o[:, CH:]
                results.append((w, o[:, 0:CH] * inverse, inverse))
            for p, (w, o, inverse) in zip(pairs, results):
                prob[c, p] = w
                att[rows_of(p), heads] = o.astype(BF16)
                norm[c, rows_of(p), :] = inverse
            return 0

        lax.fori_loop(0, NPAIR // UNROLL, window_pairs, 0)

        @pl.when(j == 1)
        def _():
            for i in range(1, CHUNKS):
                pass_on(OUT, i)
            for w in (UP, DOWN):
                pass_around(w, 1)

        @pl.when(j == 2)
        def _():
            for w in (UP, DOWN):
                pass_around(w, 2)

        @pl.when(j == 3)
        def _():
            for w in (UP, DOWN):
                pass_around(w, 3)
                pass_across(w, 1)

        return 0

    lax.fori_loop(0, CHUNKS, attend, 0)

    own_w[OUT].wait()
    for j in range(1, CHUNKS):
        have(OUT, j)
    tmp[:, 0:D] = dot(att[...], out_w[...].reshape(D, D))
    out_b = jnp.concatenate([small[c, SM_OUT_B : SM_OUT_B + 1, :] for c in range(CHUNKS)], 1)
    down_b = jnp.concatenate([small[c, SM_DOWN_B : SM_DOWN_B + 1, :] for c in range(CHUNKS)], 1)

    def norm2(half):
        total = 0.0
        for i in three:
            r = pair_rows(half, i)
            branch = tmp[r, 0:D] + out_b
            resid = mt[r, :].astype(F32) + branch
            r1[r, :] = resid
            u, inverse = unit_of(resid.astype(BF16).astype(F32))
            u2[r, :] = u.astype(BF16)
            inv[r, 1:2] = inverse
            n2[r, :] = (u * gain[1] + shift[1]).astype(BF16)
            total = total + col_sum(branch * branch * valid)
        return total

    sq_one = norm2(0) + norm2(1)
    for w in (UP, DOWN):
        pass_across(w, 2)

    for d in (1, 2, 3):
        part = g2.at[:, pl.ds(pl.multiple_of(lax.rem(chan + CHUNKS - d, CHUNKS) * CH, CH), CH)]
        send(part, part, ID_COT + d - 1, at_y(d)).wait_recv()

    grads = (d_qkv, d_out, d_up, d_down)
    firsts = (l1_qkv, l1_out, l1_up, l1_down)
    order = (1, 3, 2)
    around = range(1, PLANE + 1)
    here = x * 4 + z

    def step(n, lead=0):
        return pl.ds(pl.multiple_of(lead, 16), n)

    def half_grad(w, c, k):
        return grads[w].at[c, step(halves[w], k * halves[w])]

    def core_copy(w, j, c):
        return send(half_grad(w, c, 1 - core), firsts[w].at[j], ID_CORE + w * CHUNKS + j, sibling)

    def core_sum(w, j, off):
        c = lax.rem(chan + off, CHUNKS)
        core_copy(w, j, c).wait_recv()
        size = min(halves[w], 64)
        for t in range(0, halves[w], size):
            r = step(size, core * halves[w] + t)
            total = grads[w][c, r, :].astype(F32) + firsts[w][j, t : t + size, :].astype(F32)
            grads[w][c, r, :] = total.astype(BF16)

    owners = {DOWN: (0, l2_down), OUT: (1, l2_out)}

    def owner_copy(w, off):
        n, into = owners[w]
        c = lax.rem(chan + off, CHUNKS)
        return send(half_grad(w, c, core), into.at[off - 1], ID_Y + n * PEERS + off - 1, at_y(off))

    def to_owner(w, off):
        @pl.when(off > 0)
        def _():
            owner_copy(w, off).start()

    def owner_wait(w):
        n, into = owners[w]
        for d in order:
            send(into.at[d - 1], into.at[d - 1], ID_Y + n * PEERS + d - 1, at_y(d)).wait_recv()

    def owner_sum(w, t, size):
        total = grads[w][chan, step(size, core * halves[w] + t), :].astype(F32)
        for d in range(PEERS):
            total += owners[w][1][d, t : t + size, :].astype(F32)
        return total.astype(BF16)

    class Plane:
        def __init__(self, n, g, rx, gf):
            self.n, self.g, self.rx, self.gf = n, g, rx, gf

        def out_copies(self):
            for m in around:
                src = self.g.at[step(16, place_of(m) * 16)]
                yield send(src, self.rx.at[m - 1], ID_A + self.n * 2 * PLANE + m - 1, at_plane(m))

        def back_copies(self, wait):
            for m in around:
                part = self.gf.at[core, step(16, (place_before(m) if wait else here) * 16)]
                yield send(part, part, ID_A + (self.n * 2 + 1) * PLANE + m - 1, at_plane(m))

        def start(self):
            for copy in self.out_copies():
                copy.start()

        def back_start(self):
            for copy in self.out_copies():
                copy.wait_recv()
            total = self.g[step(16, here * 16), :].astype(F32)
            for m in around:
                total += self.rx[m - 1].astype(F32)
            self.gf[core, step(16, here * 16), :] = total.astype(BF16)
            for copy in self.back_copies(False):
                copy.start()

        def finish(self):
            for copy in self.back_copies(True):
                copy.wait_recv()

        def left(self):
            for copy in [*self.out_copies(), *self.back_copies(False)]:
                copy.wait_send()

    plane_a = Plane(0, ga, rxa, gf_down)
    plane_b = Plane(1, gb, rxb, gfb)

    class Spread:
        def __init__(self, n, src, first, h, third, into):
            self.n, self.src, self.first, self.h, self.third, self.into = n, src, first, h, third, into

        def first_copies(self, j, c):
            for m in around:
                src = self.src(c, place_of(m) * 16, 16)
                n = ID_FIRST + (self.n * CHUNKS + j) * PLANE + m - 1
                yield send(src, self.first.at[c, m - 1], n, at_plane(m))

        def first_start(self, j, c):
            for copy in self.first_copies(j, c):
                copy.start()

        def third_copies(self):
            for d in order:
                src = self.h.at[lax.rem(chan + d, CHUNKS)]
                yield send(src, self.third.at[d - 1], ID_THIRD + self.n * PEERS + d - 1, at_y(d))

        def third_start(self, chunk_of):
            for j in range(CHUNKS):
                c = chunk_of(j)
                for copy in self.first_copies(j, c):
                    copy.wait_recv()
                total = self.src(c, here * 16, 16)[...].astype(F32)
                for m in around:
                    total += self.first[c, m - 1].astype(F32)
                self.h[c] = total.astype(BF16)
            for copy in self.third_copies():
                copy.start()

        def third_sum(self):
            for copy in self.third_copies():
                copy.wait_recv()
            total = self.h[chan].astype(F32)
            for d in range(PEERS):
                total += self.third[d].astype(F32)
            self.into(chan, here * 16, 16)[...] = total.astype(BF16)

        def back_y(self, wait):
            for d in order:
                part = self.into(lax.rem(chan + (CHUNKS - d if wait else 0), CHUNKS), here * 16, 16)
                yield send(part, part, ID_BACK_Y + d - 1, at_y(d))

        def back_copies(self, wait):
            for m in around:
                part = self.into(None, (place_before(m) if wait else here) * 16, 16)
                yield send(part, part, ID_BACK + self.n * PLANE + m - 1, at_plane(m))

        def back_start(self):
            for copy in self.back_copies(False):
                copy.start()

        def finish(self):
            for copy in self.back_copies(True):
                copy.wait_recv()

        def left(self, chunk_of):
            for j in range(CHUNKS):
                for copy in self.first_copies(j, chunk_of(j)):
                    copy.wait_send()
            for copy in [*self.third_copies(), *self.back_copies(False)]:
                copy.wait_send()

    def half_rows(w):
        return lambda c, row, n: grads[w].at[c, step(n, core * halves[w] + row)]

    group_a, group_b = 2 * core, 2 * core + 1
    spread_up = Spread(0, half_rows(UP), up_1, up_h, up_3, lambda c, row, n: gf_up.at[core, step(n, row)])
    spread_qkv = Spread(1, half_rows(QKV), qkv_1, qkv_h, qkv_3, lambda c, row, n: gf_qkv.at[core, step(n, row)])
    spread_m = Spread(
        2, lambda c, row, n: d_merge.at[group_b, c, step(n, row)], mb_1, mb_h, mb_3,
        lambda c, row, n: mf.at[group_b, slice(None) if c is None else c, step(n, row)],
    )

    def core_out(n, part):
        return send(part, part, ID_GC + n, sibling)

    def feed_chunk(j):
        return lax.rem(chan + feed_off(j), CHUNKS)

    def back_chunk(j):
        return lax.rem(chan + back_off(j), CHUNKS)

    def feed_sums(j):
        core_sum(DOWN, j, feed_off(j))
        to_owner(DOWN, feed_off(j))
        core_sum(UP, j, feed_off(j))
        spread_up.first_start(j, feed_chunk(j))

    def back_sums(j):
        core_sum(OUT, j, back_off(j))
        to_owner(OUT, back_off(j))
        core_sum(QKV, j, back_off(j))
        spread_qkv.first_start(j, back_chunk(j))

    class Small:
        def __init__(self, n, own, into):
            self.n, self.own, self.into = n, own, into

        def copies(self, level):
            base = ID_SG + self.n * (1 + 3 * PEERS)
            if level == 0:
                return [send(self.own.at[0], self.into[0].at[0], base, sibling)]
            at = (at_y, at_z, at_x)[level - 1]
            base += (level - 1) * PEERS
            return [send(self.own.at[level], self.into[level].at[d - 1], base + d, at(d)) for d in order]

        def start(self, level):
            for copy in self.copies(level):
                copy.start()

        def sum(self, level):
            for copy in self.copies(level):
                copy.wait_recv()
            total = self.own[level]
            for d in range(self.into[level].shape[0]):
                total += self.into[level][d]
            self.own[level + 1] = total

    small_early = Small(0, se, (se_c, se_y, se_z, se_x))
    small_late = Small(1, sl, (sl_c, sl_y, sl_z, sl_x))

    def lay(ref, at, row):
        for i in range(row.shape[1] // 128):
            ref[0, at + i : at + i + 1, :] = row[:, i * 128 : i * 128 + 128]

    tmp[...] = jnp.zeros_like(tmp)
    for copy in own_mlp:
        copy.wait()

    def feed(j, _):
        c = feed_chunk(j)

        @pl.when(j > 0)
        def _():
            have_across(UP, j)
            have_across(DOWN, j)

        @pl.when(j == 1)
        def _():
            for w in (UP, DOWN):
                pass_across(w, 3)

        up_c, down_c = up_w[c].reshape(D, 512), down_w[c].reshape(512, D)
        up_b = row_of(small, c, SM_UP_B, 4)
        d_up_b = 0.0
        for first in range(0, T, T // 3):
            r = slice(first, first + T // 3)
            value, slope = gelu_parts(dot(n2[r, :], up_c) + up_b)
            hid[r, :] = value.astype(BF16)
            d = slope * dot_nt(g2[r, :], down_c)
            dpre[r, :] = d.astype(BF16)
            d_up_b = d_up_b + col_sum(d)
        for i in range(4):
            d_small[c, SM_UP_B + i : SM_UP_B + i + 1, :] = d_up_b[:, i * 128 : i * 128 + 128]
        d_down[c] = dot_tn(hid[...], g2[...]).astype(BF16)
        core_copy(DOWN, j, c).start()
        d_up[c] = dot_tn(n2[...], dpre[...]).astype(BF16)
        core_copy(UP, j, c).start()
        tmp[:, 0:D] += dot(hid[...], down_c)
        tmp[:, D : 2 * D] += dot_nt(dpre[...], up_c)

        feed_sums(j)
        return 0

    lax.fori_loop(0, CHUNKS, feed, 0)

    for copy in [cot_halo] + cot_copies:
        copy.wait_send()
    blk_tx = cot_tx
    def norm2_back(half):
        totals = [0.0] * 6
        for i in three:
            r = pair_rows(half, i)
            branch = tmp[r, 0:D] + down_b
            result = r1[r, :] + branch
            for c in range(CHUNKS):
                blk_tx[c, r, :] = result[:, c * CH : c * CH + CH].astype(BF16)
            u = u2[r, :].astype(F32)
            dy = tmp[r, D : 2 * D]
            g = g2[r, :].astype(F32)
            grad = g + norm_back(dy, u, inv[r, 1:2], gain[1])
            tmp[r, 0:D] = grad
            g1[r, :] = grad.astype(BF16)
            terms = (branch * branch * valid, result * result * valid, g, dy * u, dy, grad)
            totals = [total + col_sum(term) for total, term in zip(totals, terms)]
        return totals

    sq_two, sq_out, d_down_b, d_gain1, d_shift1, d_out_b = (a + b for a, b in zip(norm2_back(0), norm2_back(1)))
    for c in range(CHUNKS):
        d_small[c, SM_DOWN_B : SM_DOWN_B + 1, :] = d_down_b[:, c * CH : c * CH + CH]
        d_small[c, SM_OUT_B : SM_OUT_B + 1, :] = d_out_b[:, c * CH : c * CH + CH]

    for c in range(CHUNKS):
        se[0, c * 6 : c * 6 + 6, :] = d_small[c, EARLY:16, :]
    lay(se, SE_NORM, d_gain1)
    lay(se, SE_NORM + 4, d_shift1)
    squares = [sum(sq[:, i * 128 : i * 128 + 128] for i in range(4)) for sq in (sq_out, sq_one, sq_two)]
    se[0, SE_SQ:SE_ROWS, :] = jnp.concatenate(squares + [jnp.zeros((5, 128), F32)], 0)
    small_early.start(0)

    blk_copies = [
        send(blk_tx.at[lax.rem(chan + d, CHUNKS)], blk_rx.at[chan], ID_BLK + d - 1, at_y(d)) for d in (1, 3, 2)
    ]
    blk_rx[chan] = blk_tx[chan]

    normed_halo.wait_recv()
    mn[band(1), :] = with_halo(mn[band(1), :].astype(F32), mn_hrx[...].astype(F32)).astype(BF16)

    sel_copies[2].wait()
    d_out[...] = dot_tn(att[...], g1[...]).astype(BF16).reshape(CHUNKS, CH, D)
    hid[...] = dot_nt(g1[...], out_w[...].reshape(D, D)).astype(BF16)

    def attend_back(j, _):
        c = lax.rem(chan + back_off(j), CHUNKS)
        heads = pl.ds(pl.multiple_of(c * CH, CH), CH)
        core_copy(OUT, j, c).start()
        sum_rows = pl.ds(pl.multiple_of(c * PAIR, 16), PAIR)

        def window_pairs(t, carry):
            pairs = [UNROLL * t + i for i in range(UNROLL)]
            parts = [[qkv[c, rows_of(p), i * CH : i * CH + CH] for i in range(3)] for p in pairs]
            d_atts = [hid[rows_of(p), heads].astype(F32) * norm[c, rows_of(p), :] for p in pairs]
            outs = [att[rows_of(p), heads] for p in pairs]
            probs = [prob[c, p] for p in pairs]
            results, total = [], 0.0
            for (q, k, v), d_att, o, w in zip(parts, d_atts, outs, probs):
                left = jnp.concatenate([d_att, -d_att * o.astype(F32)], 1).astype(BF16)
                d_s = w.astype(F32) * dot_nt(left, jnp.concatenate([spread(v), ones[...]], 1))
                total = total + d_s
                d_s = d_s.astype(BF16)
                d_q = dot(d_s, spread(k)) * SCALE
                d_k = dot_tn(by_head(d_s), stacked(q))[0:PAIR]
                d_v = dot_tn(by_head(w), stacked(left[:, 0:CH]))[0:PAIR]
                results.append(jnp.concatenate([d_q, d_k, d_v], 1).astype(BF16))
            for p, result in zip(pairs, results):
                dqkv[c, rows_of(p), :] = result
            return carry + total

        r1[sum_rows, :] = lax.fori_loop(0, NPAIR // UNROLL, window_pairs, jnp.zeros((PAIR, 512), F32))
        d_qkv[c] = dot_tn(n1[...], dqkv[c]).astype(BF16)
        core_copy(QKV, j, c).start()

        @pl.when(j > 0)
        def _():
            back_sums(j - 1)

        @pl.when(j == 0)
        def _():
            small_early.sum(0)
            small_early.start(1)

        @pl.when(j == 1)
        def _():
            owner_wait(DOWN)
            for t in range(0, HALF, 64):
                ga[t : t + 64, :] = owner_sum(DOWN, t, 64)
            plane_a.start()
            spread_up.third_start(feed_chunk)
            for copy in blk_copies:
                copy.start()

        @pl.when(j == 2)
        def _():
            small_early.sum(1)
            small_early.start(2)

        @pl.when(j == 3)
        def _():
            plane_a.back_start()
            spread_up.third_sum()
            spread_up.back_start()

        return 0

    lax.fori_loop(0, CHUNKS, attend_back, 0)

    def norm1_back(half):
        rows = band(half)
        tmp[rows, D : 2 * D] = sum(dot_nt(dqkv[c, rows, :], wide(c)) for c in range(CHUNKS))
        d_gain, d_shift = 0.0, 0.0
        for i in three:
            r = pair_rows(half, i)
            u, inverse = unit_of(mt[r, :].astype(F32))
            dy = tmp[r, D : 2 * D]
            gz[r, :] = (tmp[r, 0:D] + norm_back(dy, u, inverse, gain[0])).astype(BF16)
            d_gain, d_shift = d_gain + col_sum(dy * u), d_shift + col_sum(dy)
        return d_gain, d_shift

    d_gain0, d_shift0 = norm1_back(1)
    g_htx[...] = halo_of(gz[band(1), :].astype(F32)).astype(BF16)
    grad_halo = send(g_htx, g_hrx, ID_PG, down_rank)
    grad_halo.start()
    more_gain, more_shift = norm1_back(0)
    d_gain0, d_shift0 = d_gain0 + more_gain, d_shift0 + more_shift
    back_sums(PEERS)

    merge_core = send(d_merge.at[pl.ds(2 - 2 * core, 2)], l1_m, ID_CORE_M, sibling)

    def merge_grad(k):
        lanes = pl.ds(pl.multiple_of(k * HALF, HALF), HALF)
        total = dot_tn(mn[...], gz[:, lanes]).astype(BF16)
        for i in range(2):
            d_merge[2 * k + i] = total[:, i * 128 : i * 128 + 128].reshape(CHUNKS, HALF, 128)

    merge_grad(1 - core)
    merge_core.start()
    merge_grad(core)
    small_early.sum(2)
    small_early.start(3)

    for d in (1, 2, 3):
        part = blk_rx.at[lax.rem(chan + CHUNKS - d, CHUNKS)]
        send(part, part, ID_BLK + d - 1, at_y(d)).wait_recv()
    blk_htx[...] = halo_of(blk_rx[PEERS, BAND:T, :].astype(F32)).astype(BF16)
    blk_halo = send(blk_htx, blk_hrx, ID_BLK_HALO, down_band)
    blk_halo.start()

    merge_core.wait_recv()
    for i in range(2):
        for c in range(CHUNKS):
            total = d_merge[2 * core + i, c].astype(F32) + l1_m[i, c].astype(F32)
            d_merge[2 * core + i, c] = total.astype(BF16)

    def merge_owner(d):
        return send(d_merge.at[group_a, lax.rem(chan + d, CHUNKS)], l2_m.at[d - 1], ID_Y_M + d - 1, at_y(d))

    for d in order:
        merge_owner(d).start()
    for c in range(CHUNKS):
        spread_m.first_start(c, c)

    grad_halo.wait_recv()
    gz[band(1), :] = with_halo(gz[band(1), :].astype(F32), g_hrx[...].astype(F32)).astype(BF16)
    sel_copies[1].wait()
    tmp[...] = dot_nt(gz[...], merge_w[...])
    d_gain_m, d_shift_m = 0.0, 0.0
    for half in range(2):
        for i in three:
            r = pair_rows(half, i)
            u = x0[r, :].astype(F32)
            dy = tmp[r, :]
            tmp[r, :] = norm_back(dy, u, inv[r, 0:1], repl[RP_GAIN0 : RP_GAIN0 + 1, :])
            d_gain_m, d_shift_m = d_gain_m + col_sum(dy * u), d_shift_m + col_sum(dy)

    def head_sums(c, _):
        total = jnp.zeros((1, 3 * CH), F32)
        for i in range(NPAIR):
            total += col_sum(dqkv[c, i * PAIR : i * PAIR + PAIR, :].astype(F32))
        d_small[c, SM_QV : SM_QV + 1, :] = total[:, 0:CH]
        d_small[c, SM_QV + 1 : SM_QV + 2, :] = total[:, 2 * CH : 3 * CH]
        half = WIN * SLOT
        both = r1[c * PAIR : c * PAIR + PAIR, :]
        for h in range(HEADS_C):
            lanes = slice(h * 128, h * 128 + 128)
            folded = both[0:half, lanes] + pltpu.roll(both[half:PAIR, lanes], 128 - half, 1)
            acc = jnp.zeros((SLOT, 128), F32)
            for a in range(WIN):
                slab = folded[a * SLOT : a * SLOT + SLOT]
                moved = (WIN - 1 - a) * SLOT
                acc += pltpu.roll(slab, moved, 1) if moved else slab
            lmat[h * SLOT : h * SLOT + SLOT, :] = acc
        d_table = jnp.zeros((SLOT, 256), F32)
        for b_q in range(WIN):
            rows = [lmat[h * SLOT + b_q : h * SLOT + b_q + 1, :] for h in range(HEADS_C)]
            rows = jnp.concatenate(rows + [jnp.zeros((SLOT - HEADS_C, 128), F32)], 0)
            d_table += dot_nt(rows.astype(BF16), table_sel[:, b_q * 128 : b_q * 128 + 128])
        d_small[c, SM_TABLE : SM_TABLE + 4, :] = d_table[0:4, 0:128]
        d_small[c, SM_TABLE + 4 : SM_TABLE + 8, :] = d_table[0:4, 128:256]
        return 0

    for c in range(CHUNKS):
        head_sums(c, 0)
    for c in range(CHUNKS):
        sl[0, EARLY * c : EARLY * c + EARLY, :] = d_small[c, 0:EARLY, :]
    lay(sl, SL_NORM, d_gain0)
    lay(sl, SL_NORM + 4, d_shift0)
    lay(sl, SL_MERGE, d_gain_m)
    lay(sl, SL_MERGE + 8, d_shift_m)
    small_late.start(0)
    plane_a.finish()
    spread_up.finish()
    core_out(0, gf_down.at[core]).start()
    core_out(1, gf_up.at[core]).start()
    small_early.sum(3)

    owner_wait(OUT)
    out_half = owner_sum(OUT, 0, 64)
    for g in range(4):
        gb[g * 64 : g * 64 + 64, 0:128] = out_half[:, g * 128 : g * 128 + 128]
    for d in order:
        merge_owner(d).wait_recv()
    total = d_merge[group_a, chan].astype(F32)
    for d in range(PEERS):
        total += l2_m[d].astype(F32)
    gb[:, 128:256] = total.astype(BF16)
    plane_b.start()
    spread_m.third_start(lambda c: c)
    spread_qkv.third_start(back_chunk)
    small_late.sum(0)
    small_late.start(1)

    def page_rows(i, _):
        base = (i // WIN) * BAND + lax.rem(i, WIN) * SLOT
        for q in range(2):
            parts = []
            for par in range(2):
                lanes = par * 512 + q * 256
                for wc in range(WC):
                    at = pl.multiple_of(base + wc * WIN * SLOT, SLOT)
                    parts.append(tmp[pl.ds(at, SLOT), lanes : lanes + 256])
            y = dot(pages_sel_t[...], jnp.concatenate(parts, 0).astype(BF16))
            pg[lax.rem(2 * i + q + LIFT, 2 * ROWS)] = y.astype(BF16)
        return 0

    lax.fori_loop(0, ROWS, page_rows, 0)
    pages_copy = local(pg, pages_o, 14)
    pages_copy.start()

    plane_b.back_start()
    spread_m.third_sum()
    for copy in spread_m.back_y(False):
        copy.start()
    spread_qkv.third_sum()
    spread_qkv.back_start()
    small_late.sum(1)
    small_late.start(2)

    blk_halo.wait_recv()
    outs = [local(blk_rx, block_o, 10), local(blk_hrx, block_halo_o, 9), local(se.at[4], early_o, 11)]
    core_out(0, gf_down.at[1 - core]).wait_recv()
    outs.append(local(gf_down, down_o, 12))
    core_out(1, gf_up.at[1 - core]).wait_recv()
    outs.append(local(gf_up, up_o, 13))
    for copy in outs:
        copy.start()

    plane_b.finish()
    gf_out[core] = gfb[core, :, 0:128]
    mf[group_a, chan] = gfb[core, :, 128:256]

    def merge_back(c, d):
        part = mf.at[group_a, c]
        return send(part, part, ID_BACK_Y + PEERS + d - 1, at_y(d))

    for d in order:
        merge_back(chan, d).start()
    core_out(3, gf_out.at[core]).start()
    for copy in spread_m.back_y(True):
        copy.wait_recv()
    spread_m.back_start()
    spread_qkv.finish()
    core_out(2, gf_qkv.at[core]).start()
    small_late.sum(2)
    small_late.start(3)
    late = [local(sl.at[4], late_o, 15)]
    core_out(2, gf_qkv.at[1 - core]).wait_recv()
    late.append(local(gf_qkv, qkv_o, 16))
    late[1].start()
    for d in order:
        merge_back(lax.rem(chan + CHUNKS - d, CHUNKS), d).wait_recv()
    core_out(4, mf.at[group_a]).start()
    spread_m.finish()
    core_out(5, mf.at[group_b]).start()
    core_out(3, gf_out.at[1 - core]).wait_recv()
    last = [local(gf_out, out_o, 17)]
    last[0].start()
    small_late.sum(3)
    late[0].start()
    for i in range(2):
        core_out(4 + i, mf.at[2 - 2 * core + i]).wait_recv()
    last.append(local(mf, merge_o, 18))
    last[1].start()

    for copy in [merged_halo, normed_halo, blk_halo, grad_halo, merge_core] + small_copies + blk_copies:
        copy.wait_send()
    for w in range(4):
        for copy in weight_copies[w]:
            copy.wait_send()
        for d in order:
            c = lax.rem(chan + CHUNKS - d, CHUNKS)
            if w in (QKV, OUT):
                copies = forward_copies(w, d, c)
            else:
                copies = [*around_copies(w, d, c), across_copy(w, d, c)]
            for copy in copies:
                copy.wait_send()
        for j in range(CHUNKS):
            core_copy(w, j, feed_chunk(j) if w in (UP, DOWN) else back_chunk(j)).wait_send()
    for d in order:
        owner_copy(DOWN, d).wait_send()
        owner_copy(OUT, d).wait_send()
        merge_owner(d).wait_send()
        merge_back(chan, d).wait_send()
    plane_a.left()
    plane_b.left()
    spread_up.left(feed_chunk)
    spread_qkv.left(back_chunk)
    spread_m.left(lambda c: c)
    for copy in spread_m.back_y(False):
        copy.wait_send()
    for group in (small_early, small_late):
        for level in range(4):
            for copy in group.copies(level):
                copy.wait_send()
    parts = (gf_down.at[core], gf_up.at[core], gf_qkv.at[core], gf_out.at[core], mf.at[group_a], mf.at[group_b])
    for n, part in enumerate(parts):
        core_out(n, part).wait_send()
    for copy in outs + late + last + [pages_copy]:
        copy.wait()


def kernel_call(args):
    hbm = pl.BlockSpec(memory_space=pl.ANY)
    s = jax.ShapeDtypeStruct
    outs = [
        s((CHUNKS, T, CH), BF16),
        s((WC * SHIFT * SLOT, CH), BF16),
        s((2 * ROWS, 2 * COLS, 256), BF16),
        s((2, HALF, D), BF16),
        s((2, HALF, 512), BF16),
        s((2, HALF, 3 * CH), BF16),
        s((2, HALF, 128), BF16),
        s((CHUNKS, CHUNKS, HALF, 128), BF16),
        s((SE_ROWS, 128), F32),
        s((SL_ROWS, 128), F32),
    ]

    def v(shape, dtype):
        return pltpu.VMEM(shape, dtype)

    scratch = [
        *[v(a.shape, BF16) for a in args[7:20]], v((8, 1024), F32),
        v((2 * ROWS, 2 * COLS, 256), BF16), *[v((WC * SHIFT * SLOT, D), BF16)] * 4, *[v((WC * SHIFT * SLOT, 2 * D), BF16)] * 2, v((COLS, 4 * ROWS, CH), BF16), v((CHUNKS, T, CH), BF16),
        v((WC * SHIFT * SLOT, CH), F32), v((WC * SHIFT * SLOT, CH), BF16), v((WC * SHIFT * SLOT, CH), BF16),
        v((1024, D), BF16), v((CHUNKS, 3, D, CH), BF16), v((CHUNKS, CH, D), BF16),
        v((CHUNKS, 4, 2, 64, 512), BF16), v((CHUNKS, 4, 2, 64, D), BF16), v((CHUNKS, 16, 128), F32),
        v((T, 1024), BF16), v((T, 2), F32), v((T, 1024), BF16), v((T, D), BF16), v((T, D), BF16),
        v((CHUNKS, T, 3 * CH), BF16), v((CHUNKS, NPAIR, PAIR, 512), BF16), v((T, D), BF16), v((CHUNKS, T, CH), F32),
        v((T, D), F32), v((T, D), BF16), v((T, D), BF16), v((T, D), BF16),
        v((T, 512), BF16), v((T, 512), BF16),
        v((4, CHUNKS, 512, 128), BF16), v((512, CH), BF16), v((PAIR, 128), BF16), v((HEADS_C * SLOT, 128), F32),
        v((CHUNKS, T, 3 * CH), BF16), v((T, D), BF16), v((T, D), BF16), v((T, 1024), F32),
        v((CHUNKS, T, CH), BF16), v((WC * SHIFT * SLOT, CH), BF16), v((WC * SHIFT * SLOT, CH), BF16),
        v((2 * ROWS, 2 * COLS, 256), BF16),
        v((CHUNKS, CHUNKS, HALF, 128), BF16), v((CHUNKS, D, 3 * CH), BF16), v((CHUNKS, CH, D), BF16),
        v((CHUNKS, D, 512), BF16), v((CHUNKS, 512, D), BF16), v((CHUNKS, 16, 128), F32),
        v((CHUNKS, HALF, 3 * CH), BF16), v((CHUNKS, CH // 2, D), BF16), v((CHUNKS, HALF, 512), BF16),
        v((CHUNKS, HALF, D), BF16), v((2, CHUNKS, HALF, 128), BF16),
        v((PEERS, CH // 2, D), BF16), v((PEERS, HALF, D), BF16), v((PEERS, HALF, 128), BF16),
    ]
    for lanes in (512, 384, 128):
        scratch += [v((CHUNKS, PLANE, 16, lanes), BF16), v((CHUNKS, 16, lanes), BF16), v((PEERS, 16, lanes), BF16)]
    for lanes in (512, 256):
        scratch += [v((HALF, lanes), BF16), v((PLANE, 16, lanes), BF16), v((2, HALF, lanes), BF16)]
    scratch += [v((2, HALF, 512), BF16), v((2, HALF, 384), BF16), v((2, HALF, 128), BF16), v((CHUNKS, CHUNKS, HALF, 128), BF16)]
    for rows in (SE_ROWS, SL_ROWS):
        scratch += [v((5, rows, 128), F32), v((1, rows, 128), F32)] + [v((PEERS, rows, 128), F32)] * 3
    scratch += [
        pltpu.SemaphoreType.DMA((IDS.count,)),
        pltpu.SemaphoreType.DMA((IDS.count,)),
        pltpu.SemaphoreType.DMA((LOCAL,)),
    ]
    return pl.pallas_call(
        compute,
        out_shape=outs,
        in_specs=[hbm] * len(args),
        out_specs=[hbm] * len(outs),
        scratch_shapes=scratch,
        compiler_params=pltpu.CompilerParams(
            vmem_limit_bytes=63 * 1024 * 1024, collective_id=0, has_side_effects=True
        ),
    )(*args)


def finish(
    block, pages, down, up, qkv, out, merge, block_halo, early, late,
    block_o, pages_o, gain_m_o, shift_m_o, merge_o, gain_o, shift_o, qkv_o, qv_o, table_o, out_o, out_b_o, up_o, up_b_o,
    down_o, down_b_o, rms_o,
    block_i, pages_i, down_i, up_i, qkv_i, out_i, merge_i, block_f, pages_f, down_f, up_f, qkv_f, out_f, merge_f, slots_f, halo_f, isem, osem,
):
    chan = lax.axis_index("chan")
    ins = (down, up, qkv, merge, pages, block, out)
    bufs = (down_i, up_i, qkv_i, merge_i, pages_i, block_i, out_i)
    copies = [pltpu.make_async_copy(a, b, isem.at[i]) for i, (a, b) in enumerate(zip(ins, bufs))]
    for copy in copies:
        copy.start()

    def early_row(i):
        return early[pl.ds(chan * 6 + i - EARLY, 1), :]

    def late_row(i):
        return late[pl.ds(chan * EARLY + i, 1), :]

    def joined(ref, at, n):
        return jnp.concatenate([ref[at + i : at + i + 1, :] for i in range(n)], 1)

    gain_m_o[...] = late[SL_MERGE : SL_MERGE + 8, :]
    shift_m_o[...] = late[SL_MERGE + 8 : SL_MERGE + 16, :]
    gain_o[...] = jnp.concatenate([joined(late, SL_NORM, 4), joined(early, SE_NORM, 4)], 0)
    shift_o[...] = jnp.concatenate([joined(late, SL_NORM + 4, 4), joined(early, SE_NORM + 4, 4)], 0)
    qv_o[...] = jnp.concatenate([late_row(SM_QV), late_row(SM_QV + 1)], 0)
    for h in range(HEADS_C):
        table_o[h : h + 1, 0:128] = late_row(SM_TABLE + h)
        table_o[h : h + 1, 128:169] = late_row(SM_TABLE + HEADS_C + h)[:, 0:41]
    out_b_o[...] = early_row(SM_OUT_B)
    for i in range(4):
        up_b_o[i : i + 1, :] = early_row(SM_UP_B + i)
    down_b_o[...] = early_row(SM_DOWN_B)
    sums = jnp.sum(early[SE_SQ : SE_SQ + 8, :], 1, keepdims=True)
    roots = jnp.sqrt(sums * (1.0 / (1792 * COLS * D)))
    for i in range(3):
        rms_o[i] = roots[i, 0]

    outs = (down_o, up_o, qkv_o, merge_o, pages_o, block_o, out_o)
    stages = (down_f, up_f, qkv_f, merge_f, pages_f, block_f, out_f)
    done = [pltpu.make_async_copy(a, b, osem.at[i]) for i, (a, b) in enumerate(zip(stages, outs))]

    for n, (i, f) in enumerate(((down_i, down_f), (up_i, up_f))):
        copies[n].wait()
        f[...] = i[...].astype(F32)
        done[n].start()
    copies[2].wait()
    for i in range(3):
        qkv_f[i] = qkv_i[:, i * CH : i * CH + CH].astype(F32)
    done[2].start()
    copies[3].wait()
    for i in range(CHUNKS):
        merge_f[:, i * 128 : i * 128 + 128] = merge_i[i].astype(F32)
    done[3].start()
    copies[4].wait()

    def page(i, _):
        pages_f[i] = pages_i[i].astype(F32)
        return 0

    lax.fori_loop(0, 2 * ROWS, page, 0)
    done[4].start()
    copies[5].wait()
    slots_f[...] = block_i[...].astype(F32)
    halo_f[...] = block_halo[...].astype(F32)
    for wc in range(WC):
        for b in range(WIN):
            j = (wc * WIN + b + SHIFT) % COLS
            block_f[j, 0:SHIFT, :] = halo_f[pl.ds(wc * SHIFT * SLOT + b, SHIFT, stride=SLOT), :]
            for m in range(4 * ROWS // WIN):
                c, wr = m // 2, m % 2
                n = WIN - SHIFT if m == 4 * ROWS // WIN - 1 else WIN
                slot = wr * BAND + wc * WIN * SLOT + b
                block_f[j, SHIFT + WIN * m : SHIFT + WIN * m + n, :] = slots_f[c, pl.ds(slot, n, stride=SLOT), :]
    done[5].start()
    copies[6].wait()
    for k in range(2):
        for g in range(4):
            out_f[k * 64 : k * 64 + 64, g * 128 : g * 128 + 128] = out_i[k, g * 64 : g * 64 + 64, :].astype(F32)
    done[6].start()
    for copy in done:
        copy.wait()


def finish_call(parts):
    block, block_halo, pages, down, up, qkv, out, merge, early, late = parts
    vm = pl.BlockSpec(memory_space=pltpu.VMEM)
    hbm = pl.BlockSpec(memory_space=pl.ANY)

    def s(*shape):
        return jax.ShapeDtypeStruct(shape, F32)

    big = {
        "block": s(COLS, 4 * ROWS, CH), "pages": s(2 * ROWS, 2 * COLS, 256), "merge": s(1024, D),
        "qkv": s(3, D, CH), "out": s(CH, D), "up": s(D, 512), "down": s(512, D),
    }
    shapes = [
        big["block"], big["pages"], s(8, 128), s(8, 128), big["merge"], s(2, D), s(2, D), big["qkv"], s(2, CH), s(HEADS_C, 169),
        big["out"], s(1, 128), big["up"], s(4, 128), big["down"], s(1, 128), s(3),
    ]
    large = [any(shape is b for b in big.values()) for shape in shapes]
    ins = [block, pages, down.reshape(512, D), up.reshape(D, 512), qkv.reshape(D, 3 * CH), out, merge.reshape(CHUNKS, 1024, 128)]
    results = pl.pallas_call(
        finish,
        out_shape=shapes,
        in_specs=[hbm] * 7 + [vm] * 3,
        out_specs=[hbm if b else vm for b in large[:-1]] + [pl.BlockSpec(memory_space=pltpu.SMEM)],
        scratch_shapes=[pltpu.VMEM(a.shape, BF16) for a in ins]
        + [pltpu.VMEM(big[n].shape, F32) for n in ("block", "pages", "down", "up", "qkv", "out", "merge")]
        + [pltpu.VMEM(block.shape, F32), pltpu.VMEM(block_halo.shape, F32)]
        + [pltpu.SemaphoreType.DMA((7,)), pltpu.SemaphoreType.DMA((7,))],
        compiler_params=pltpu.CompilerParams(vmem_limit_bytes=63 * 1024 * 1024),
    )(*ins, block_halo, early, late)
    r = list(results)
    r[0] = r[0].transpose(1, 0, 2)
    r[2], r[3] = r[2].reshape(1024), r[3].reshape(1024)
    r[7] = r[7].transpose(1, 0, 2)
    r[11], r[13], r[15] = r[11].reshape(CH), r[13].reshape(512), r[15].reshape(CH)
    return tuple(r)


def body(
    pages, merge_gain, merge_shift, merge_weight, norm_gain, norm_shift, qkv_weight, qv_bias, rel_table,
    out_weight, out_bias, up_weight, up_bias, down_weight, down_bias, cotangent,
):
    args = [
        pages, cotangent.transpose(1, 0, 2), merge_weight, qkv_weight.transpose(1, 0, 2), out_weight, up_weight, down_weight,
        qv_bias, rel_table, out_bias, up_bias, down_bias, merge_gain, merge_shift, norm_gain, norm_shift, *constants(),
    ]
    return finish_call(kernel_call(args))


def solution(mesh):
    placed = (
        P(("space", "chan"), None, None), P(), P(), P(), P(), P(), P(None, None, "chan"), P(None, "chan"),
        P("chan", None), P("chan", None), P("chan"), P(None, "chan"), P("chan"), P("chan", None), P("chan"),
        P("space", None, "chan"),
    )
    outs = (
        P("space", None, "chan"), P(("space", "chan"), None, None), P(), P(), P(), P(), P(),
        P(None, None, "chan"), P(None, "chan"), P("chan", None), P("chan", None), P("chan"),
        P(None, "chan"), P("chan"), P("chan", None), P("chan"), P(),
    )
    return jax.shard_map(body, mesh=mesh, in_specs=placed, out_specs=outs, check_vma=False)
```

```python
import functools

import jax
import jax.numpy as jnp
import numpy as np
from jax import lax
from jax.experimental import pallas as pl
from jax.experimental.pallas import tpu as pltpu
from jax.sharding import PartitionSpec as P

D = 512
HEADS = 16
HD = 32
FF = 2048
WIN = 7
SHIFT = 3
COLS = 42
ROWS = 14
WC = COLS // WIN
SLOT = 8
PAIR = 2 * WIN * SLOT
NPAIR = WC
T = PAIR * NPAIR
BAND = WC * WIN * SLOT
CHUNKS = 4
CH = D // CHUNKS
HEADS_C = HEADS // CHUNKS
LIFT = 2 * SHIFT
EPS = 1e-05
MASKED = -1e9
SCALE = HD ** (-0.5)
F32 = jnp.float32
BF16 = jnp.bfloat16


def dot(a, b):
    return jnp.dot(a, b, preferred_element_type=F32)


def dot_nt(a, b):
    return lax.dot_general(a, b, (((1,), (1,)), ((), ())), preferred_element_type=F32)


def dot_tn(a, b):
    return lax.dot_general(a, b, (((0,), (0,)), ((), ())), preferred_element_type=F32)


def constants():
    slots = np.arange(WC * SLOT)
    column = slots // SLOT * WIN + slots % SLOT
    real = slots % SLOT < WIN
    pages_sel = np.zeros((2, WC * SLOT, 2 * COLS), np.float32)
    for parity in range(2):
        source = (2 * column + parity + LIFT) % (2 * COLS)
        pages_sel[parity, slots[real], source[real]] = 1
    pages_sel = pages_sel.reshape(2 * WC * SLOT, 2 * COLS)
    table_sel = np.zeros((256, SLOT, 128), np.float32)
    for b_q in range(WIN):
        for i in range(2 * WIN - 1):
            for b_k in range(WIN):
                code = (12 - i) * 13 + b_q - b_k + 6
                table_sel[code, b_q, i * SLOT + b_k] = 1
    table_sel = table_sel.reshape(256, SLOT * 128)
    table_sel_t = np.zeros((256, SLOT, 128), np.float32)
    for b_k in range(WIN):
        for i in range(2 * WIN - 1):
            for b_q in range(WIN):
                table_sel_t[i * 13 + b_q - b_k + 6, b_k, i * SLOT + b_q] = 1
    table_sel_t = table_sel_t.reshape(256, SLOT * 128)
    arrays = (pages_sel, pages_sel.T, table_sel, table_sel_t)
    return [jnp.asarray(a, BF16) for a in arrays]


def iota(shape, dim):
    return lax.broadcasted_iota(jnp.int32, shape, dim)


def gelu_parts(x):
    z = jnp.abs(x) * (0.5**0.5)
    t = 1.0 / (1.0 + 0.3275911 * z)
    e = jnp.exp(-z * z)
    poly = t * (0.254829592 + t * (-0.284496736 + t * (1.421413741 + t * (-1.453152027 + t * 1.061405429))))
    tail = 0.5 * poly * e
    cdf = jnp.where(x >= 0, 1.0 - tail, tail)
    return x * cdf, cdf + x * e * 0.3989422804014327


def unit_of(x):
    centered = x - jnp.mean(x, -1, keepdims=True)
    inverse = lax.rsqrt(jnp.mean(centered * centered, -1, keepdims=True) + EPS)
    return centered * inverse, inverse


def norm_back(dy, u, inverse, gain):
    scaled = dy * gain
    first = jnp.mean(scaled, -1, keepdims=True)
    second = jnp.mean(scaled * u, -1, keepdims=True)
    return inverse * (scaled - first - u * second)


def col_sum(x):
    return jnp.sum(x, 0, keepdims=True)


def pair_mask(row_cut, col_cut):
    k, q = iota((128, 128), 0), iota((128, 128), 1)
    half = PAIR // 2
    win_q, win_k = q // half, k // half
    a_q, a_k = (q % half) // SLOT, (k % half) // SLOT
    b_q, b_k = q % SLOT, k % SLOT
    ok = (win_q == win_k) & (k < PAIR) & (b_k < WIN)
    cut = WIN - SHIFT
    if row_cut:
        ok &= (a_q < cut) == (a_k < cut)
    if col_cut:
        ok &= ((b_q < cut) == (b_k < cut)) | (win_q == 0)
    return jnp.where(ok, 0.0, MASKED)


def head_lanes(x, h):
    lane = iota((1, CH), 1)
    return jnp.where(lane // HD == h, x, jnp.zeros_like(x))


def spread(x):
    padded = jnp.concatenate([x, jnp.zeros((128 - PAIR, CH), x.dtype)], 0)
    return jnp.concatenate([head_lanes(padded, h) for h in range(HEADS_C)], 0)


def stacked(x):
    return jnp.concatenate([head_lanes(x, h) for h in range(HEADS_C)], 0)


def by_head(x):
    return jnp.concatenate([x[:, 128 * h : 128 * h + 128] for h in range(HEADS_C)], 0)


def rows_of(p, count=PAIR):
    return pl.ds(pl.multiple_of(p * count, 16), count)


SM_QV, SM_TABLE, SM_OUT_B, SM_UP_B, SM_DOWN_B = 0, 2, 10, 11, 15
RP_GAIN0, RP_SHIFT0, RP_GAIN, RP_SHIFT = 0, 1, 2, 4


def row_of(ref, c, first, count):
    return jnp.concatenate([ref[c, first + i : first + i + 1, :] for i in range(count)], 1)


MESH = pl.DeviceIdType.MESH
HALF = 256
PEERS = CHUNKS - 1
PLANE = 15


class Sems:
    def __init__(self):
        self.count = 0

    def take(self, n):
        self.count += n
        return self.count - n


IDS = Sems()
ID_PAGES = IDS.take(1)
ID_SMALL = IDS.take(PEERS)
ID_W = IDS.take(4 * PEERS)
ID_WF = IDS.take(4 * PEERS)
ID_WN = IDS.take(4 * PEERS * 4)
ID_COT_HALO = IDS.take(1)
ID_COT = IDS.take(PEERS)
ID_BLK = IDS.take(PEERS)
ID_BLK_HALO = IDS.take(1)
ID_CORE = IDS.take(4 * CHUNKS)
ID_CORE_M = IDS.take(2)
ID_Y = IDS.take(2 * PEERS)
ID_Y_M = IDS.take(PEERS)
ID_FIRST = IDS.take(3 * CHUNKS * PLANE)
ID_THIRD = IDS.take(3 * PEERS)
ID_BACK_Y = IDS.take(2 * PEERS)
ID_BACK = IDS.take(3 * PLANE)
ID_A = IDS.take(2 * 2 * PLANE)
ID_GC = IDS.take(6)
ID_PG = IDS.take(1)
ID_MN = IDS.take(1)
ID_SG = IDS.take(2 * (1 + 3 * PEERS))
LOCAL = 56
UNROLL = 3
QKV, OUT, UP, DOWN = 0, 1, 2, 3

EARLY = 10
SE_NORM, SE_SQ, SE_ROWS = CHUNKS * (16 - EARLY), CHUNKS * (16 - EARLY) + 8, 40
SL_NORM, SL_MERGE, SL_ROWS = CHUNKS * EARLY, CHUNKS * EARLY + 8, 64


def chunk_off(j):
    return lax.rem(3 * j, 5) - 2 * (j // 3)


def feed_off(j):
    return lax.rem(CHUNKS - j, CHUNKS)


def back_off(j):
    return lax.rem(j + 1, CHUNKS)


def compute(
    pages_in, cot_in, merge_in, qkv_in, out_in, up_in, down_in,
    qv_in, table_in, out_b_in, up_b_in, down_b_in, gain_m_in, shift_m_in, gain_in, shift_in,
    pages_sel_in, pages_sel_t_in, table_sel_in, table_sel_t_in,
    block_o, block_halo_o, pages_o, down_o, up_o, qkv_o, out_o, merge_o, early_o, late_o,
    qv_v, table_v, out_b_v, up_b_v, down_b_v, gain_m_v, shift_m_v, gain_v, shift_v,
    pages_sel, pages_sel_t, table_sel, table_sel_t, repl,
    pages, m_htx, m_hrx, g_htx, g_hrx, mn_htx, mn_hrx, cot_v, cot_tx, cot_hf, cot_htx, cot_hrx, merge_w, qkv_w, out_w, up_w, down_w, small,
    x0, inv, mn, mt, n1, qkv, prob, att, norm, r1, u2, n2, g2,
    hid, dpre, bias, ones, unit, lmat, dqkv, g1, gz, tmp,
    blk_rx, blk_htx, blk_hrx, pg,
    d_merge, d_qkv, d_out, d_up, d_down, d_small,
    l1_qkv, l1_out, l1_up, l1_down, l1_m, l2_out, l2_down, l2_m,
    up_1, up_h, up_3, qkv_1, qkv_h, qkv_3, mb_1, mb_h, mb_3,
    ga, rxa, gf_down, gb, rxb, gfb, gf_up, gf_qkv, gf_out, mf,
    se, se_c, se_y, se_z, se_x, sl, sl_c, sl_y, sl_z, sl_x,
    ssem, rsem, lsem,
):
    chan = lax.axis_index("chan")
    space = lax.axis_index("space")
    n_space = lax.axis_size("space")
    core = lax.rem(space, 2)
    z = lax.rem(space // 2, 4)
    x = space // 8
    last_chan = chan == CHUNKS - 1
    valid = (iota((PAIR, 1), 0) % SLOT < WIN).astype(F32)

    def at_y(d):
        return (space, lax.rem(chan + d, CHUNKS))

    def at_z(d):
        return (x * 8 + lax.rem(z + d, 4) * 2 + core, chan)

    def at_x(d):
        return (lax.rem(x + d, 4) * 8 + z * 2 + core, chan)

    def at_plane(m):
        return (lax.rem(x + m // 4, 4) * 8 + lax.rem(z + m % 4, 4) * 2 + core, chan)

    def place_of(m):
        return lax.rem(x + m // 4, 4) * 4 + lax.rem(z + m % 4, 4)

    def place_before(m):
        return lax.rem(x + 4 - m // 4, 4) * 4 + lax.rem(z + 4 - m % 4, 4)

    sibling = (x * 8 + z * 2 + 1 - core, chan)
    up_band = (lax.rem(space + n_space - 1, n_space), chan)
    down_band = (lax.rem(space + 1, n_space), chan)
    rank = space * CHUNKS + chan
    n_rank = n_space * CHUNKS
    before = lax.rem(rank + n_rank - 1, n_rank)
    after = lax.rem(rank + 1, n_rank)
    up_rank = (before // CHUNKS, lax.rem(before, CHUNKS))
    down_rank = (after // CHUNKS, lax.rem(after, CHUNKS))

    def send(src, dst, n, device, into=None):
        return pltpu.make_async_remote_copy(
            src_ref=src, dst_ref=dst, send_sem=ssem.at[n], recv_sem=rsem.at[n if into is None else into],
            device_id=device, device_id_type=MESH,
        )

    def local(src, dst, n):
        return pltpu.make_async_copy(src, dst, lsem.at[n])

    own_pages = local(pages_in, pages, 0)
    own_merge = local(merge_in, merge_w, 1)
    own_w = [
        local(src, dst.at[chan], 2 + i)
        for i, (src, dst) in enumerate(((qkv_in, qkv_w), (out_in, out_w)))
    ]
    own_mlp = [
        local(src.at[pl.ds(64 * i, 64)], dst.at[chan, i // 2, i % 2], 40 + 8 * n + i)
        for n, (src, dst) in enumerate(((up_in, up_w), (down_in, down_w)))
        for i in range(8)
    ]
    own_cot = local(cot_in, cot_v, 6)
    tiny = (qv_in, table_in, out_b_in, up_b_in, down_b_in, gain_m_in, shift_m_in, gain_in, shift_in)
    tiny_v = (qv_v, table_v, out_b_v, up_b_v, down_b_v, gain_m_v, shift_m_v, gain_v, shift_v)
    tiny_copies = [local(src, dst, 24 + i) for i, (src, dst) in enumerate(zip(tiny, tiny_v))]
    tables_in = (pages_sel_in, pages_sel_t_in, table_sel_in, table_sel_t_in)
    sel_copies = [
        local(src, dst, 33 + i) for i, (src, dst) in enumerate(zip(tables_in, (pages_sel, pages_sel_t, table_sel, table_sel_t)))
    ]
    for copy in tiny_copies + sel_copies[0:1] + [own_pages, own_cot, own_merge, sel_copies[3], own_w[QKV]]:
        copy.start()
    for copy in [own_w[OUT]] + own_mlp + [sel_copies[1], sel_copies[2]]:
        copy.start()

    barrier = pltpu.get_barrier_semaphore()
    greeted = [at_y(d) for d in (1, 2, 3)] + [at_plane(m) for m in range(1, PLANE + 1)]
    greeted += [sibling, up_band, down_band, up_rank, down_rank]
    for by in (1, 3):
        greeted.append((lax.rem(x + by, 4) * 8 + z * 2 + 1 - core, chan))
        greeted.append((x * 8 + lax.rem(z + by, 4) * 2 + 1 - core, chan))
    for device in greeted:
        pl.semaphore_signal(barrier, inc=1, device_id=device, device_id_type=MESH)

    for copy in tiny_copies:
        copy.wait()
    lane_rows = lambda ref, n: ref[...].astype(F32).reshape(1, n)
    small[chan, SM_QV : SM_QV + 2, :] = qv_v[...].astype(F32)
    table = table_v[...].astype(F32)
    small[chan, SM_TABLE : SM_TABLE + 4, :] = table[:, 0:128]
    small[chan, SM_TABLE + 4 : SM_TABLE + 8, :] = jnp.concatenate([table[:, 128:169], jnp.zeros((4, 87), F32)], 1)
    small[chan, SM_OUT_B : SM_OUT_B + 1, :] = lane_rows(out_b_v, 128)
    up_row = lane_rows(up_b_v, 512)
    for i in range(4):
        small[chan, SM_UP_B + i : SM_UP_B + i + 1, :] = up_row[:, i * 128 : i * 128 + 128]
    small[chan, SM_DOWN_B : SM_DOWN_B + 1, :] = lane_rows(down_b_v, 128)
    repl[RP_GAIN0 : RP_GAIN0 + 1, :] = lane_rows(gain_m_v, 1024)
    repl[RP_SHIFT0 : RP_SHIFT0 + 1, :] = lane_rows(shift_m_v, 1024)
    repl[RP_GAIN : RP_GAIN + 2, 0:D] = gain_v[...].astype(F32)
    repl[RP_SHIFT : RP_SHIFT + 2, 0:D] = shift_v[...].astype(F32)
    pl.semaphore_wait(barrier, len(greeted))

    halves = (HALF, CH // 2, HALF, HALF)
    weights = (qkv_w, out_w, up_w, down_w)
    sources = (qkv_in, out_in, up_in, down_in)

    def axis_of(w):
        return (x, lambda d, k: (lax.rem(x + d, 4) * 8 + z * 2 + k, chan)) if w in (QKV, UP) else (
            z, lambda d, k: (x * 8 + lax.rem(z + d, 4) * 2 + k, chan)
        )

    def rows_in(ref, w, first, n, c=None):
        rows = pl.ds(pl.multiple_of(first, 16), n)
        if c is None:
            return ref.at[:, rows] if w == QKV else ref.at[rows]
        return ref.at[c, :, rows] if w == QKV else ref.at[c, rows]

    def quarter(w, k):
        return lax.rem(axis_of(w)[0], 2) * halves[w] + k * (halves[w] // 2)

    def weight_copy(w, d):
        n = halves[w] // 2
        src = rows_in(sources[w], w, quarter(w, core), n)
        return send(src, rows_in(weights[w], w, quarter(w, core), n, chan), ID_W + w * PEERS + d - 1, at_y(d))

    def arrived(w, d, c):
        part = rows_in(weights[w], w, quarter(w, core), halves[w] // 2, c)
        send(part, part, ID_W + w * PEERS + d - 1, at_y(d)).wait_recv()

    def forward_copies(w, d, c):
        part = rows_in(weights[w], w, quarter(w, core), halves[w] // 2, c)
        yield send(part, part, ID_WF + w * PEERS + d - 1, sibling)
        n = halves[w] // 4
        base = ID_WN + (w * PEERS + d - 1) * 4
        for i, by in enumerate((1, 3)):
            part = rows_in(weights[w], w, quarter(w, core) + i * n, n, c)
            for same in range(2):
                device = axis_of(w)[1](by, core if same else 1 - core)
                yield send(part, part, base + i * 2 + same, device, base + i * 2 + core)

    def forwarded(w, d, c):
        part = rows_in(weights[w], w, quarter(w, 1 - core), halves[w] // 2, c)
        send(part, part, ID_WF + w * PEERS + d - 1, sibling).wait_recv()
        n = halves[w] // 4
        base = ID_WN + (w * PEERS + d - 1) * 4
        half = (1 - lax.rem(axis_of(w)[0], 2)) * halves[w]
        for i in range(2):
            for k in range(2):
                part = rows_in(weights[w], w, half + (k * 2 + i) * n, n, c)
                send(part, part, base + i * 2 + k, sibling).wait_recv()

    fourth = lax.rem(x + 2 * z, 4)

    def eighth_copy(w, d):
        part = weights[w].at[chan, fourth, core]
        src = sources[w].at[pl.ds(pl.multiple_of(fourth * 128 + core * 64, 64), 64)]
        return send(src, part, ID_W + w * PEERS + d - 1, at_y(d))

    def around_copies(w, d, c):
        part = weights[w].at[c, fourth, core]
        base = ID_WN + (w * PEERS + d - 1) * 4
        yield send(part, part, base, at_x(1))
        yield send(part, part, base + 1, at_x(3))
        for i, by in enumerate((1, 3)):
            half = part.at[pl.ds(32 * i, 32)]
            yield send(half, half, base + 2 + i, at_z(by))

    def across_copy(w, d, c):
        part = weights[w].at[c, :, core]
        return send(part, part, ID_WF + w * PEERS + d - 1, sibling)

    def chunk_peer(j):
        off = feed_off(j)
        return CHUNKS - off, lax.rem(chan + off, CHUNKS)

    def pass_around(w, j):
        d, c = chunk_peer(j)
        part = weights[w].at[c, fourth, core]
        send(part, part, ID_W + w * PEERS + d - 1, at_y(d)).wait_recv()
        for copy in around_copies(w, d, c):
            copy.start()

    def pass_across(w, j):
        d, c = chunk_peer(j)
        base = ID_WN + (w * PEERS + d - 1) * 4
        for i, by in enumerate((3, 1)):
            part = weights[w].at[c, lax.rem(fourth + by, 4), core]
            send(part, part, base + i, sibling).wait_recv()
        for i in range(2):
            part = weights[w].at[c, lax.rem(fourth + 2, 4), core, pl.ds(32 * i, 32)]
            send(part, part, base + 2 + i, sibling).wait_recv()
        across_copy(w, d, c).start()

    def have_across(w, j):
        d, c = chunk_peer(j)
        part = weights[w].at[c, :, 1 - core]
        send(part, part, ID_WF + w * PEERS + d - 1, sibling).wait_recv()

    def pass_on(w, j):
        off = chunk_off(j)
        c, d = lax.rem(chan + off, CHUNKS), CHUNKS - off
        arrived(w, d, c)
        for copy in forward_copies(w, d, c):
            copy.start()

    def have(w, j):
        off = chunk_off(j)
        forwarded(w, CHUNKS - off, lax.rem(chan + off, CHUNKS))

    small_copies = [send(small.at[chan], small.at[chan], ID_SMALL + d - 1, at_y(d)) for d in (1, 3, 2)]
    weight_copies = [[(weight_copy if w in (QKV, OUT) else eighth_copy)(w, d) for d in (1, 3, 2)] for w in range(4)]
    for copy in small_copies + weight_copies[QKV][0:2]:
        copy.start()

    def quads(i, _):
        base = (i // WIN) * BAND + lax.rem(i, WIN) * SLOT
        for q in range(2):
            y = dot(pages_sel[...], pages[lax.rem(2 * i + q + LIFT, 2 * ROWS)])
            for par in range(2):
                for wc in range(WC):
                    lanes = par * 512 + q * 256
                    at = pl.multiple_of(base + wc * WIN * SLOT, SLOT)
                    first = par * WC * SLOT + wc * SLOT
                    tmp[pl.ds(at, SLOT), lanes : lanes + 256] = y[first : first + SLOT]
        return 0

    own_pages.wait()
    sel_copies[0].wait()
    gain = [repl[RP_GAIN + i : RP_GAIN + i + 1, 0:D] for i in range(2)]
    shift = [repl[RP_SHIFT + i : RP_SHIFT + i + 1, 0:D] for i in range(2)]
    three = range(NPAIR // 2)
    cut_rows = WIN - SHIFT
    n_halo = SHIFT * SLOT

    def pair_rows(half, i):
        return slice(half * BAND + i * PAIR, half * BAND + i * PAIR + PAIR)

    def band(half):
        return slice(half * BAND, half * BAND + BAND)

    def merge_rows(half):
        lax.fori_loop(half * WIN, half * WIN + WIN, quads, 0)
        for i in three:
            r = pair_rows(half, i)
            u, inverse = unit_of(tmp[r, :])
            x0[r, :] = u.astype(BF16)
            inv[r, 0:1] = inverse
            mn[r, :] = (u * repl[RP_GAIN0 : RP_GAIN0 + 1, :] + repl[RP_SHIFT0 : RP_SHIFT0 + 1, :]).astype(BF16)
        return dot(mn[band(half), :], merge_w[...])

    def norm1(half):
        for i in three:
            r = pair_rows(half, i)
            u, _inverse = unit_of(mt[r, :].astype(F32))
            n1[r, :] = (u * gain[0] + shift[0]).astype(BF16)

    def halo_of(rows):
        starts = [wc * WIN * SLOT + cut_rows * SLOT for wc in range(WC)]
        return jnp.concatenate([rows[at : at + n_halo] for at in starts], 0)

    def with_halo(rows, halo):
        parts = []
        for wc in range(WC):
            at = wc * WIN * SLOT
            parts += [rows[at : at + cut_rows * SLOT], halo[wc * n_halo : wc * n_halo + n_halo]]
        return jnp.concatenate(parts, 0)

    own_merge.wait()
    merged_last = merge_rows(1)
    mt[band(1), :] = merged_last.astype(BF16)
    m_htx[...] = halo_of(merged_last).astype(BF16)
    merged_halo = send(m_htx, m_hrx, ID_PAGES, up_rank)
    merged_halo.start()
    for copy in weight_copies[QKV][2:] + weight_copies[OUT]:
        copy.start()
    for i in (0, 2, 1):
        for w in (UP, DOWN):
            weight_copies[w][i].start()
    mt[band(0), :] = merge_rows(0).astype(BF16)
    norm1(0)

    own_cot.wait()
    norm[...] = jnp.zeros_like(norm)
    cot_hf[...] = jnp.zeros_like(cot_hf)
    for wc in range(WC):
        for b in range(WIN):
            column = cot_v[(wc * WIN + b + SHIFT) % COLS].astype(F32)
            cot_hf[pl.ds(wc * SHIFT * SLOT + b, SHIFT, stride=SLOT), :] = column[0:SHIFT]
            for m in range(4 * ROWS // WIN):
                c, wr = m // 2, m % 2
                n = cut_rows if m == 4 * ROWS // WIN - 1 else WIN
                slot = wr * BAND + wc * WIN * SLOT + b
                norm[c, pl.ds(slot, n, stride=SLOT), :] = column[SHIFT + WIN * m : SHIFT + WIN * m + n]
    cot_htx[...] = cot_hf[...].astype(BF16)
    cot_halo = send(cot_htx, cot_hrx, ID_COT_HALO, up_band)
    cot_halo.start()

    sel_copies[3].wait()
    for d in (1, 2, 3):
        part = small.at[lax.rem(chan + CHUNKS - d, CHUNKS)]
        send(part, part, ID_SMALL + d - 1, at_y(d)).wait_recv()
    lmat[...] = jnp.zeros_like(lmat)
    masks = [pair_mask(kind // 2, kind % 2) for kind in range(4)]
    for h in range(HEADS_C):
        lanes = jnp.where(iota((128, CH), 1) // HD == h, 1.0, 0.0)
        ones[h * 128 : h * 128 + 128, :] = lanes.astype(BF16)
    unit[...] = jnp.where(iota((PAIR, 128), 0) == iota((PAIR, 128), 1), 1.0, 0.0).astype(BF16)

    def tables(c, _):
        table = jnp.concatenate([small[c, SM_TABLE : SM_TABLE + 4, :], small[c, SM_TABLE + 4 : SM_TABLE + 8, :]], 1)
        table = jnp.concatenate([table, jnp.zeros_like(table)], 0).astype(BF16)
        placed = dot(table, table_sel_t[...])
        for b_k in range(WIN):
            for h in range(HEADS_C):
                lmat[h * SLOT + b_k : h * SLOT + b_k + 1, :] = placed[h : h + 1, b_k * 128 : b_k * 128 + 128]
        for h in range(HEADS_C):
            tab = lmat[h * SLOT : h * SLOT + SLOT, :]
            lane = iota((SLOT, 128), 1)
            slabs = []
            for a in range(WIN):
                moved = pltpu.roll(tab, (128 - (WIN - 1 - a) * SLOT) % 128, 1) if a < WIN - 1 else tab
                low = jnp.where(lane < WIN * SLOT, moved, 0.0)
                slabs.append(low + pltpu.roll(low, WIN * SLOT, 1))
            one = jnp.concatenate(slabs * 2 + [jnp.zeros((128 - PAIR, 128), F32)], 0)
            for kind in range(4):
                bias[kind, c, h * 128 : h * 128 + 128, :] = (one + masks[kind]).astype(BF16)
        return 0

    lax.fori_loop(0, CHUNKS, tables, 0)

    pass_on(QKV, 1)
    merged_halo.wait_recv()
    mt[band(1), :] = with_halo(mt[band(1), :].astype(F32), m_hrx[...].astype(F32)).astype(BF16)
    norm1(1)
    pass_on(QKV, 2)

    cot_halo.wait_recv()
    norm[PEERS, BAND:T, :] = with_halo(norm[PEERS, BAND:T, :], cot_hrx[...].astype(F32))
    cot_tx[...] = norm[...].astype(BF16)
    lanes_here = pl.ds(pl.multiple_of(chan * CH, CH), CH)
    cot_copies = [
        send(cot_tx.at[lax.rem(chan + d, CHUNKS)], g2.at[:, lanes_here], ID_COT + d - 1, at_y(d)) for d in (1, 3, 2)
    ]
    for copy in cot_copies:
        copy.start()
    g2[:, lanes_here] = cot_tx[chan]

    mn_htx[...] = halo_of(mn[band(1), :].astype(F32)).astype(BF16)
    normed_halo = send(mn_htx, mn_hrx, ID_MN, up_rank)
    normed_halo.start()

    def wide(c):
        return jnp.concatenate([qkv_w[c, i] for i in range(3)], 1)

    own_w[QKV].wait()

    def attend(j, _):
        c = lax.rem(chan + chunk_off(j), CHUNKS)
        heads = pl.ds(pl.multiple_of(c * CH, CH), CH)

        @pl.when(j > 0)
        def _():
            have(QKV, j)

        projected = dot(n1[...], wide(c))
        zeros = jnp.zeros((1, CH), F32)
        offset = jnp.concatenate([small[c, SM_QV : SM_QV + 1, :], zeros, small[c, SM_QV + 1 : SM_QV + 2, :]], 1)
        scaled = jnp.concatenate([jnp.full((1, CH), SCALE, F32), jnp.ones((1, 2 * CH), F32)], 1)
        qkv[c] = ((projected + offset) * scaled).astype(BF16)

        @pl.when(j == 0)
        def _():
            pass_on(QKV, 3)

        def window_pairs(t, _):
            pairs = [UNROLL * t + i for i in range(UNROLL)]
            parts = [[qkv[c, rows_of(p), i * CH : i * CH + CH] for i in range(3)] for p in pairs]
            results = []
            for i, (q, k, v) in enumerate(parts):
                table = bias[2 * (chan // PEERS) * t + i // (UNROLL - 1), c]
                s = dot_nt(jnp.concatenate([q, unit[...]], 1), jnp.concatenate([spread(k), table], 1))
                weights = []
                for h in range(HEADS_C):
                    sh = s[:, 128 * h : 128 * h + 128]
                    weights.append(jnp.exp(sh - jnp.max(sh, -1, keepdims=True)).astype(BF16))
                w = jnp.concatenate(weights, 1)
                o = dot(w, jnp.concatenate([spread(v), ones[...]], 1))
                inverse = 1.0 / o[:, CH:]
                results.append((w, o[:, 0:CH] * inverse, inverse))
            for p, (w, o, inverse) in zip(pairs, results):
                prob[c, p] = w
                att[rows_of(p), heads] = o.astype(BF16)
                norm[c, rows_of(p), :] = inverse
            return 0

        lax.fori_loop(0, NPAIR // UNROLL, window_pairs, 0)

        @pl.when(j == 1)
        def _():
            for i in range(1, CHUNKS):
                pass_on(OUT, i)
            for w in (UP, DOWN):
                pass_around(w, 1)

        @pl.when(j == 2)
        def _():
            for w in (UP, DOWN):
                pass_around(w, 2)

        @pl.when(j == 3)
        def _():
            for w in (UP, DOWN):
                pass_around(w, 3)
                pass_across(w, 1)

        return 0

    lax.fori_loop(0, CHUNKS, attend, 0)

    own_w[OUT].wait()
    for j in range(1, CHUNKS):
        have(OUT, j)
    tmp[:, 0:D] = dot(att[...], out_w[...].reshape(D, D))
    out_b = jnp.concatenate([small[c, SM_OUT_B : SM_OUT_B + 1, :] for c in range(CHUNKS)], 1)
    down_b = jnp.concatenate([small[c, SM_DOWN_B : SM_DOWN_B + 1, :] for c in range(CHUNKS)], 1)

    def norm2(half):
        total = 0.0
        for i in three:
            r = pair_rows(half, i)
            branch = tmp[r, 0:D] + out_b
            resid = mt[r, :].astype(F32) + branch
            r1[r, :] = resid
            u, inverse = unit_of(resid.astype(BF16).astype(F32))
            u2[r, :] = u.astype(BF16)
            inv[r, 1:2] = inverse
            n2[r, :] = (u * gain[1] + shift[1]).astype(BF16)
            total = total + col_sum(branch * branch * valid)
        return total

    sq_one = norm2(0) + norm2(1)
    for w in (UP, DOWN):
        pass_across(w, 2)

    for d in (1, 2, 3):
        part = g2.at[:, pl.ds(pl.multiple_of(lax.rem(chan + CHUNKS - d, CHUNKS) * CH, CH), CH)]
        send(part, part, ID_COT + d - 1, at_y(d)).wait_recv()

    grads = (d_qkv, d_out, d_up, d_down)
    firsts = (l1_qkv, l1_out, l1_up, l1_down)
    order = (1, 3, 2)
    around = range(1, PLANE + 1)
    here = x * 4 + z

    def step(n, lead=0):
        return pl.ds(pl.multiple_of(lead, 16), n)

    def half_grad(w, c, k):
        return grads[w].at[c, step(halves[w], k * halves[w])]

    def core_copy(w, j, c):
        return send(half_grad(w, c, 1 - core), firsts[w].at[j], ID_CORE + w * CHUNKS + j, sibling)

    def core_sum(w, j, off):
        c = lax.rem(chan + off, CHUNKS)
        core_copy(w, j, c).wait_recv()
        size = min(halves[w], 64)
        for t in range(0, halves[w], size):
            r = step(size, core * halves[w] + t)
            total = grads[w][c, r, :].astype(F32) + firsts[w][j, t : t + size, :].astype(F32)
            grads[w][c, r, :] = total.astype(BF16)

    owners = {DOWN: (0, l2_down), OUT: (1, l2_out)}

    def owner_copy(w, off):
        n, into = owners[w]
        c = lax.rem(chan + off, CHUNKS)
        return send(half_grad(w, c, core), into.at[off - 1], ID_Y + n * PEERS + off - 1, at_y(off))

    def to_owner(w, off):
        @pl.when(off > 0)
        def _():
            owner_copy(w, off).start()

    def owner_wait(w):
        n, into = owners[w]
        for d in order:
            send(into.at[d - 1], into.at[d - 1], ID_Y + n * PEERS + d - 1, at_y(d)).wait_recv()

    def owner_sum(w, t, size):
        total = grads[w][chan, step(size, core * halves[w] + t), :].astype(F32)
        for d in range(PEERS):
            total += owners[w][1][d, t : t + size, :].astype(F32)
        return total.astype(BF16)

    class Plane:
        def __init__(self, n, g, rx, gf):
            self.n, self.g, self.rx, self.gf = n, g, rx, gf

        def out_copies(self):
            for m in around:
                src = self.g.at[step(16, place_of(m) * 16)]
                yield send(src, self.rx.at[m - 1], ID_A + self.n * 2 * PLANE + m - 1, at_plane(m))

        def back_copies(self, wait):
            for m in around:
                part = self.gf.at[core, step(16, (place_before(m) if wait else here) * 16)]
                yield send(part, part, ID_A + (self.n * 2 + 1) * PLANE + m - 1, at_plane(m))

        def start(self):
            for copy in self.out_copies():
                copy.start()

        def back_start(self):
            for copy in self.out_copies():
                copy.wait_recv()
            total = self.g[step(16, here * 16), :].astype(F32)
            for m in around:
                total += self.rx[m - 1].astype(F32)
            self.gf[core, step(16, here * 16), :] = total.astype(BF16)
            for copy in self.back_copies(False):
                copy.start()

        def finish(self):
            for copy in self.back_copies(True):
                copy.wait_recv()

        def left(self):
            for copy in [*self.out_copies(), *self.back_copies(False)]:
                copy.wait_send()

    plane_a = Plane(0, ga, rxa, gf_down)
    plane_b = Plane(1, gb, rxb, gfb)

    class Spread:
        def __init__(self, n, src, first, h, third, into):
            self.n, self.src, self.first, self.h, self.third, self.into = n, src, first, h, third, into

        def first_copies(self, j, c):
            for m in around:
                src = self.src(c, place_of(m) * 16, 16)
                n = ID_FIRST + (self.n * CHUNKS + j) * PLANE + m - 1
                yield send(src, self.first.at[c, m - 1], n, at_plane(m))

        def first_start(self, j, c):
            for copy in self.first_copies(j, c):
                copy.start()

        def third_copies(self):
            for d in order:
                src = self.h.at[lax.rem(chan + d, CHUNKS)]
                yield send(src, self.third.at[d - 1], ID_THIRD + self.n * PEERS + d - 1, at_y(d))

        def third_start(self, chunk_of):
            for j in range(CHUNKS):
                c = chunk_of(j)
                for copy in self.first_copies(j, c):
                    copy.wait_recv()
                total = self.src(c, here * 16, 16)[...].astype(F32)
                for m in around:
                    total += self.first[c, m - 1].astype(F32)
                self.h[c] = total.astype(BF16)
            for copy in self.third_copies():
                copy.start()

        def third_sum(self):
            for copy in self.third_copies():
                copy.wait_recv()
            total = self.h[chan].astype(F32)
            for d in range(PEERS):
                total += self.third[d].astype(F32)
            self.into(chan, here * 16, 16)[...] = total.astype(BF16)

        def back_y(self, wait):
            for d in order:
                part = self.into(lax.rem(chan + (CHUNKS - d if wait else 0), CHUNKS), here * 16, 16)
                yield send(part, part, ID_BACK_Y + d - 1, at_y(d))

        def back_copies(self, wait):
            for m in around:
                part = self.into(None, (place_before(m) if wait else here) * 16, 16)
                yield send(part, part, ID_BACK + self.n * PLANE + m - 1, at_plane(m))

        def back_start(self):
            for copy in self.back_copies(False):
                copy.start()

        def finish(self):
            for copy in self.back_copies(True):
                copy.wait_recv()

        def left_first(self, chunk_of):
            for j in range(CHUNKS):
                for copy in self.first_copies(j, chunk_of(j)):
                    copy.wait_send()

        def left_later(self):
            for copy in [*self.third_copies(), *self.back_copies(False)]:
                copy.wait_send()

        def left(self, chunk_of):
            self.left_first(chunk_of)
            self.left_later()

    def half_rows(w):
        return lambda c, row, n: grads[w].at[c, step(n, core * halves[w] + row)]

    group_a, group_b = 2 * core, 2 * core + 1
    spread_up = Spread(0, half_rows(UP), up_1, up_h, up_3, lambda c, row, n: gf_up.at[core, step(n, row)])
    spread_qkv = Spread(1, half_rows(QKV), qkv_1, qkv_h, qkv_3, lambda c, row, n: gf_qkv.at[core, step(n, row)])
    spread_m = Spread(
        2, lambda c, row, n: d_merge.at[group_b, c, step(n, row)], mb_1, mb_h, mb_3,
        lambda c, row, n: mf.at[group_b, slice(None) if c is None else c, step(n, row)],
    )

    def core_out(n, part):
        return send(part, part, ID_GC + n, sibling)

    def feed_chunk(j):
        return lax.rem(chan + feed_off(j), CHUNKS)

    def back_chunk(j):
        return lax.rem(chan + back_off(j), CHUNKS)

    def feed_sums(j):
        core_sum(DOWN, j, feed_off(j))
        to_owner(DOWN, feed_off(j))
        core_sum(UP, j, feed_off(j))
        spread_up.first_start(j, feed_chunk(j))

    def back_sums(j):
        core_sum(OUT, j, back_off(j))
        to_owner(OUT, back_off(j))
        core_sum(QKV, j, back_off(j))
        spread_qkv.first_start(j, back_chunk(j))

    class Small:
        def __init__(self, n, own, into):
            self.n, self.own, self.into = n, own, into

        def copies(self, level):
            base = ID_SG + self.n * (1 + 3 * PEERS)
            if level == 0:
                return [send(self.own.at[0], self.into[0].at[0], base, sibling)]
            at = (at_y, at_z, at_x)[level - 1]
            base += (level - 1) * PEERS
            return [send(self.own.at[level], self.into[level].at[d - 1], base + d, at(d)) for d in order]

        def start(self, level):
            for copy in self.copies(level):
                copy.start()

        def sum(self, level):
            for copy in self.copies(level):
                copy.wait_recv()
            total = self.own[level]
            for d in range(self.into[level].shape[0]):
                total += self.into[level][d]
            self.own[level + 1] = total

    small_early = Small(0, se, (se_c, se_y, se_z, se_x))
    small_late = Small(1, sl, (sl_c, sl_y, sl_z, sl_x))

    def lay(ref, at, row):
        for i in range(row.shape[1] // 128):
            ref[0, at + i : at + i + 1, :] = row[:, i * 128 : i * 128 + 128]

    tmp[...] = jnp.zeros_like(tmp)
    for copy in own_mlp:
        copy.wait()

    def feed(j, _):
        c = feed_chunk(j)

        @pl.when(j > 0)
        def _():
            have_across(UP, j)
            have_across(DOWN, j)

        @pl.when(j == 1)
        def _():
            for w in (UP, DOWN):
                pass_across(w, 3)

        up_c, down_c = up_w[c].reshape(D, 512), down_w[c].reshape(512, D)
        up_b = row_of(small, c, SM_UP_B, 4)
        d_up_b = 0.0
        for first in range(0, T, T // 3):
            r = slice(first, first + T // 3)
            value, slope = gelu_parts(dot(n2[r, :], up_c) + up_b)
            hid[r, :] = value.astype(BF16)
            d = slope * dot_nt(g2[r, :], down_c)
            dpre[r, :] = d.astype(BF16)
            d_up_b = d_up_b + col_sum(d)
        for i in range(4):
            d_small[c, SM_UP_B + i : SM_UP_B + i + 1, :] = d_up_b[:, i * 128 : i * 128 + 128]
        d_down[c] = dot_tn(hid[...], g2[...]).astype(BF16)
        core_copy(DOWN, j, c).start()
        d_up[c] = dot_tn(n2[...], dpre[...]).astype(BF16)
        core_copy(UP, j, c).start()
        tmp[:, 0:D] += dot(hid[...], down_c)
        tmp[:, D : 2 * D] += dot_nt(dpre[...], up_c)

        feed_sums(j)
        return 0

    lax.fori_loop(0, CHUNKS, feed, 0)

    for copy in [cot_halo] + cot_copies:
        copy.wait_send()
    blk_tx = cot_tx
    def norm2_back(half):
        totals = [0.0] * 6
        for i in three:
            r = pair_rows(half, i)
            branch = tmp[r, 0:D] + down_b
            result = r1[r, :] + branch
            for c in range(CHUNKS):
                blk_tx[c, r, :] = result[:, c * CH : c * CH + CH].astype(BF16)
            u = u2[r, :].astype(F32)
            dy = tmp[r, D : 2 * D]
            g = g2[r, :].astype(F32)
            grad = g + norm_back(dy, u, inv[r, 1:2], gain[1])
            tmp[r, 0:D] = grad
            g1[r, :] = grad.astype(BF16)
            terms = (branch * branch * valid, result * result * valid, g, dy * u, dy, grad)
            totals = [total + col_sum(term) for total, term in zip(totals, terms)]
        return totals

    sq_two, sq_out, d_down_b, d_gain1, d_shift1, d_out_b = (a + b for a, b in zip(norm2_back(0), norm2_back(1)))
    for c in range(CHUNKS):
        d_small[c, SM_DOWN_B : SM_DOWN_B + 1, :] = d_down_b[:, c * CH : c * CH + CH]
        d_small[c, SM_OUT_B : SM_OUT_B + 1, :] = d_out_b[:, c * CH : c * CH + CH]

    for c in range(CHUNKS):
        se[0, c * 6 : c * 6 + 6, :] = d_small[c, EARLY:16, :]
    lay(se, SE_NORM, d_gain1)
    lay(se, SE_NORM + 4, d_shift1)
    squares = [sum(sq[:, i * 128 : i * 128 + 128] for i in range(4)) for sq in (sq_out, sq_one, sq_two)]
    se[0, SE_SQ:SE_ROWS, :] = jnp.concatenate(squares + [jnp.zeros((5, 128), F32)], 0)
    small_early.start(0)

    blk_copies = [
        send(blk_tx.at[lax.rem(chan + d, CHUNKS)], blk_rx.at[chan], ID_BLK + d - 1, at_y(d)) for d in (1, 3, 2)
    ]
    blk_rx[chan] = blk_tx[chan]

    normed_halo.wait_recv()
    mn[band(1), :] = with_halo(mn[band(1), :].astype(F32), mn_hrx[...].astype(F32)).astype(BF16)

    sel_copies[2].wait()
    d_out[...] = dot_tn(att[...], g1[...]).astype(BF16).reshape(CHUNKS, CH, D)
    hid[...] = dot_nt(g1[...], out_w[...].reshape(D, D)).astype(BF16)

    def attend_back(j, _):
        c = lax.rem(chan + back_off(j), CHUNKS)
        heads = pl.ds(pl.multiple_of(c * CH, CH), CH)
        core_copy(OUT, j, c).start()
        sum_rows = pl.ds(pl.multiple_of(c * PAIR, 16), PAIR)

        def window_pairs(t, carry):
            pairs = [UNROLL * t + i for i in range(UNROLL)]
            parts = [[qkv[c, rows_of(p), i * CH : i * CH + CH] for i in range(3)] for p in pairs]
            d_atts = [hid[rows_of(p), heads].astype(F32) * norm[c, rows_of(p), :] for p in pairs]
            outs = [att[rows_of(p), heads] for p in pairs]
            probs = [prob[c, p] for p in pairs]
            results, total = [], 0.0
            for (q, k, v), d_att, o, w in zip(parts, d_atts, outs, probs):
                left = jnp.concatenate([d_att, -d_att * o.astype(F32)], 1).astype(BF16)
                d_s = w.astype(F32) * dot_nt(left, jnp.concatenate([spread(v), ones[...]], 1))
                total = total + d_s
                d_s = d_s.astype(BF16)
                d_q = dot(d_s, spread(k)) * SCALE
                d_k = dot_tn(by_head(d_s), stacked(q))[0:PAIR]
                d_v = dot_tn(by_head(w), stacked(left[:, 0:CH]))[0:PAIR]
                results.append(jnp.concatenate([d_q, d_k, d_v], 1).astype(BF16))
            for p, result in zip(pairs, results):
                dqkv[c, rows_of(p), :] = result
            return carry + total

        r1[sum_rows, :] = lax.fori_loop(0, NPAIR // UNROLL, window_pairs, jnp.zeros((PAIR, 512), F32))
        d_qkv[c] = dot_tn(n1[...], dqkv[c]).astype(BF16)
        core_copy(QKV, j, c).start()

        @pl.when(j > 0)
        def _():
            back_sums(j - 1)

        @pl.when(j == 0)
        def _():
            small_early.sum(0)
            small_early.start(1)

        @pl.when(j == 1)
        def _():
            for copy in blk_copies:
                copy.start()

        @pl.when(j == 2)
        def _():
            owner_wait(DOWN)
            for t in range(0, HALF, 64):
                ga[t : t + 64, :] = owner_sum(DOWN, t, 64)
            plane_a.start()
            spread_up.third_start(feed_chunk)
            small_early.sum(1)
            small_early.start(2)

        return 0

    lax.fori_loop(0, CHUNKS, attend_back, 0)

    def norm1_back(half):
        rows = band(half)
        tmp[rows, D : 2 * D] = sum(dot_nt(dqkv[c, rows, :], wide(c)) for c in range(CHUNKS))
        d_gain, d_shift = 0.0, 0.0
        for i in three:
            r = pair_rows(half, i)
            u, inverse = unit_of(mt[r, :].astype(F32))
            dy = tmp[r, D : 2 * D]
            gz[r, :] = (tmp[r, 0:D] + norm_back(dy, u, inverse, gain[0])).astype(BF16)
            d_gain, d_shift = d_gain + col_sum(dy * u), d_shift + col_sum(dy)
        return d_gain, d_shift

    d_gain0, d_shift0 = norm1_back(1)
    g_htx[...] = halo_of(gz[band(1), :].astype(F32)).astype(BF16)
    grad_halo = send(g_htx, g_hrx, ID_PG, down_rank)
    grad_halo.start()
    more_gain, more_shift = norm1_back(0)
    d_gain0, d_shift0 = d_gain0 + more_gain, d_shift0 + more_shift
    back_sums(PEERS)

    merge_core = [send(d_merge.at[2 - 2 * core + i], l1_m.at[i], ID_CORE_M + i, sibling) for i in range(2)]

    def merge_grad(k):
        lanes = pl.ds(pl.multiple_of(k * HALF, HALF), HALF)
        total = dot_tn(mn[...], gz[:, lanes]).astype(BF16)
        for i in range(2):
            d_merge[2 * k + i] = total[:, i * 128 : i * 128 + 128].reshape(CHUNKS, HALF, 128)

    merge_grad(1 - core)
    for copy in merge_core:
        copy.start()
    merge_grad(core)

    def merge_sum(i):
        merge_core[i].wait_recv()
        for c in range(CHUNKS):
            total = d_merge[2 * core + i, c].astype(F32) + l1_m[i, c].astype(F32)
            d_merge[2 * core + i, c] = total.astype(BF16)

    def merge_owner(d):
        return send(d_merge.at[group_a, lax.rem(chan + d, CHUNKS)], l2_m.at[d - 1], ID_Y_M + d - 1, at_y(d))

    merge_sum(0)
    for d in order:
        merge_owner(d).start()
    merge_sum(1)
    for c in range(CHUNKS):
        spread_m.first_start(c, c)

    plane_a.back_start()
    spread_up.third_sum()
    spread_up.back_start()
    small_early.sum(2)
    small_early.start(3)

    for d in (1, 2, 3):
        part = blk_rx.at[lax.rem(chan + CHUNKS - d, CHUNKS)]
        send(part, part, ID_BLK + d - 1, at_y(d)).wait_recv()
    blk_htx[...] = halo_of(blk_rx[PEERS, BAND:T, :].astype(F32)).astype(BF16)
    blk_halo = send(blk_htx, blk_hrx, ID_BLK_HALO, down_band)
    blk_halo.start()

    grad_halo.wait_recv()
    gz[band(1), :] = with_halo(gz[band(1), :].astype(F32), g_hrx[...].astype(F32)).astype(BF16)
    sel_copies[1].wait()
    tmp[...] = dot_nt(gz[...], merge_w[...])
    d_gain_m, d_shift_m = 0.0, 0.0
    for half in range(2):
        for i in three:
            r = pair_rows(half, i)
            u = x0[r, :].astype(F32)
            dy = tmp[r, :]
            tmp[r, :] = norm_back(dy, u, inv[r, 0:1], repl[RP_GAIN0 : RP_GAIN0 + 1, :])
            d_gain_m, d_shift_m = d_gain_m + col_sum(dy * u), d_shift_m + col_sum(dy)

    def head_sums(c, _):
        total = jnp.zeros((1, 3 * CH), F32)
        for i in range(NPAIR):
            total += col_sum(dqkv[c, i * PAIR : i * PAIR + PAIR, :].astype(F32))
        d_small[c, SM_QV : SM_QV + 1, :] = total[:, 0:CH]
        d_small[c, SM_QV + 1 : SM_QV + 2, :] = total[:, 2 * CH : 3 * CH]
        half = WIN * SLOT
        both = r1[c * PAIR : c * PAIR + PAIR, :]
        for h in range(HEADS_C):
            lanes = slice(h * 128, h * 128 + 128)
            folded = both[0:half, lanes] + pltpu.roll(both[half:PAIR, lanes], 128 - half, 1)
            acc = jnp.zeros((SLOT, 128), F32)
            for a in range(WIN):
                slab = folded[a * SLOT : a * SLOT + SLOT]
                moved = (WIN - 1 - a) * SLOT
                acc += pltpu.roll(slab, moved, 1) if moved else slab
            lmat[h * SLOT : h * SLOT + SLOT, :] = acc
        d_table = jnp.zeros((SLOT, 256), F32)
        for b_q in range(WIN):
            rows = [lmat[h * SLOT + b_q : h * SLOT + b_q + 1, :] for h in range(HEADS_C)]
            rows = jnp.concatenate(rows + [jnp.zeros((SLOT - HEADS_C, 128), F32)], 0)
            d_table += dot_nt(rows.astype(BF16), table_sel[:, b_q * 128 : b_q * 128 + 128])
        d_small[c, SM_TABLE : SM_TABLE + 4, :] = d_table[0:4, 0:128]
        d_small[c, SM_TABLE + 4 : SM_TABLE + 8, :] = d_table[0:4, 128:256]
        return 0

    for c in range(CHUNKS):
        head_sums(c, 0)
    for c in range(CHUNKS):
        sl[0, EARLY * c : EARLY * c + EARLY, :] = d_small[c, 0:EARLY, :]
    lay(sl, SL_NORM, d_gain0)
    lay(sl, SL_NORM + 4, d_shift0)
    lay(sl, SL_MERGE, d_gain_m)
    lay(sl, SL_MERGE + 8, d_shift_m)
    small_late.start(0)

    owner_wait(OUT)
    out_half = owner_sum(OUT, 0, 64)
    for g in range(4):
        gb[g * 64 : g * 64 + 64, 0:128] = out_half[:, g * 128 : g * 128 + 128]
    for d in order:
        merge_owner(d).wait_recv()
    total = d_merge[group_a, chan].astype(F32)
    for d in range(PEERS):
        total += l2_m[d].astype(F32)
    gb[:, 128:256] = total.astype(BF16)
    plane_b.start()
    spread_m.third_start(lambda c: c)
    spread_qkv.third_start(back_chunk)
    small_late.sum(0)
    small_late.start(1)

    def page_rows(i, _):
        base = (i // WIN) * BAND + lax.rem(i, WIN) * SLOT
        for q in range(2):
            parts = []
            for par in range(2):
                lanes = par * 512 + q * 256
                for wc in range(WC):
                    at = pl.multiple_of(base + wc * WIN * SLOT, SLOT)
                    parts.append(tmp[pl.ds(at, SLOT), lanes : lanes + 256])
            y = dot(pages_sel_t[...], jnp.concatenate(parts, 0).astype(BF16))
            pg[lax.rem(2 * i + q + LIFT, 2 * ROWS)] = y.astype(BF16)
        return 0

    lax.fori_loop(0, ROWS, page_rows, 0)
    pages_copy = local(pg, pages_o, 14)
    pages_copy.start()

    plane_b.back_start()
    spread_m.third_sum()
    for copy in spread_m.back_y(False):
        copy.start()
    spread_qkv.third_sum()
    spread_qkv.back_start()
    small_late.sum(1)
    small_late.start(2)

    for copy in spread_m.back_y(True):
        copy.wait_recv()
    spread_m.back_start()
    plane_b.finish()
    gf_out[core] = gfb[core, :, 0:128]
    mf[group_a, chan] = gfb[core, :, 128:256]

    def merge_back(c, d):
        part = mf.at[group_a, c]
        return send(part, part, ID_BACK_Y + PEERS + d - 1, at_y(d))

    for d in order:
        merge_back(chan, d).start()
    core_out(3, gf_out.at[core]).start()
    spread_qkv.finish()
    core_out(2, gf_qkv.at[core]).start()
    small_late.sum(2)
    small_late.start(3)
    late = [local(sl.at[4], late_o, 15)]
    core_out(2, gf_qkv.at[1 - core]).wait_recv()
    late.append(local(gf_qkv, qkv_o, 16))
    late[1].start()
    plane_a.finish()
    spread_up.finish()
    core_out(0, gf_down.at[core]).start()
    core_out(1, gf_up.at[core]).start()
    small_early.sum(3)

    blk_halo.wait_recv()
    outs = [local(blk_rx, block_o, 10), local(blk_hrx, block_halo_o, 9), local(se.at[4], early_o, 11)]
    core_out(0, gf_down.at[1 - core]).wait_recv()
    outs.append(local(gf_down, down_o, 12))
    core_out(1, gf_up.at[1 - core]).wait_recv()
    outs.append(local(gf_up, up_o, 13))
    for copy in outs:
        copy.start()

    for copy in [merged_halo, normed_halo, blk_halo, grad_halo] + merge_core + small_copies + blk_copies:
        copy.wait_send()
    for w in range(4):
        for copy in weight_copies[w]:
            copy.wait_send()
        for d in order:
            c = lax.rem(chan + CHUNKS - d, CHUNKS)
            if w in (QKV, OUT):
                copies = forward_copies(w, d, c)
            else:
                copies = [*around_copies(w, d, c), across_copy(w, d, c)]
            for copy in copies:
                copy.wait_send()
        for j in range(CHUNKS):
            core_copy(w, j, feed_chunk(j) if w in (UP, DOWN) else back_chunk(j)).wait_send()
    for d in order:
        owner_copy(DOWN, d).wait_send()
        owner_copy(OUT, d).wait_send()
        merge_owner(d).wait_send()
    plane_a.left()
    spread_up.left(feed_chunk)
    spread_qkv.left_first(back_chunk)
    spread_m.left_first(lambda c: c)
    for level in range(4):
        for copy in small_early.copies(level):
            copy.wait_send()

    for d in order:
        merge_back(lax.rem(chan + CHUNKS - d, CHUNKS), d).wait_recv()
    core_out(4, mf.at[group_a]).start()
    spread_m.finish()
    core_out(5, mf.at[group_b]).start()
    here_merge = local(mf.at[pl.ds(2 * core, 2)], merge_o.at[pl.ds(2 * core, 2)], 18)
    here_merge.start()
    core_out(3, gf_out.at[1 - core]).wait_recv()
    last = [local(gf_out, out_o, 17)]
    last[0].start()
    for i in range(2):
        core_out(4 + i, mf.at[2 - 2 * core + i]).wait_recv()
    last.append(local(mf.at[pl.ds(2 - 2 * core, 2)], merge_o.at[pl.ds(2 - 2 * core, 2)], 19))
    last[1].start()
    small_late.sum(3)
    late[0].start()

    for d in order:
        merge_back(chan, d).wait_send()
    plane_b.left()
    spread_qkv.left_later()
    spread_m.left_later()
    for copy in spread_m.back_y(False):
        copy.wait_send()
    for level in range(4):
        for copy in small_late.copies(level):
            copy.wait_send()
    parts = (gf_down.at[core], gf_up.at[core], gf_qkv.at[core], gf_out.at[core], mf.at[group_a], mf.at[group_b])
    for n, part in enumerate(parts):
        core_out(n, part).wait_send()
    for copy in outs + late + last + [pages_copy, here_merge]:
        copy.wait()


def kernel_call(args):
    hbm = pl.BlockSpec(memory_space=pl.ANY)
    s = jax.ShapeDtypeStruct
    outs = [
        s((CHUNKS, T, CH), BF16),
        s((WC * SHIFT * SLOT, CH), BF16),
        s((2 * ROWS, 2 * COLS, 256), BF16),
        s((2, HALF, D), BF16),
        s((2, HALF, 512), BF16),
        s((2, HALF, 3 * CH), BF16),
        s((2, HALF, 128), BF16),
        s((CHUNKS, CHUNKS, HALF, 128), BF16),
        s((SE_ROWS, 128), F32),
        s((SL_ROWS, 128), F32),
    ]

    def v(shape, dtype):
        return pltpu.VMEM(shape, dtype)

    scratch = [
        *[v(a.shape, BF16) for a in args[7:20]], v((8, 1024), F32),
        v((2 * ROWS, 2 * COLS, 256), BF16), *[v((WC * SHIFT * SLOT, D), BF16)] * 4, *[v((WC * SHIFT * SLOT, 2 * D), BF16)] * 2, v((COLS, 4 * ROWS, CH), BF16), v((CHUNKS, T, CH), BF16),
        v((WC * SHIFT * SLOT, CH), F32), v((WC * SHIFT * SLOT, CH), BF16), v((WC * SHIFT * SLOT, CH), BF16),
        v((1024, D), BF16), v((CHUNKS, 3, D, CH), BF16), v((CHUNKS, CH, D), BF16),
        v((CHUNKS, 4, 2, 64, 512), BF16), v((CHUNKS, 4, 2, 64, D), BF16), v((CHUNKS, 16, 128), F32),
        v((T, 1024), BF16), v((T, 2), F32), v((T, 1024), BF16), v((T, D), BF16), v((T, D), BF16),
        v((CHUNKS, T, 3 * CH), BF16), v((CHUNKS, NPAIR, PAIR, 512), BF16), v((T, D), BF16), v((CHUNKS, T, CH), F32),
        v((T, D), F32), v((T, D), BF16), v((T, D), BF16), v((T, D), BF16),
        v((T, 512), BF16), v((T, 512), BF16),
        v((4, CHUNKS, 512, 128), BF16), v((512, CH), BF16), v((PAIR, 128), BF16), v((HEADS_C * SLOT, 128), F32),
        v((CHUNKS, T, 3 * CH), BF16), v((T, D), BF16), v((T, D), BF16), v((T, 1024), F32),
        v((CHUNKS, T, CH), BF16), v((WC * SHIFT * SLOT, CH), BF16), v((WC * SHIFT * SLOT, CH), BF16),
        v((2 * ROWS, 2 * COLS, 256), BF16),
        v((CHUNKS, CHUNKS, HALF, 128), BF16), v((CHUNKS, D, 3 * CH), BF16), v((CHUNKS, CH, D), BF16),
        v((CHUNKS, D, 512), BF16), v((CHUNKS, 512, D), BF16), v((CHUNKS, 16, 128), F32),
        v((CHUNKS, HALF, 3 * CH), BF16), v((CHUNKS, CH // 2, D), BF16), v((CHUNKS, HALF, 512), BF16),
        v((CHUNKS, HALF, D), BF16), v((2, CHUNKS, HALF, 128), BF16),
        v((PEERS, CH // 2, D), BF16), v((PEERS, HALF, D), BF16), v((PEERS, HALF, 128), BF16),
    ]
    for lanes in (512, 384, 128):
        scratch += [v((CHUNKS, PLANE, 16, lanes), BF16), v((CHUNKS, 16, lanes), BF16), v((PEERS, 16, lanes), BF16)]
    for lanes in (512, 256):
        scratch += [v((HALF, lanes), BF16), v((PLANE, 16, lanes), BF16), v((2, HALF, lanes), BF16)]
    scratch += [v((2, HALF, 512), BF16), v((2, HALF, 384), BF16), v((2, HALF, 128), BF16), v((CHUNKS, CHUNKS, HALF, 128), BF16)]
    for rows in (SE_ROWS, SL_ROWS):
        scratch += [v((5, rows, 128), F32), v((1, rows, 128), F32)] + [v((PEERS, rows, 128), F32)] * 3
    scratch += [
        pltpu.SemaphoreType.DMA((IDS.count,)),
        pltpu.SemaphoreType.DMA((IDS.count,)),
        pltpu.SemaphoreType.DMA((LOCAL,)),
    ]
    return pl.pallas_call(
        compute,
        out_shape=outs,
        in_specs=[hbm] * len(args),
        out_specs=[hbm] * len(outs),
        scratch_shapes=scratch,
        compiler_params=pltpu.CompilerParams(
            vmem_limit_bytes=63 * 1024 * 1024, collective_id=0, has_side_effects=True
        ),
    )(*args)


def finish(
    block, pages, down, up, qkv, out, merge, block_halo, early, late,
    block_o, pages_o, gain_m_o, shift_m_o, merge_o, gain_o, shift_o, qkv_o, qv_o, table_o, out_o, out_b_o, up_o, up_b_o,
    down_o, down_b_o, rms_o,
    block_i, pages_i, down_i, up_i, qkv_i, out_i, merge_i, block_f, pages_f, down_f, up_f, qkv_f, out_f, merge_f, slots_f, halo_f, isem, osem,
):
    chan = lax.axis_index("chan")
    ins = (down, up, qkv, merge, pages, block, out)
    bufs = (down_i, up_i, qkv_i, merge_i, pages_i, block_i, out_i)
    copies = [pltpu.make_async_copy(a, b, isem.at[i]) for i, (a, b) in enumerate(zip(ins, bufs))]
    for copy in copies:
        copy.start()

    def early_row(i):
        return early[pl.ds(chan * 6 + i - EARLY, 1), :]

    def late_row(i):
        return late[pl.ds(chan * EARLY + i, 1), :]

    def joined(ref, at, n):
        return jnp.concatenate([ref[at + i : at + i + 1, :] for i in range(n)], 1)

    gain_m_o[...] = late[SL_MERGE : SL_MERGE + 8, :]
    shift_m_o[...] = late[SL_MERGE + 8 : SL_MERGE + 16, :]
    gain_o[...] = jnp.concatenate([joined(late, SL_NORM, 4), joined(early, SE_NORM, 4)], 0)
    shift_o[...] = jnp.concatenate([joined(late, SL_NORM + 4, 4), joined(early, SE_NORM + 4, 4)], 0)
    qv_o[...] = jnp.concatenate([late_row(SM_QV), late_row(SM_QV + 1)], 0)
    for h in range(HEADS_C):
        table_o[h : h + 1, 0:128] = late_row(SM_TABLE + h)
        table_o[h : h + 1, 128:169] = late_row(SM_TABLE + HEADS_C + h)[:, 0:41]
    out_b_o[...] = early_row(SM_OUT_B)
    for i in range(4):
        up_b_o[i : i + 1, :] = early_row(SM_UP_B + i)
    down_b_o[...] = early_row(SM_DOWN_B)
    sums = jnp.sum(early[SE_SQ : SE_SQ + 8, :], 1, keepdims=True)
    roots = jnp.sqrt(sums * (1.0 / (1792 * COLS * D)))
    for i in range(3):
        rms_o[i] = roots[i, 0]

    outs = (down_o, up_o, qkv_o, merge_o, pages_o, block_o, out_o)
    stages = (down_f, up_f, qkv_f, merge_f, pages_f, block_f, out_f)
    done = [pltpu.make_async_copy(a, b, osem.at[i]) for i, (a, b) in enumerate(zip(stages, outs))]

    for n, (i, f) in enumerate(((down_i, down_f), (up_i, up_f))):
        copies[n].wait()
        f[...] = i[...].astype(F32)
        done[n].start()
    copies[2].wait()
    for i in range(3):
        qkv_f[i] = qkv_i[:, i * CH : i * CH + CH].astype(F32)
    done[2].start()
    copies[3].wait()
    for i in range(CHUNKS):
        merge_f[:, i * 128 : i * 128 + 128] = merge_i[i].astype(F32)
    done[3].start()
    copies[4].wait()

    def page(i, _):
        pages_f[i] = pages_i[i].astype(F32)
        return 0

    lax.fori_loop(0, 2 * ROWS, page, 0)
    done[4].start()
    copies[5].wait()
    slots_f[...] = block_i[...].astype(F32)
    halo_f[...] = block_halo[...].astype(F32)
    for wc in range(WC):
        for b in range(WIN):
            j = (wc * WIN + b + SHIFT) % COLS
            block_f[j, 0:SHIFT, :] = halo_f[pl.ds(wc * SHIFT * SLOT + b, SHIFT, stride=SLOT), :]
            for m in range(4 * ROWS // WIN):
                c, wr = m // 2, m % 2
                n = WIN - SHIFT if m == 4 * ROWS // WIN - 1 else WIN
                slot = wr * BAND + wc * WIN * SLOT + b
                block_f[j, SHIFT + WIN * m : SHIFT + WIN * m + n, :] = slots_f[c, pl.ds(slot, n, stride=SLOT), :]
    done[5].start()
    copies[6].wait()
    for k in range(2):
        for g in range(4):
            out_f[k * 64 : k * 64 + 64, g * 128 : g * 128 + 128] = out_i[k, g * 64 : g * 64 + 64, :].astype(F32)
    done[6].start()
    for copy in done:
        copy.wait()


def finish_call(parts):
    block, block_halo, pages, down, up, qkv, out, merge, early, late = parts
    vm = pl.BlockSpec(memory_space=pltpu.VMEM)
    hbm = pl.BlockSpec(memory_space=pl.ANY)

    def s(*shape):
        return jax.ShapeDtypeStruct(shape, F32)

    big = {
        "block": s(COLS, 4 * ROWS, CH), "pages": s(2 * ROWS, 2 * COLS, 256), "merge": s(1024, D),
        "qkv": s(3, D, CH), "out": s(CH, D), "up": s(D, 512), "down": s(512, D),
    }
    shapes = [
        big["block"], big["pages"], s(8, 128), s(8, 128), big["merge"], s(2, D), s(2, D), big["qkv"], s(2, CH), s(HEADS_C, 169),
        big["out"], s(1, 128), big["up"], s(4, 128), big["down"], s(1, 128), s(3),
    ]
    large = [any(shape is b for b in big.values()) for shape in shapes]
    ins = [block, pages, down.reshape(512, D), up.reshape(D, 512), qkv.reshape(D, 3 * CH), out, merge.reshape(CHUNKS, 1024, 128)]
    results = pl.pallas_call(
        finish,
        out_shape=shapes,
        in_specs=[hbm] * 7 + [vm] * 3,
        out_specs=[hbm if b else vm for b in large[:-1]] + [pl.BlockSpec(memory_space=pltpu.SMEM)],
        scratch_shapes=[pltpu.VMEM(a.shape, BF16) for a in ins]
        + [pltpu.VMEM(big[n].shape, F32) for n in ("block", "pages", "down", "up", "qkv", "out", "merge")]
        + [pltpu.VMEM(block.shape, F32), pltpu.VMEM(block_halo.shape, F32)]
        + [pltpu.SemaphoreType.DMA((7,)), pltpu.SemaphoreType.DMA((7,))],
        compiler_params=pltpu.CompilerParams(vmem_limit_bytes=63 * 1024 * 1024),
    )(*ins, block_halo, early, late)
    r = list(results)
    r[0] = r[0].transpose(1, 0, 2)
    r[2], r[3] = r[2].reshape(1024), r[3].reshape(1024)
    r[7] = r[7].transpose(1, 0, 2)
    r[11], r[13], r[15] = r[11].reshape(CH), r[13].reshape(512), r[15].reshape(CH)
    return tuple(r)


def body(
    pages, merge_gain, merge_shift, merge_weight, norm_gain, norm_shift, qkv_weight, qv_bias, rel_table,
    out_weight, out_bias, up_weight, up_bias, down_weight, down_bias, cotangent,
):
    args = [
        pages, cotangent.transpose(1, 0, 2), merge_weight, qkv_weight.transpose(1, 0, 2), out_weight, up_weight, down_weight,
        qv_bias, rel_table, out_bias, up_bias, down_bias, merge_gain, merge_shift, norm_gain, norm_shift, *constants(),
    ]
    return finish_call(kernel_call(args))


def solution(mesh):
    placed = (
        P(("space", "chan"), None, None), P(), P(), P(), P(), P(), P(None, None, "chan"), P(None, "chan"),
        P("chan", None), P("chan", None), P("chan"), P(None, "chan"), P("chan"), P("chan", None), P("chan"),
        P("space", None, "chan"),
    )
    outs = (
        P("space", None, "chan"), P(("space", "chan"), None, None), P(), P(), P(), P(), P(),
        P(None, None, "chan"), P(None, "chan"), P("chan", None), P("chan", None), P("chan"),
        P(None, "chan"), P("chan"), P("chan", None), P("chan"), P(),
    )
    return jax.shard_map(body, mesh=mesh, in_specs=placed, out_specs=outs, check_vma=False)
```
